32 devices in a mesh: pipe: 4 (over y, x), dp: 8 (over z, core).
Axes of the slice: x: 2, y: 2, z: 4, core: 2. Of those that a mesh axis runs over, the one named last changes fastest.
Arguments:
- tokens: bfloat16 [16, 64, 1024], P('dp', 'pipe'), may hold values from -6 to 6
- cotangent: bfloat16 [16, 64, 1024], P('dp', 'pipe'), may hold values from -6 to 6
- lengths: int32 [16, 4], P('dp'), may hold values from 1 to 32, 64 in all within a row
- carried: float32 [16, 4, 4, 5, 1024], P('dp', None, 'pipe'), may hold values from -4 to 4, as said below
- norm_gain: float32 [4, 2, 1024], P('pipe'), may hold values from 0.5 to 1.5
- norm_bias: float32 [4, 2, 1024], P('pipe'), may hold values from -0.8 to 0.8
- mix_rates: float32 [4, 5, 1024], P('pipe'), may hold values from 0.05 to 0.95
- time_decay: float32 [4, 1024], P('pipe'), may hold values from -6 to -0.5
- time_first: float32 [4, 1024], P('pipe'), may hold values from -1 to 1
- attention_accept_proj: bfloat16 [4, 1024, 1024], P('pipe', 'dp'), may hold values from -0.1875 to 0.1875
- attention_lookup_proj: bfloat16 [4, 1024, 1024], P('pipe', 'dp'), may hold values from -0.1875 to 0.1875
- attention_content_proj: bfloat16 [4, 1024, 1024], P('pipe', 'dp'), may hold values from -0.1875 to 0.1875
- attention_result_proj: bfloat16 [4, 1024, 1024], P('pipe', 'dp'), may hold values from -0.5 to 0.5
- feedforward_accept_proj: bfloat16 [4, 1024, 1024], P('pipe', 'dp'), may hold values from -0.1875 to 0.1875
- feedforward_lookup_proj: bfloat16 [4, 1024, 4096], P('pipe', 'dp'), may hold values from -0.1875 to 0.1875
- feedforward_content_proj: bfloat16 [4, 4096, 1024], P('pipe', 'dp'), may hold values from -0.09375 to 0.09375
Outputs:
- mixed: bfloat16 [16, 64, 1024], P('dp', 'pipe')
- token_grad: float32 [16, 64, 1024], P('dp', 'pipe')
- final_carry: float32 [16, 4, 4, 5, 1024], P('dp', None, 'pipe')
- norm_gain_grad: float32 [4, 2, 1024], P('pipe', None, 'dp')
- norm_bias_grad: float32 [4, 2, 1024], P('pipe', None, 'dp')
- mix_rates_grad: float32 [4, 5, 1024], P('pipe', None, 'dp')
- time_decay_grad: float32 [4, 1024], P('pipe', 'dp')
- time_first_grad: float32 [4, 1024], P('pipe', 'dp')
- time_recept_grad: float32 [4, 1024, 1024], P('pipe', 'dp')
- time_key_grad: float32 [4, 1024, 1024], P('pipe', 'dp')
- time_value_grad: float32 [4, 1024, 1024], P('pipe', 'dp')
- time_output_grad: float32 [4, 1024, 1024], P('pipe', 'dp')
- channel_recept_grad: float32 [4, 1024, 1024], P('pipe', 'dp')
- channel_key_grad: float32 [4, 1024, 4096], P('pipe', 'dp')
- channel_value_grad: float32 [4, 4096, 1024], P('pipe', 'dp')
The draws below stay inside these ranges and needn't reach their ends.
Inputs may be any that keep to these rules, and one draw needn't show every extreme that they name: Each row of lengths sums to 64, and the longest of each row is 32. `carried`: the denominators (index 1 of the fourth dimension) lie in [0.5, 4], the offsets (index 2) in [-1, 1].
All inputs are finite; a program needn't handle non-finite values.
Results may differ from the reference program's by a relative error of at most 0.02.
Values may be sent and summed in bfloat16 or wider, within the bound.
A program may use at most 320 MiB of HBM per device.

```python
import math
import jax
import jax.numpy as jnp
import numpy as np
from jax import lax

D = 1024
FF = 4096
MB_TOK = 64
SEQ_MB = 4
LAYERS = 4
LONGEST = 32
BATCHES = 16


def draw_carried(key, part):
    key = jax.random.fold_in(key, 7)
    subkeys = jax.random.split(key, 5)
    shape = (BATCHES, SEQ_MB, LAYERS, D)
    numerator = jax.random.truncated_normal(subkeys[0], -4.0, 4.0, shape, jnp.float32)
    denominator = jnp.exp(jax.random.uniform(subkeys[1], shape, jnp.float32, math.log(0.5), math.log(4.0)))
    shift_amount = jax.random.uniform(subkeys[2], shape, jnp.float32, -1.0, 1.0)
    shift_time = jax.random.truncated_normal(subkeys[3], -4.0, 4.0, shape, jnp.float32)
    shift_channel = jax.random.truncated_normal(subkeys[4], -4.0, 4.0, shape, jnp.float32)
    return jnp.stack([numerator, denominator, shift_amount, shift_time, shift_channel], axis=3)


def levels(key, extent, cuts, least, top_value):
    gain = 1.0
    for dim, parts in cuts:
        steps = jax.random.uniform(jax.random.fold_in(jax.random.fold_in(key, 6), dim), (parts,), jnp.float32, least / len(cuts), top_value / len(cuts))
        gain = gain * jnp.repeat(jnp.exp(steps), extent[dim] // parts).reshape((-1,) + (1,) * (len(extent) - 1 - dim))
    return gain


def profile(number_of, total, limit, lean):
    portions = [(1 << 20) // math.isqrt(grade ** lean) + 1 for grade in range(2, number_of + 1)]
    rest, holding = total - limit - (number_of - 1), [1] * (number_of - 1)
    while rest > 0:
        free = [i for i in range(number_of - 1) if holding[i] < limit]
        pool, budget = sum([portions[i] for i in free]), rest
        for i in free:
            addition = min(limit - holding[i], max(1, budget * portions[i] // pool), rest)
            holding[i] = holding[i] + addition
            rest = rest - addition
    return np.array([limit] + holding)


def uneven(key, count, total, limit, slope):
    if count == 2:
        one = jax.random.randint(key, (), max(1, total - limit), min(limit, total - 1) + 1)
        return jnp.stack([one, total - one])
    sizes = jnp.asarray(profile(count, total, limit, slope), jnp.int32)
    twos = (count - 1) // 2
    donor, receiver = sizes[1:1 + 2 * twos:2], sizes[2:2 + 2 * twos:2]
    margin = jnp.minimum(donor - 1, limit - receiver)
    passed = jax.random.randint(jax.random.fold_in(key, 1), (twos,), 0, 1 << 20) % (margin + 1)
    sizes = sizes.at[1:1 + 2 * twos:2].set(donor - passed).at[2:2 + 2 * twos:2].set(receiver + passed)
    return sizes[jax.random.permutation(jax.random.fold_in(key, 2), count)]


def gaussian(rng, extent, deviation, reach, cuts=(), kind=jnp.bfloat16):
    level = levels(rng, extent, cuts, -0.22, 0.18) if cuts else 1.0
    values = jax.random.normal(rng, extent, jnp.float32) * deviation * level
    return jnp.minimum(jnp.maximum(values, -reach), reach).astype(kind)


def setup_inputs(seed: int = 0) -> dict:
    streams_of = jax.random.split(jax.random.key(seed), 17)
    tokens = gaussian(streams_of[0], (BATCHES, MB_TOK, D), 1.0, 6.0, ((0, 8), (1, 4)))
    cotangent = gaussian(streams_of[1], (BATCHES, MB_TOK, D), 1.0, 6.0, ((0, 8), (1, 4)))
    lengths = jax.vmap(lambda own: uneven(own, SEQ_MB, MB_TOK, LONGEST, 1))(jax.random.split(streams_of[2], BATCHES)).reshape((BATCHES, SEQ_MB)).astype(jnp.int32)
    carried = draw_carried(jax.random.fold_in(streams_of[16], 71), 0)
    norm_gain = jnp.clip(1.0 + 0.1 * jax.random.normal(streams_of[4], (LAYERS, 2, D), jnp.float32), 0.5, 1.5)
    norm_bias = gaussian(streams_of[5], (LAYERS, 2, D), 0.2, 0.8, ((0, 4),), jnp.float32)
    mix_rates = jnp.clip(0.05 + 0.9 * jax.random.uniform(streams_of[6], (LAYERS, 5, D), jnp.float32) ** levels(streams_of[6], (LAYERS, 5, D), ((0, 4),), -0.2, 0.2), 0.05, 0.95)
    time_decay = jnp.clip(-6.0 + 5.5 * jax.random.uniform(streams_of[7], (LAYERS, D), jnp.float32) ** levels(streams_of[7], (LAYERS, D), ((0, 4),), -0.2, 0.2), -6.0, -0.5)
    time_first = jnp.clip(jax.random.uniform(streams_of[8], (LAYERS, D), jnp.float32, -1.0, 1.0) * levels(streams_of[8], (LAYERS, D), ((0, 4),), -0.4, 0.0), -1.0, 1.0)
    attention_accept_proj = gaussian(streams_of[9], (LAYERS, D, D), D ** -0.5, 0.1875, ((0, 4), (1, 8)))
    attention_lookup_proj = gaussian(streams_of[10], (LAYERS, D, D), D ** -0.5, 0.1875, ((0, 4), (1, 8)))
    attention_content_proj = gaussian(streams_of[11], (LAYERS, D, D), D ** -0.5, 0.1875, ((0, 4), (1, 8)))
    attention_result_proj = gaussian(streams_of[12], (LAYERS, D, D), (D // 8) ** -0.5, 0.5, ((0, 4), (1, 8)))
    feedforward_accept_proj = gaussian(streams_of[13], (LAYERS, D, D), D ** -0.5, 0.1875, ((0, 4), (1, 8)))
    feedforward_lookup_proj = gaussian(streams_of[14], (LAYERS, D, FF), D ** -0.5, 0.1875, ((0, 4), (1, 8)))
    feedforward_content_proj = gaussian(streams_of[15], (LAYERS, FF, D), FF ** -0.5, 0.09375, ((0, 4), (1, 8)))
    return dict(tokens=tokens, cotangent=cotangent, lengths=lengths, carried=carried, norm_gain=norm_gain, norm_bias=norm_bias, mix_rates=mix_rates, time_decay=time_decay, time_first=time_first, attention_accept_proj=attention_accept_proj, attention_lookup_proj=attention_lookup_proj, attention_content_proj=attention_content_proj, attention_result_proj=attention_result_proj, feedforward_accept_proj=feedforward_accept_proj, feedforward_lookup_proj=feedforward_lookup_proj, feedforward_content_proj=feedforward_content_proj)


epsilon = 1e-05
exactly = lax.Precision.HIGHEST

@jax.custom_vjp
def low(v):
    return lax.optimization_barrier(v.astype(jnp.bfloat16)).astype(jnp.float32)

@jax.custom_vjp
def low_back(v):
    return v

def low_keep(v):
    return (low(v), None)

def low_pass(kept, grad):
    return (grad,)

def back_keep(v):
    return (v, None)

def back_low(kept, grad):
    return (low(grad),)
low.defvjp(low_keep, low_pass)
low_back.defvjp(back_keep, back_low)

def matmul(former, latter):
    return jnp.dot(former, latter, precision=exactly, preferred_element_type=jnp.float32)

def matmul_tn(former, latter):
    return lax.dot_general(former, latter, (((0,), (0,)), ((), ())), precision=exactly, preferred_element_type=jnp.float32)

def layer_norm(stream, norm_scale, norm_offset):
    center = stream - lax.optimization_barrier(jnp.mean(stream, axis=-1, keepdims=True))
    spread = lax.optimization_barrier(jnp.mean(center * center, axis=-1, keepdims=True))
    return center * lax.rsqrt(spread + epsilon) * norm_scale + norm_offset

def tables(lengths_row, row_count):
    finishes = jnp.cumsum(lengths_row).astype(jnp.int32)
    beginnings = finishes - lengths_row.astype(jnp.int32)
    places = jnp.arange(row_count, dtype=jnp.int32)[:, None]
    first_hot = (places == beginnings[None, :]).astype(jnp.float32)
    last_hot = (places == (finishes - 1)[None, :]).astype(jnp.float32)
    return (first_hot, last_hot, lax.optimization_barrier(jnp.sum(first_hot, axis=1)))

def mix_front(stream, norm_scale, norm_offset, blend_fractions, start_rows, first_hot, series_onsets):
    normed = layer_norm(stream, norm_scale, norm_offset)
    previous = jnp.concatenate([jnp.zeros_like(normed[:1]), normed[:-1]], axis=0)
    previous = previous * (1.0 - series_onsets)[:, None] + matmul(first_hot, start_rows)
    mixtures = tuple((normed * blend_fractions[member] + previous * (1.0 - blend_fractions[member]) for member in range(blend_fractions.shape[0])))
    return (mixtures, normed)

def exponential_scan(lookup_entries, content_entries, fading_multiplier, first_token_boost, initial_memory, series_onsets):
    decay_step = -jnp.exp(fading_multiplier)

    def advance(state, current):
        numerator, denominator, shift_amount = state
        present_lookup, value_now, starting, fresh_num, fresh_den, fresh_off = current
        keeping = 1.0 - starting
        numerator = numerator * keeping + fresh_num
        denominator = denominator * keeping + fresh_den
        shift_amount = shift_amount * keeping + fresh_off
        first_token_extra = first_token_boost + present_lookup
        largest_entry = jnp.maximum(shift_amount, first_token_extra)
        old_part = jnp.exp(shift_amount - largest_entry)
        fresh_portion = jnp.exp(first_token_extra - largest_entry)
        output = (old_part * numerator + fresh_portion * value_now) / (old_part * denominator + fresh_portion)
        decayed = shift_amount + decay_step
        largest_entry = jnp.maximum(decayed, present_lookup)
        old_part = jnp.exp(decayed - largest_entry)
        fresh_portion = jnp.exp(present_lookup - largest_entry)
        numerator = old_part * numerator + fresh_portion * value_now
        denominator = old_part * denominator + fresh_portion
        return ((numerator, denominator, largest_entry), (output, numerator, denominator, largest_entry))
    zeroes = jnp.zeros_like(fading_multiplier)
    scanned = lax.scan(advance, (zeroes, zeroes, zeroes), (lookup_entries, content_entries, series_onsets, initial_memory[0], initial_memory[1], initial_memory[2]))[1]
    return (scanned[0], (scanned[1], scanned[2], scanned[3]))

def attention_routine(lookup_entries, content_entries, acceptance_entries, fading_multiplier, first_token_boost, initial_memory, series_onsets):
    result_entries, carried_memories = exponential_scan(lookup_entries, content_entries, fading_multiplier, first_token_boost, initial_memory, series_onsets)
    return (jax.nn.sigmoid(acceptance_entries) * result_entries, carried_memories)

def last_states(last_hot, carried_memories, normed, normed_channel):
    stacked = jnp.stack([carried_memories[0], carried_memories[1], carried_memories[2], normed, normed_channel], axis=1)
    flattened = stacked.reshape(stacked.shape[0], 5 * stacked.shape[2])
    return matmul_tn(last_hot, flattened).reshape(last_hot.shape[1], 5, stacked.shape[2])

def layer_forward(stream, level_coefficients, carry_rows, layout):
    normalizer_gains, series_boundaries, blend_fractions, fading_multiplier, first_token_boost, attention_accept_proj, attention_lookup_proj, attention_content_proj, attention_result_proj, feedforward_accept_proj, feedforward_lookup_proj, feedforward_content_proj = level_coefficients
    first_hot, last_hot, series_onsets = layout
    mixtures, normed = mix_front(stream, normalizer_gains[0], series_boundaries[0], blend_fractions[0:3], carry_rows[:, 3], first_hot, series_onsets)
    lookup_entries = low_back(matmul(low(mixtures[0]), attention_lookup_proj))
    content_entries = low_back(matmul(low(mixtures[1]), attention_content_proj))
    acceptance_entries = low_back(matmul(low(mixtures[2]), attention_accept_proj))
    initial_memory = tuple((matmul(first_hot, carry_rows[:, member]) for member in range(3)))
    sigmoid_masked_result, carried_memories = attention_routine(lookup_entries, content_entries, acceptance_entries, fading_multiplier, first_token_boost, initial_memory, series_onsets)
    middle = stream + low_back(matmul(low(sigmoid_masked_result), attention_result_proj))
    mixtures, normed_channel = mix_front(middle, normalizer_gains[1], series_boundaries[1], blend_fractions[3:5], carry_rows[:, 4], first_hot, series_onsets)
    hidden = low_back(matmul(low(mixtures[0]), feedforward_lookup_proj))
    active = jax.nn.relu(hidden)
    carried_value = low_back(matmul(low(active * active), feedforward_content_proj))
    recept_channel = low_back(matmul(low(mixtures[1]), feedforward_accept_proj))
    result = middle + jax.nn.sigmoid(recept_channel) * carried_value
    return (result, last_states(last_hot, carried_memories, normed, normed_channel))

def block_forward(level_coefficients, carry_rows, lengths_row, stream):
    layout = tables(lengths_row, stream.shape[0])
    collected = []
    for layer_index in range(LAYERS):
        if layer_index > 0:
            stream = low_back(low(stream))
        layer_weights = tuple((member[layer_index] for member in level_coefficients))
        stream, final_rows = layer_forward(stream, layer_weights, carry_rows[:, layer_index], layout)
        collected.append(final_rows)
    return (stream, jnp.stack(collected, axis=1))

def reference(tokens, cotangent, lengths, carried, norm_gain, norm_bias, mix_rates, time_decay, time_first, attention_accept_proj, attention_lookup_proj, attention_content_proj, attention_result_proj, feedforward_accept_proj, feedforward_lookup_proj, feedforward_content_proj):
    level_coefficients = tuple((member.astype(jnp.float32) for member in (norm_gain, norm_bias, mix_rates, time_decay, time_first, attention_accept_proj, attention_lookup_proj, attention_content_proj, attention_result_proj, feedforward_accept_proj, feedforward_lookup_proj, feedforward_content_proj)))

    def forward(stream, *layer_weights):

        def one_block(pieces):
            return block_forward(layer_weights, pieces[0], pieces[1], pieces[2])
        return lax.map(jax.checkpoint(one_block), (carried, lengths, stream))
    result_entries, pullback, finals = jax.vjp(forward, tokens.astype(jnp.float32), *level_coefficients, has_aux=True)
    gradients = pullback(cotangent.astype(jnp.float32))
    return (result_entries.astype(jnp.bfloat16), gradients[0], finals, gradients[1], gradients[2], gradients[3], gradients[4], gradients[5], gradients[6], gradients[7], gradients[8], gradients[9], gradients[10], gradients[11], gradients[12])
```

```python
from functools import partial

import jax
import jax.numpy as jnp
from jax import lax
from jax.sharding import PartitionSpec as P
from jax.experimental import pallas as pl
from jax.experimental.pallas import tpu as pltpu

EPS = 1e-05
BF = jnp.bfloat16
F32 = jnp.float32
HIGH = lax.Precision.HIGHEST
MESH = pl.DeviceIdType.MESH
RANKS = 4
HALVES = 2


def dot(a, b, precision=None):
    return jnp.dot(a, b, precision=precision, preferred_element_type=F32)


def dot_nt(a, b):
    return lax.dot_general(a, b, (((1,), (1,)), ((), ())), preferred_element_type=F32)


def dot_tn(a, b):
    return lax.dot_general(a, b, (((0,), (0,)), ((), ())), preferred_element_type=F32)


def rolled(x, shift):
    return pltpu.roll(x, shift % x.shape[0], 0)


def normed(h):
    center = h - jnp.mean(h, axis=-1, keepdims=True)
    spread = jnp.mean(center * center, axis=-1, keepdims=True)
    rstd = lax.rsqrt(spread + EPS)
    return center * rstd, rstd


def norm_back(dn, gain, hat, rstd):
    dh = dn * gain
    return rstd * (
        dh
        - jnp.mean(dh, axis=-1, keepdims=True)
        - hat * jnp.mean(dh * hat, axis=-1, keepdims=True)
    )


def column_sum(x):
    return jnp.sum(x, axis=0, keepdims=True)


def ring_place(pipe):
    return pipe + (pipe // 2) * (5 - 2 * pipe)


A0, A1, V0, V1, K0, K1, OO = range(7)
FORTH = ((A0, 0), (A1, 1), (OO, 1), (V0, 2), (V1, 3), (K0, 4), (K1, 5))
BACK = ((V0, 0), (V1, 1), (K0, 2), (K1, 3), (A0, 4), (A1, 5), (OO, 5))
GROUPS = (A0, V0, K0, OO)


def layers_kernel(
    outer,
    longest,
    tok,
    cot,
    lens,
    held,
    gain,
    bias,
    mixes,
    decay,
    first,
    wk,
    wv,
    wr,
    wfr,
    wo,
    wfk,
    wfv,
    mixed,
    tgrad,
    finout,
    small,
    gk,
    gv,
    gr,
    gfr,
    go,
    gfk,
    gfv,
    wA,
    wO,
    wK,
    wV,
    dA,
    dO,
    dK,
    dV,
    tokb,
    cotb,
    info,
    infob,
    stsrc,
    stb,
    shsrc,
    shb,
    par,
    parb,
    nsave,
    n2save,
    hsave,
    msave,
    kvsave,
    gatesave,
    zsave,
    alsave,
    besave,
    smsave,
    part,
    rbuf,
    r2st,
    r2full,
    cur,
    finb,
    mixb,
    gradb,
    dkvall,
    dmall,
    dr2o,
    dr2c,
    sg,
    sgr,
    sgt,
    sg8,
    x_s,
    x_r,
    st_s,
    st_r,
    sh_s,
    sh_r,
    par_s,
    par_r,
    w1_s,
    w1_r,
    w1_l,
    rw_s,
    rw_r,
    w3_s,
    w3_r,
    ag_s,
    ag_r,
    rs_s,
    rs_r,
    a2_s,
    a2_r,
    a2b_s,
    a2b_r,
    fin_s,
    fin_r,
    out_s,
    out_r,
    a_s,
    a_r,
    rd_s,
    rd_r,
    r1_s,
    r1_r,
    r1_l,
    sg_s,
    sg_r,
    sg8_s,
    sg8_r,
    credit,
    sib_credit,
):
    p = lax.axis_index("pipe")
    d = lax.axis_index("dp")
    t = d // (HALVES * outer)
    c = (d // outer) % HALVES
    o = d % outer
    ring = ring_place(p)
    micro, chunk, width = tok.shape
    layers = stb.shape[0]
    rows = micro * chunk * RANKS
    quarter = width // RANKS
    mine = pl.ds(pl.multiple_of(chunk * t, chunk), chunk)
    my_cols = pl.ds(pl.multiple_of(quarter * t, quarter), quarter)
    hidden = wfk.shape[1] // RANKS
    my_hidden = pl.ds(pl.multiple_of(hidden * t, hidden), hidden)
    block = wk.shape[0]
    seqs = held.shape[0] * held.shape[1]
    per = held.shape[1]

    def place(rank, half):
        return (rank * HALVES + half) * outer + o

    def next_rank(r):
        return (t + r) % RANKS

    def next_pipe(r):
        return (p + r) % RANKS

    def on_ring(r):
        return ring_place((ring + r) % RANKS)

    def remote(src, dst, ss, rs, pipe, rank, half):
        return pltpu.make_async_remote_copy(
            src_ref=src,
            dst_ref=dst,
            send_sem=ss,
            recv_sem=rs,
            device_id=(pipe, place(rank, half)),
            device_id_type=MESH,
        )

    def peer(src, dst, ss, rs, r):
        return remote(src, dst, ss, rs, p, next_rank(r), c)

    def plane(src, dst, ss, rs, r):
        return remote(src, dst, ss, rs, next_pipe(r), t, c)

    def sibling(src, dst, ss, rs):
        return remote(src, dst, ss, rs, p, t, 1 - c)

    def start_any(is_self, src, dst, ss, rs, pipe, rank):
        @pl.when(is_self)
        def _():
            pltpu.make_async_copy(src, dst, ss).start()

        @pl.when(jnp.logical_not(is_self))
        def _():
            remote(src, dst, ss, rs, pipe, rank, c).start()

    def sent_any(is_self, src, dst, ss, rs, pipe, rank):
        @pl.when(is_self)
        def _():
            pltpu.make_async_copy(src, dst, ss).wait()

        @pl.when(jnp.logical_not(is_self))
        def _():
            remote(src, dst, ss, rs, pipe, rank, c).wait_send()

    def got(dst, rs):
        remote(dst, dst, rs, rs, next_pipe(1), t, c).wait_recv()

    def got_any(is_self, dst, rs):
        @pl.when(jnp.logical_not(is_self))
        def _():
            got(dst, rs)

    barrier = pltpu.get_barrier_semaphore()
    for a in range(RANKS):
        for b in range(RANKS):
            if a or b:
                pl.semaphore_signal(
                    barrier,
                    inc=1,
                    device_id=(next_pipe(a), place(next_rank(b), c)),
                    device_id_type=MESH,
                )
    for b in range(RANKS):
        pl.semaphore_signal(
            barrier, inc=1, device_id=(p, place(next_rank(b), 1 - c)), device_id_type=MESH
        )
    pl.semaphore_wait(barrier, RANKS * RANKS - 1 + RANKS)

    raw = (wk, wv, wr, wfr)

    def w1(m, r):
        rank = next_rank(r)
        if m < 4:
            cols = pl.ds(pl.multiple_of(quarter * rank, quarter), quarter)
            return peer(
                raw[m].at[:, cols],
                wA.at[p, t, c, :, pl.ds(m * quarter, quarter)],
                w1_s.at[m, r - 1],
                w1_r.at[m, r - 1],
                r,
            )
        cols = pl.ds(pl.multiple_of(hidden * rank, hidden), hidden)
        return peer(wfk.at[:, cols], wK.at[p, t, c], w1_s.at[m, r - 1], w1_r.at[m, r - 1], r)

    def w1_own(m):
        if m < 4:
            return pltpu.make_async_copy(
                raw[m].at[:, my_cols], wA.at[p, t, c, :, pl.ds(m * quarter, quarter)], w1_l.at[m]
            )
        if m == 4:
            return pltpu.make_async_copy(wfk.at[:, my_hidden], wK.at[p, t, c], w1_l.at[m])
        if m == 5:
            return pltpu.make_async_copy(wo, wO.at[p, c], w1_l.at[m])
        return pltpu.make_async_copy(wfv, wV.at[p, c], w1_l.at[m])

    for m in range(4):
        for r in range(1, RANKS):
            w1(m, r).start()
    for m in range(7):
        w1_own(m).start()

    lane = lax.broadcasted_iota(jnp.int32, info.shape, 1)
    line = lax.broadcasted_iota(jnp.int32, info.shape, 0)
    marks = jnp.full(info.shape, -1, jnp.int32)
    for b in range(micro):
        at = b * (rows // micro)
        for s in range(per):
            index = b * per + s
            marks = jnp.where(jnp.logical_and(line == 0, lane == index), at, marks)
            at = at + lens[b, s]
            marks = jnp.where(line == 8 + index, at - 1, marks)
    info[...] = marks.astype(F32)

    swap_self = p == t
    swaps = [(tok, tokb), (info, infob), (cot, cotb)]
    for i, (src, dst) in enumerate(swaps):
        start_any(swap_self, src, dst, x_s.at[i], x_r.at[i], t, p)

    par[0:2, :] = gain[0]
    par[2:4, :] = bias[0]
    par[4:9, :] = mixes[0]
    par[9:10, :] = decay[...]
    par[10:11, :] = first[...]
    par[11:16, :] = jnp.zeros((5, width), F32)

    def par_copy(r):
        return plane(par, parb.at[p], par_s.at[r - 1], par_r.at[p], r)

    for r in range(1, RANKS):
        par_copy(r).start()
    parb[p] = par[...]

    carried_rows = held[:, :, 0].reshape(seqs, 5, width)
    spare = jnp.zeros((8, width), F32)
    stsrc[...] = jnp.concatenate([carried_rows[:, i] for i in range(3)] + [spare], axis=0).astype(BF)
    shsrc[...] = jnp.concatenate([carried_rows[:, 3], carried_rows[:, 4]], axis=0).astype(BF)

    def state_args(rank):
        return (
            jnp.logical_and(swap_self, rank == t),
            stsrc.at[:, pl.ds(quarter * rank, quarter)],
            stb.at[p],
            st_s.at[rank],
            st_r.at[p],
            t,
            rank,
        )

    def shift_args(rank):
        return (
            jnp.logical_and(swap_self, rank == t),
            shsrc,
            shb.at[p],
            sh_s.at[rank],
            sh_r.at[p],
            t,
            rank,
        )

    def send_carried(l):
        @pl.when(p == l)
        def _():
            for rank in range(RANKS):
                start_any(*shift_args(rank))
                start_any(*state_args(rank))

    def get_carried(l):
        from_self = jnp.logical_and(swap_self, p == l)

        @pl.when(from_self)
        def _():
            for rank in range(RANKS):

                @pl.when(rank == t)
                def _():
                    pltpu.make_async_copy(*shift_args(rank)[1:4]).wait()
                    pltpu.make_async_copy(*state_args(rank)[1:4]).wait()

        got_any(from_self, shb.at[l], sh_r.at[l])
        got_any(from_self, stb.at[l], st_r.at[l])
        got_any(p == l, parb.at[l], par_r.at[l])

    def carried_sent():
        for rank in range(RANKS):

            @pl.when(jnp.logical_not(jnp.logical_and(swap_self, rank == t)))
            def _():
                remote(*shift_args(rank)[1:], c).wait_send()
                remote(*state_args(rank)[1:], c).wait_send()

    def piece(store, at, i, way, half):
        a, small_one, k, v = store
        if i in (A0, A1):
            return a.at[at, 2 * way + i - A0, half]
        if i in (K0, K1):
            return k.at[at, 2 * way + i - K0, half]
        size = (small_one if i == OO else v).shape[2] // 2
        if i == OO:
            return small_one.at[at, half, pl.ds(way * size, size)]
        return v.at[at, half, pl.ds(way * size + (i - V0) * (size // 2), size // 2)]

    def group(store, at, i, half):
        a, small_one, k, v = store
        if i == A0:
            return a.at[at, :, half]
        if i == K0:
            return k.at[at, :, half]
        return small_one.at[at, half] if i == OO else v.at[at, half]

    def group_of(i):
        return GROUPS.index({A1: A0, V1: V0, K1: K0}.get(i, i))

    weights = (wA, wO, wK, wV)
    grads = (dA, dO, dK, dV)

    def steps_from(l, way):
        home = ring_place(l)
        return (ring - home + RANKS) % RANKS if way == 0 else (home - ring + RANKS) % RANKS

    def forth_copy(l, i, way):
        return remote(
            piece(weights, l, i, way, c),
            piece(weights, l, i, way, c),
            rw_s.at[l, i, way],
            rw_r.at[l, i, way],
            on_ring(1 if way == 0 else RANKS - 1),
            t,
            c,
        )

    def pair_copy(l, i, way):
        g = group_of(i)
        return sibling(
            piece(weights, l, i, way, c),
            piece(weights, l, i, way, c),
            w3_s.at[l, g],
            w3_r.at[l, g],
        )

    def bring(l, i, hop):
        for way in range(2):

            @pl.when(steps_from(l, way) == hop)
            def _():
                if hop:
                    forth_copy(l, i, way).wait_recv()
                if hop < RANKS - 1:
                    forth_copy(l, i, way).start()
                pair_copy(l, i, way).start()

    def serve_forth(l, time):
        for i, slot in FORTH:
            lag = time - slot
            if lag >= 0 and lag % 2 == 0 and lag // 2 < RANKS:
                bring(l, i, lag // 2)

    def weights_here(l, i):
        ref = group(weights, l, i, 1 - c)
        sem = w3_r.at[l, group_of(i)]
        sibling(ref, ref, sem, sem).wait_recv()

    send_carried(0)
    for m in range(4):
        w1_own(m).wait()
        for r in range(1, RANKS):
            w1(m, r).wait_recv()
    for r in range(1, RANKS):
        w1(4, r).start()
    for time in range(2 * RANKS):
        if time == 1:
            w1_own(5).wait()
        if time == 2:
            w1_own(6).wait()
        if time == 4:
            w1_own(4).wait()
            for r in range(1, RANKS):
                w1(4, r).wait_recv()
        serve_forth(0, time)

    for i in range(2):
        src, dst = swaps[i]
        sent_any(swap_self, src, dst, x_s.at[i], x_r.at[i], t, p)
        got_any(swap_self, dst, x_r.at[i])

    def ag(buf, r):
        return peer(buf.at[:, mine], buf.at[:, mine], ag_s.at[r - 1], ag_r.at[r - 1], r)

    def ag_start(buf):
        for r in range(1, RANKS):
            ag(buf, r).start()

    def ag_wait(buf):
        for r in range(1, RANKS):
            ag(buf, r).wait()

    def rs(r):
        theirs = pl.ds(pl.multiple_of(chunk * next_rank(r), chunk), chunk)
        return peer(part.at[:, theirs], rbuf.at[r - 1], rs_s.at[r - 1], rs_r.at[r - 1], r)

    def rs_start(values):
        part[...] = values.astype(BF).reshape(part.shape)
        for r in range(1, RANKS):
            rs(r).start()

    def rs_wait():
        for r in range(1, RANKS):
            rs(r).wait()
        total = part[:, mine, :].astype(F32)
        for r in range(1, RANKS):
            total = total + rbuf[r - 1].astype(F32)
        return total.reshape(micro * chunk, width)

    cur[...] = tokb[...].astype(F32).reshape(cur.shape)

    starts = infob[0:1, 0:seqs]
    ends = infob[8 : 8 + seqs, :]
    line = lax.broadcasted_iota(jnp.int32, (rows, seqs), 0).astype(F32)
    hot = (line == starts).astype(F32)
    onset = jnp.sum(hot, axis=1, keepdims=True)
    stay = 1.0 - onset
    none = jnp.zeros_like(hot)
    hots = [jnp.concatenate(pair, axis=1).astype(BF) for pair in ((hot, none), (none, hot))]
    place_in = line[:, 0:1] - jnp.max(jnp.where(starts <= line, starts, 0.0), axis=1, keepdims=True)
    lane = lax.broadcasted_iota(jnp.int32, (seqs, rows), 1).astype(F32)
    last_hot = (lane == ends).astype(F32)
    last_low = last_hot.astype(BF)
    reaches = []
    reach = 1
    while reach < longest:
        reaches.append(reach)
        reach *= 2

    def whole(ref):
        return ref[...].reshape(rows, ref.shape[-1])

    def before(n, l, which):
        return rolled(n, 1) * stay + dot(hots[which], shb[l])

    def rate(l, i):
        return parb[l, 4 + i : 5 + i, :]

    def fin_args(l):
        return (
            jnp.logical_and(l == p, swap_self),
            finb.at[l],
            finout.at[:, :, my_cols],
            fin_s.at[l],
            fin_r.at[t],
            l,
            p,
        )

    def forward(l, carry):
        def serve(k):
            if k < RANKS:
                serve_forth(l, k + 2 * RANKS)

            @pl.when(l + 1 < layers)
            def _():
                if k == 0:
                    send_carried(l + 1)
                serve_forth(l + 1, k)

        h = cur[...]
        hsave[l] = h
        get_carried(l)
        hat, _ = normed(h)
        n = hat * parb[l, 0:1, :] + parb[l, 2:3, :]
        here = nsave.at[l]
        here[:, mine, :] = n.astype(BF).reshape(micro, chunk, width)
        ag_start(here)
        serve(0)
        serve(1)
        ag_wait(here)
        n = whole(here).astype(F32)
        prev = before(n, l, 0)
        gap = n - prev
        weights_here(l, A0)
        mats = []
        for i in range(3):
            mix = (prev + gap * rate(l, i)).astype(BF)
            mats.append(
                dot(mix, wA[l, :, :, :, i * quarter : (i + 1) * quarter].reshape(width, quarter))
            )
        k, v, r = mats
        w = -jnp.exp(parb[l, 9:10, my_cols])
        u = parb[l, 10:11, my_cols]
        states = stb[l].astype(F32)
        init = [dot(hot, states[i * seqs : (i + 1) * seqs]) for i in range(3)]
        top = jnp.where(onset > 0.5, jnp.maximum(k, w + init[2]), k)
        for s in reaches:
            top = jnp.maximum(top, jnp.where(place_in >= s, rolled(top, s) + s * w, -1e30))
        top_prev = rolled(top, 1) * stay + init[2]
        al = jnp.exp(w + top_prev - top)
        be = jnp.exp(k - top)
        num = be * v + onset * al * init[0]
        den = be + onset * al * init[1]
        keep = al * stay
        for i, s in enumerate(reaches):
            num = num + keep * rolled(num, s)
            den = den + keep * rolled(den, s)
            if i + 1 < len(reaches):
                keep = keep * rolled(keep, s)
        num_prev = rolled(num, 1) * stay + init[0]
        den_prev = rolled(den, 1) * stay + init[1]
        now = u + k
        peak = jnp.maximum(top_prev, now)
        e1 = jnp.exp(top_prev - peak)
        e2 = jnp.exp(now - peak)
        inv = 1.0 / (e1 * den_prev + e2)
        e1 = e1 * inv
        e2 = e2 * inv
        y = e1 * num_prev + e2 * v
        sr = jax.nn.sigmoid(r)
        g = (sr * y).astype(BF)
        weights_here(l, OO)
        rs_start(dot(g, wO[l].reshape(quarter, width)))
        alsave[l] = al
        besave[l] = be
        for i, value in enumerate((v, y, sr, e1, e2, num_prev, den_prev)):
            smsave[l, i] = value.astype(BF)
        for i, value in enumerate((num, den, top)):
            finb[l, i] = dot(last_hot, value, HIGH)
        finb[l, 3] = dot(last_low, nsave[l, :, :, my_cols].reshape(rows, quarter))
        serve(2)
        serve(3)
        m = h + rs_wait()
        msave[l] = m
        hat, _ = normed(m)
        n2 = hat * parb[l, 1:2, :] + parb[l, 3:4, :]
        here = n2save.at[l]
        here[:, mine, :] = n2.astype(BF).reshape(micro, chunk, width)
        ag_start(here)
        serve(4)
        serve(5)
        ag_wait(here)
        n = whole(here).astype(F32)
        prev = before(n, l, 1)
        gap = n - prev
        mix = (prev + gap * rate(l, 4)).astype(BF)
        r2st[...] = (
            dot(mix, wA[l, :, :, :, 3 * quarter :].reshape(width, quarter))
            .astype(BF)
            .reshape(r2st.shape)
        )

        def a2(r):
            theirs = pl.ds(pl.multiple_of(chunk * next_rank(r), chunk), chunk)
            return peer(
                r2st.at[:, theirs], r2full.at[:, :, my_cols], a2_s.at[r - 1], a2_r.at[r - 1], r
            )

        for r in range(1, RANKS):
            a2(r).start()
        r2full[:, :, my_cols] = r2st[:, mine, :]
        mix = (prev + gap * rate(l, 3)).astype(BF)
        weights_here(l, K0)
        z = dot(mix, wK[l].reshape(width, hidden))
        act = jnp.maximum(z, 0.0)
        weights_here(l, V0)
        rs_start(dot((act * act).astype(BF), wV[l].reshape(hidden, width)))
        zsave[l] = z.astype(BF)
        finb[l, 4] = dot(last_low, n2save[l, :, :, my_cols].reshape(rows, quarter))
        start_any(*fin_args(l))
        serve(6)
        serve(7)
        for r in range(1, RANKS):
            a2(r).wait()
        kv = rs_wait()
        gate = jax.nn.sigmoid(r2full[...].astype(F32).reshape(kv.shape))
        kvsave[l] = kv
        gatesave[l] = gate
        result = (m + gate * kv).astype(BF)
        mixb[...] = result.reshape(mixb.shape)
        cur[...] = result.astype(F32)
        return carry

    lax.fori_loop(0, layers, forward, 0)

    for m in range(5):
        for r in range(1, RANKS):
            w1(m, r).wait_send()
    for l in range(layers):
        for i, _ in FORTH:
            for way in range(2):

                @pl.when(steps_from(l, way) < RANKS - 1)
                def _():
                    forth_copy(l, i, way).wait_send()

        for i in GROUPS:
            ref = group(weights, l, i, c)
            sem = w3_s.at[l, group_of(i)]
            sibling(ref, ref, sem, sem).wait_send()

    start_any(swap_self, mixb, mixed, out_s.at[0], out_r.at[0], t, p)
    sent_any(swap_self, cot, cotb, x_s.at[2], x_r.at[2], t, p)
    got_any(swap_self, cotb, x_r.at[2])
    cur[...] = cotb[...].astype(F32).reshape(cur.shape)
    sg[...] = jnp.zeros_like(sg)

    def free(kind):
        for way in range(2):
            pl.semaphore_signal(
                credit.at[kind, way],
                inc=1,
                device_id=(on_ring(1 if way == 0 else RANKS - 1), place(t, c)),
                device_id_type=MESH,
            )
        pl.semaphore_signal(
            sib_credit.at[kind], inc=1, device_id=(p, place(t, 1 - c)), device_id_type=MESH
        )

    def add_to(ours, theirs):
        ours[...] = (ours[...].astype(F32) + theirs[...].astype(F32)).astype(BF)

    def half_copy(l, parity, i):
        g = group_of(i)
        return sibling(
            group(grads, parity, i, 1 - c), group(weights, l, i, c), a_s.at[l, g], a_r.at[l, g]
        )

    def half_sum(l, parity, i):
        half_copy(l, parity, i).wait_recv()
        for j, _ in BACK:
            if GROUPS[group_of(j)] == i:
                for way in range(2):
                    add_to(piece(grads, parity, j, way, c), piece(weights, l, j, way, 1 - c))

    def back_copy(l, parity, i, way):
        return remote(
            piece(grads, parity, i, way, c),
            piece(weights, l, i, way, c),
            rd_s.at[l, i, way],
            rd_r.at[l, i, way],
            on_ring(RANKS - 1 if way == 0 else 1),
            t,
            c,
        )

    def home_args(parity, i, way):
        ours = piece(grads, parity, i, way, c)
        if i in (A0, A1):
            rank = 2 * way + i - A0
            return [
                (
                    t == rank,
                    ours.at[:, pl.ds(m * quarter, quarter)],
                    grad.at[:, my_cols],
                    r1_s.at[m, rank],
                    r1_r.at[m, t],
                    p,
                    rank,
                )
                for m, grad in enumerate((gk, gv, gr, gfr))
            ]
        rank = 2 * way + i - K0
        return [
            (t == rank, ours, gfk.at[:, my_hidden], r1_s.at[4, rank], r1_r.at[4, t], p, rank)
        ]

    def home_own(parity, i, way):
        ours = piece(grads, parity, i, way, c)
        size = ours.shape[0]
        if i == OO:
            return pltpu.make_async_copy(ours, go.at[pl.ds(way * size, size)], r1_l.at[4 + way])
        n = 2 * way + i - V0
        return pltpu.make_async_copy(ours, gfv.at[pl.ds(n * size, size)], r1_l.at[n])

    def collect(l, parity, i, hop):
        for way in range(2):

            @pl.when(steps_from(l, way) == RANKS - 1 - hop)
            def _():
                if i in (V0, A0):
                    pl.semaphore_wait(credit.at[int(i == A0), way], 1)
                if hop:
                    back_copy(l, parity, i, way).wait_recv()
                    add_to(piece(grads, parity, i, way, c), piece(weights, l, i, way, c))
                if hop < RANKS - 1:
                    back_copy(l, parity, i, way).start()
                elif i in (V0, V1, OO):
                    home_own(parity, i, way).start()
                else:
                    for args in home_args(parity, i, way):
                        start_any(*args)

    def serve_back(l, parity, time):
        for i, when in ((V0, 0), (K0, 2), (A0, 4), (OO, 5)):
            if time == when:
                half_sum(l, parity, i)
        for i, slot in BACK:
            lag = time - slot
            if lag >= 0 and lag % 2 == 0 and lag // 2 < RANKS:
                collect(l, parity, i, lag // 2)

    def all_sent(l, parity):
        for i, _ in BACK:
            for way in range(2):

                @pl.when(steps_from(l, way) != 0)
                def _():
                    back_copy(l, parity, i, way).wait_send()

        @pl.when(l == p)
        def _():
            for i, _ in BACK:
                for way in range(2):
                    if i in (V0, V1, OO):
                        home_own(parity, i, way).wait()
                    else:
                        for args in home_args(parity, i, way):
                            sent_any(*args)

    def backward(step, carry):
        l = layers - 1 - step
        parity = step % 2

        def serve(k):
            if k >= RANKS:
                serve_back(l, parity, k - RANKS)

            @pl.when(step > 0)
            def _():
                serve_back(l + 1, 1 - parity, k + RANKS)

        dout = cur[...]
        gate = gatesave[l]
        dkvall[:, mine, :] = (dout * gate).astype(BF).reshape(micro, chunk, width)
        ag_start(dkvall)
        dr2o[...] = (dout * kvsave[l] * gate * (1.0 - gate)).astype(BF).reshape(dr2o.shape)

        def a2(r):
            theirs = pl.ds(pl.multiple_of(quarter * next_rank(r), quarter), quarter)
            return peer(
                dr2o.at[:, :, theirs], dr2c.at[:, mine], a2b_s.at[r - 1], a2b_r.at[r - 1], r
            )

        for r in range(1, RANKS):
            a2(r).start()
        dr2c[:, mine, :] = dr2o[:, :, my_cols]
        n = n2save[l].reshape(rows, width).astype(F32)
        prev = before(n, l, 1)
        gap = n - prev
        act = jnp.maximum(zsave[l].astype(F32), 0.0)
        serve(0)
        serve(1)
        ag_wait(dkvall)
        for r in range(1, RANKS):
            a2(r).wait()
        dkv = whole(dkvall)
        dz = (2.0 * act * dot_nt(dkv, wV[l].reshape(hidden, width))).astype(BF)
        dr2 = whole(dr2c)
        dx = dot_nt(dz, wK[l].reshape(width, hidden))
        dxr = dot_nt(dr2, wA[l, :, :, :, 3 * quarter :].reshape(width, quarter))
        mixed_part = dx * rate(l, 3) + dxr * rate(l, 4)
        shifted = (dx + dxr - mixed_part) * stay
        rs_start(mixed_part + rolled(shifted, rows - 1))
        free(0)
        sg[l, 7:8, :] = column_sum(dx * gap)
        sg[l, 8:9, :] = column_sum(dxr * gap)

        @pl.when(step > 1)
        def _():
            all_sent(l + 2, parity)

        squared = (act * act).astype(BF)
        size = dV.shape[2] // RANKS
        for b in range(HALVES * RANKS):
            half, q = b // RANKS, b % RANKS
            dV[parity, half, q * size : (q + 1) * size, :] = dot_tn(
                squared[:, b * size : (b + 1) * size], dkv
            ).astype(BF)
        mix = (prev + gap * rate(l, 3)).astype(BF)
        for b in range(HALVES * RANKS):
            dK[parity, b // HALVES, b % HALVES] = dot_tn(
                mix[:, b * block : (b + 1) * block], dz
            ).astype(BF)
        mix = (prev + gap * rate(l, 4)).astype(BF)
        for b in range(HALVES * RANKS):
            dA[parity, b // HALVES, b % HALVES, :, 3 * quarter :] = dot_tn(
                mix[:, b * block : (b + 1) * block], dr2
            ).astype(BF)
        pl.semaphore_wait(sib_credit.at[0], 1)
        half_copy(l, parity, V0).start()
        half_copy(l, parity, K0).start()
        serve(2)
        serve(3)

        dn = rs_wait()
        hat, rstd = normed(msave[l])
        sg[l, 1:2, :] = column_sum(dn * hat)
        sg[l, 3:4, :] = column_sum(dn)
        dm = dout + norm_back(dn, parb[l, 1:2, :], hat, rstd)
        dmall[:, mine, :] = dm.astype(BF).reshape(micro, chunk, width)
        ag_start(dmall)
        n = nsave[l].reshape(rows, width).astype(F32)
        prev = before(n, l, 0)
        gap = n - prev
        al = alsave[l]
        be = besave[l]
        v, y, sr, e1, e2, num_prev, den_prev = [smsave[l, i].astype(F32) for i in range(7)]
        w = -jnp.exp(parb[l, 9:10, my_cols])
        serve(4)
        serve(5)
        ag_wait(dmall)
        dmw = whole(dmall)
        dg = dot_nt(dmw, wO[l].reshape(quarter, width))
        dr = (dg * y * sr * (1.0 - sr)).astype(BF)
        dy = dg * sr
        keep = rolled(al * stay, rows - 1)
        into = dy * e1 * stay
        ga = rolled(into, rows - 1)
        gb = -rolled(into * y, rows - 1)
        for i, s in enumerate(reaches):
            ga = ga + keep * rolled(ga, rows - s)
            gb = gb + keep * rolled(gb, rows - s)
            if i + 1 < len(reaches):
                keep = keep * rolled(keep, rows - s)
        near = dy * e2
        now = near * (v - y)
        dv = (be * ga + near).astype(BF)
        dk = (be * (v * ga + gb) + now).astype(BF)
        sg[l, 9:10, my_cols] = w * column_sum(al * (ga * num_prev + gb * den_prev))
        sg[l, 10:11, my_cols] = column_sum(now)
        lefts = (dk, dv, dr)
        total = None
        mixed_part = None
        for i in range(3):
            dx = dot_nt(
                lefts[i], wA[l, :, :, :, i * quarter : (i + 1) * quarter].reshape(width, quarter)
            )
            sg[l, 4 + i : 5 + i, :] = column_sum(dx * gap)
            scaled = dx * rate(l, i)
            total = dx if total is None else total + dx
            mixed_part = scaled if mixed_part is None else mixed_part + scaled
        shifted = (total - mixed_part) * stay
        rs_start(mixed_part + rolled(shifted, rows - 1))
        free(1)

        g = (sr * y).astype(BF)
        size = dO.shape[2]
        for half in range(HALVES):
            dO[parity, half] = dot_tn(g[:, half * size : (half + 1) * size], dmw).astype(BF)
        for i in range(3):
            mix = (prev + gap * rate(l, i)).astype(BF)
            for b in range(HALVES * RANKS):
                dA[parity, b // HALVES, b % HALVES, :, i * quarter : (i + 1) * quarter] = dot_tn(
                    mix[:, b * block : (b + 1) * block], lefts[i]
                ).astype(BF)
        pl.semaphore_wait(sib_credit.at[1], 1)
        half_copy(l, parity, A0).start()
        half_copy(l, parity, OO).start()
        serve(6)
        serve(7)

        dn = rs_wait()
        hat, rstd = normed(hsave[l])
        sg[l, 0:1, :] = column_sum(dn * hat)
        sg[l, 2:3, :] = column_sum(dn)
        dh = dm + norm_back(dn, parb[l, 0:1, :], hat, rstd)
        result = dh.astype(BF)
        gradb[...] = result.reshape(gradb.shape)
        cur[...] = result.astype(F32)
        for i in GROUPS:
            half_copy(l, parity, i).wait_send()
        return carry

    lax.fori_loop(0, layers, backward, 0)

    tg_args = (swap_self, gradb, tgrad, out_s.at[1], out_r.at[1], t, p)
    start_any(*tg_args)

    def sg_copy(r):
        return plane(sg.at[next_pipe(r)], sgr.at[r - 1], sg_s.at[r - 1], sg_r.at[r - 1], r)

    lanes = sg8.shape[-1]

    def sg_cols(rank, half):
        return pl.ds(pl.multiple_of(lanes * (rank * HALVES + half), lanes), lanes)

    def sg8_copy(a, b):
        rank, half = next_rank(a), (c + b) % HALVES
        n = a * HALVES + b
        return remote(
            sgt.at[:, sg_cols(rank, half)], sg8.at[n], sg8_s.at[n], sg8_r.at[n], p, rank, half
        )

    others = [(a, b) for a in range(RANKS) for b in range(HALVES) if a or b]
    for r in range(1, RANKS):
        sg_copy(r).start()
    last = (layers - 1) % 2
    for time in range(RANKS, 3 * RANKS):
        serve_back(0, last, time)
        if time == RANKS + 1:
            for r in range(1, RANKS):
                sg_copy(r).wait()
            total = sg[p]
            for r in range(1, RANKS):
                total = total + sgr[r - 1]
            sgt[...] = total
            for a, b in others:
                sg8_copy(a, b).start()
        if time == RANKS + 3:
            total = sgt[:, sg_cols(t, c)]
            for a, b in others:
                sg8_copy(a, b).wait()
                total = total + sg8[a * HALVES + b]
            small[...] = total

    for l in range(layers):
        sent_any(*fin_args(l))
    for r in range(1, RANKS):
        par_copy(r).wait_send()
    carried_sent()
    sent_any(swap_self, mixb, mixed, out_s.at[0], out_r.at[0], t, p)
    got_any(swap_self, mixed, out_r.at[0])
    sent_any(*tg_args)
    got_any(swap_self, tgrad, out_r.at[1])
    all_sent(1, (layers - 2) % 2)
    all_sent(0, last)
    for src in range(RANKS):
        cols = pl.ds(src * quarter, quarter)
        got_any(jnp.logical_and(swap_self, t == src), finout.at[:, :, cols], fin_r.at[src])
        for m, grad in enumerate((gk, gv, gr, gfr)):
            got_any(t == src, grad.at[:, cols], r1_r.at[m, src])
        got_any(t == src, gfk.at[:, pl.ds(src * hidden, hidden)], r1_r.at[4, src])


def on_device(
    outer,
    tokens,
    cotangent,
    lengths,
    carried,
    norm_gain,
    norm_bias,
    mix_rates,
    time_decay,
    time_first,
    attention_accept_proj,
    attention_lookup_proj,
    attention_content_proj,
    attention_result_proj,
    feedforward_accept_proj,
    feedforward_lookup_proj,
    feedforward_content_proj,
):
    layers = lax.axis_size("pipe")
    micro, chunk, width = tokens.shape
    row_count = chunk * RANKS
    rows = micro * row_count
    per = lengths.shape[1]
    seqs = micro * per
    weights = [
        attention_lookup_proj[0],
        attention_content_proj[0],
        attention_accept_proj[0],
        feedforward_accept_proj[0],
        attention_result_proj[0],
        feedforward_lookup_proj[0],
        feedforward_content_proj[0],
    ]
    near = [[b * outer + i for i in range(outer)] for b in range(RANKS * HALVES)]
    if outer > 1:
        weights = [
            lax.all_gather(w, "dp", axis=0, tiled=True, axis_index_groups=near) for w in weights
        ]
    block = width // (RANKS * HALVES)
    hidden = weights[5].shape[1] // RANKS
    quarter = width // RANKS
    vmem = pl.BlockSpec(memory_space=pltpu.VMEM)
    smem = pl.BlockSpec(memory_space=pltpu.SMEM)
    hbm = pl.BlockSpec(memory_space=pl.ANY)
    dma = pltpu.SemaphoreType.DMA
    regular = pltpu.SemaphoreType.REGULAR
    n_peers = RANKS - 1
    own = (micro, chunk, width)
    full = (micro, row_count, width)

    def stores(count):
        return [
            pltpu.VMEM((count, RANKS, HALVES, block, width), BF),
            pltpu.VMEM((count, HALVES, block, width), BF),
            pltpu.VMEM((count, RANKS, HALVES, block, hidden), BF),
            pltpu.VMEM((count, HALVES, hidden // HALVES, width), BF),
        ]

    outs = pl.pallas_call(
        partial(layers_kernel, outer, row_count // 2),
        out_shape=(
            jax.ShapeDtypeStruct(own, BF),
            jax.ShapeDtypeStruct(own, BF),
            jax.ShapeDtypeStruct((5, seqs, width), F32),
            jax.ShapeDtypeStruct((16, block), F32),
        )
        + tuple(jax.ShapeDtypeStruct(w.shape, BF) for w in weights),
        in_specs=[vmem] * 2 + [smem] + [vmem] * 6 + [hbm] * 7,
        out_specs=(vmem,) * 4 + (hbm,) * 7,
        scratch_shapes=stores(layers)
        + stores(2)
        + [
            pltpu.VMEM(own, BF),
            pltpu.VMEM(own, BF),
            pltpu.VMEM((16, 128), F32),
            pltpu.VMEM((16, 128), F32),
            pltpu.VMEM((32, width), BF),
            pltpu.VMEM((layers, 32, quarter), BF),
            pltpu.VMEM((16, width), BF),
            pltpu.VMEM((layers, 16, width), BF),
            pltpu.VMEM((16, width), F32),
            pltpu.VMEM((layers, 16, width), F32),
            pltpu.VMEM((layers,) + full, BF),
            pltpu.VMEM((layers,) + full, BF),
            pltpu.VMEM((layers, micro * chunk, width), F32),
            pltpu.VMEM((layers, micro * chunk, width), F32),
            pltpu.VMEM((layers, micro * chunk, width), F32),
            pltpu.VMEM((layers, micro * chunk, width), F32),
            pltpu.VMEM((layers, rows, hidden), BF),
            pltpu.VMEM((layers, rows, quarter), F32),
            pltpu.VMEM((layers, rows, quarter), F32),
            pltpu.VMEM((layers, 7, rows, quarter), BF),
            pltpu.VMEM(full, BF),
            pltpu.VMEM((n_peers,) + own, BF),
            pltpu.VMEM((micro, row_count, quarter), BF),
            pltpu.VMEM(own, BF),
            pltpu.VMEM((micro * chunk, width), F32),
            pltpu.VMEM((layers, 5, seqs, quarter), F32),
            pltpu.VMEM(own, BF),
            pltpu.VMEM(own, BF),
            pltpu.VMEM(full, BF),
            pltpu.VMEM(full, BF),
            pltpu.VMEM(own, BF),
            pltpu.VMEM((micro, row_count, quarter), BF),
            pltpu.VMEM((layers, 16, width), F32),
            pltpu.VMEM((n_peers, 16, width), F32),
            pltpu.VMEM((16, width), F32),
            pltpu.VMEM((RANKS * HALVES, 16, block), F32),
            dma((3,)),
            dma((3,)),
            dma((RANKS,)),
            dma((layers,)),
            dma((RANKS,)),
            dma((layers,)),
            dma((n_peers,)),
            dma((layers,)),
            dma((5, n_peers)),
            dma((5, n_peers)),
            dma((7,)),
            dma((layers, 7, 2)),
            dma((layers, 7, 2)),
            dma((layers, 4)),
            dma((layers, 4)),
            dma((n_peers,)),
            dma((n_peers,)),
            dma((n_peers,)),
            dma((n_peers,)),
            dma((n_peers,)),
            dma((n_peers,)),
            dma((n_peers,)),
            dma((n_peers,)),
            dma((layers,)),
            dma((RANKS,)),
            dma((2,)),
            dma((2,)),
            dma((layers, 4)),
            dma((layers, 4)),
            dma((layers, 7, 2)),
            dma((layers, 7, 2)),
            dma((5, RANKS)),
            dma((5, RANKS)),
            dma((6,)),
            dma((n_peers,)),
            dma((n_peers,)),
            dma((RANKS * HALVES,)),
            dma((RANKS * HALVES,)),
            regular((2, 2)),
            regular((2,)),
        ],
        compiler_params=pltpu.CompilerParams(
            collective_id=0, has_side_effects=True, vmem_limit_bytes=60 * 2**20
        ),
        name="layers",
    )(
        tokens,
        cotangent,
        lengths,
        carried,
        norm_gain,
        norm_bias,
        mix_rates,
        time_decay,
        time_first,
        *weights,
    )
    mixed, tgrad, fin, small, *grads = outs
    if outer > 1:
        grads = [
            lax.psum_scatter(g, "dp", scatter_dimension=0, tiled=True, axis_index_groups=near)
            for g in grads
        ]
        small = lax.psum_scatter(
            small, "dp", scatter_dimension=1, tiled=True, axis_index_groups=near
        )
    gk, gv, gr, gfr, go, gfk, gfv = [g.astype(F32)[None] for g in grads]
    small = small[None]
    return (
        mixed,
        tgrad.astype(F32),
        fin.transpose(1, 0, 2).reshape(micro, per, 1, 5, width),
        small[:, 0:2],
        small[:, 2:4],
        small[:, 4:9],
        small[:, 9],
        small[:, 10],
        gr,
        gk,
        gv,
        go,
        gfr,
        gfk,
        gfv,
    )


def solution(mesh):
    outer = mesh.shape["dp"] // (RANKS * HALVES)
    placed = (
        P("dp", "pipe", None),
        P("dp", "pipe", None),
        P("dp", None),
        P("dp", None, "pipe", None, None),
        P("pipe", None, None),
        P("pipe", None, None),
        P("pipe", None, None),
        P("pipe", None),
        P("pipe", None),
    ) + (P("pipe", "dp", None),) * 7
    return jax.shard_map(
        partial(on_device, outer),
        mesh=mesh,
        in_specs=placed,
        out_specs=(
            P("dp", "pipe", None),
            P("dp", "pipe", None),
            P("dp", None, "pipe", None, None),
            P("pipe", None, "dp"),
            P("pipe", None, "dp"),
            P("pipe", None, "dp"),
            P("pipe", "dp"),
            P("pipe", "dp"),
        )
        + (P("pipe", "dp", None),) * 7,
        check_vma=False,
    )
```

```python
from functools import partial

import jax
import jax.numpy as jnp
from jax import lax
from jax.sharding import PartitionSpec as P
from jax.experimental import pallas as pl
from jax.experimental.pallas import tpu as pltpu

EPS = 1e-05
BF = jnp.bfloat16
F32 = jnp.float32
HIGH = lax.Precision.HIGHEST
MESH = pl.DeviceIdType.MESH
RANKS = 4
HALVES = 2


def dot(a, b, precision=None):
    return jnp.dot(a, b, precision=precision, preferred_element_type=F32)


def dot_nt(a, b):
    return lax.dot_general(a, b, (((1,), (1,)), ((), ())), preferred_element_type=F32)


def dot_tn(a, b):
    return lax.dot_general(a, b, (((0,), (0,)), ((), ())), preferred_element_type=F32)


def rolled(x, shift):
    return pltpu.roll(x, shift % x.shape[0], 0)


def normed(h):
    center = h - jnp.mean(h, axis=-1, keepdims=True)
    spread = jnp.mean(center * center, axis=-1, keepdims=True)
    rstd = lax.rsqrt(spread + EPS)
    return center * rstd, rstd


def norm_back(dn, gain, hat, rstd):
    dh = dn * gain
    return rstd * (
        dh
        - jnp.mean(dh, axis=-1, keepdims=True)
        - hat * jnp.mean(dh * hat, axis=-1, keepdims=True)
    )


def column_sum(x):
    return jnp.sum(x, axis=0, keepdims=True)


def ring_place(pipe):
    return pipe + (pipe // 2) * (5 - 2 * pipe)


A0, A1, V0, V1, K0, K1, OO = range(7)
FORTH = (
    (0, A0, (-6, -4, 0, 1)),
    (0, A1, (-5, -3, 0, 1)),
    (0, OO, (-8, -7, -5, -3)),
    (0, V0, (-8, -5, -2, 4)),
    (0, V1, (-8, -2, 1, 4)),
    (0, K0, (-1, 1, 4, 5)),
    (0, K1, (-1, 1, 4, 5)),
    (1, A0, (-5, -2, -1, 2)),
    (1, A1, (2, 5, 6, 9)),
    (1, OO, (-8, -6, 2, 7)),
    (1, K0, (0, 6, 7, 10)),
    (1, K1, (2, 7, 10, 13)),
    (1, V0, (-2, 7, 10, 13)),
    (1, V1, (-7, 2, 3, 9)),
    (2, A0, (-1, 4, 7, 12)),
    (2, A1, (-5, 6, 12, 14)),
    (2, OO, (-8, 6, 9, 16)),
    (2, K0, (5, 11, 14, 17)),
    (2, K1, (1, 13, 18, 20)),
    (2, V0, (-8, -4, 2, 11)),
    (2, V1, (-6, -1, 6, 10)),
    (3, A0, (12, 15, 18, 22)),
    (3, A1, (-3, 1, 13, 17)),
    (3, OO, (-4, 0, 19, 22)),
    (3, K0, (10, 13, 16, 21)),
    (3, K1, (1, 11, 20, 23)),
    (3, V0, (8, 19, 24, 27)),
    (3, V1, (13, 18, 26, 28)),
)
BACK = (
    (0, V0, (4, 6, 8, 15)),
    (0, V1, (5, 7, 10, 17)),
    (0, K0, (8, 10, 13, 17)),
    (0, K1, (6, 8, 11, 16)),
    (0, A0, (10, 14, 17, 20)),
    (0, A1, (12, 15, 17, 20)),
    (0, OO, (8, 10, 13, 18)),
    (1, V0, (16, 18, 22, 24)),
    (1, V1, (12, 14, 16, 21)),
    (1, K0, (12, 15, 18, 20)),
    (1, K1, (12, 16, 19, 25)),
    (1, A0, (21, 24, 25, 28)),
    (1, A1, (16, 20, 23, 25)),
    (1, OO, (22, 25, 27, 28)),
    (2, V0, (22, 25, 27, 36)),
    (2, V1, (21, 22, 25, 28)),
    (2, K0, (20, 21, 23, 31)),
    (2, K1, (28, 29, 32, 40)),
    (2, A0, (30, 35, 39, 40)),
    (2, A1, (24, 26, 28, 40)),
    (2, OO, (24, 27, 29, 36)),
    (3, V0, (30, 36, 37, 40)),
    (3, V1, (28, 29, 30, 31)),
    (3, K0, (28, 30, 35, 36)),
    (3, K1, (29, 34, 35, 36)),
    (3, A0, (34, 38, 39, 40)),
    (3, A1, (34, 38, 39, 40)),
    (3, OO, (32, 36, 37, 39)),
)
PIECES = range(7)
SERVICES = 8
GROUPS = (A0, V0, K0, OO)


def layers_kernel(
    outer,
    longest,
    tok,
    cot,
    lens,
    held,
    gain,
    bias,
    mixes,
    decay,
    first,
    wk,
    wv,
    wr,
    wfr,
    wo,
    wfk,
    wfv,
    mixed,
    tgrad,
    finout,
    small,
    gk,
    gv,
    gr,
    gfr,
    go,
    gfk,
    gfv,
    wA,
    wO,
    wK,
    wV,
    dA,
    dO,
    dK,
    dV,
    tokb,
    cotb,
    info,
    infob,
    stsrc,
    stb,
    shsrc,
    shb,
    par,
    parb,
    nsave,
    n2save,
    hsave,
    msave,
    kvsave,
    gatesave,
    zsave,
    alsave,
    besave,
    smsave,
    part,
    rbuf,
    r2st,
    r2full,
    cur,
    finb,
    mixb,
    gradb,
    dkvall,
    dmall,
    dr2o,
    dr2c,
    sg,
    sgr,
    sgt,
    sg8,
    x_s,
    x_r,
    st_s,
    st_r,
    sh_s,
    sh_r,
    par_s,
    par_r,
    w1_s,
    w1_r,
    w1_l,
    rw_s,
    rw_r,
    w3_s,
    w3_r,
    ag_s,
    ag_r,
    rs_s,
    rs_r,
    a2_s,
    a2_r,
    a2b_s,
    a2b_r,
    fin_s,
    fin_r,
    out_s,
    out_r,
    a_s,
    a_r,
    rd_s,
    rd_r,
    r1_s,
    r1_r,
    r1_l,
    sg_s,
    sg_r,
    sg8_s,
    sg8_r,
    credit,
    sib_credit,
):
    p = lax.axis_index("pipe")
    d = lax.axis_index("dp")
    t = d // (HALVES * outer)
    c = (d // outer) % HALVES
    o = d % outer
    ring = ring_place(p)
    micro, chunk, width = tok.shape
    layers = stb.shape[0]
    rows = micro * chunk * RANKS
    quarter = width // RANKS
    mine = pl.ds(pl.multiple_of(chunk * t, chunk), chunk)
    my_cols = pl.ds(pl.multiple_of(quarter * t, quarter), quarter)
    hidden = wfk.shape[1] // RANKS
    my_hidden = pl.ds(pl.multiple_of(hidden * t, hidden), hidden)
    block = wk.shape[0]
    seqs = held.shape[0] * held.shape[1]
    per = held.shape[1]

    def place(rank, half):
        return (rank * HALVES + half) * outer + o

    def next_rank(r):
        return (t + r) % RANKS

    def next_pipe(r):
        return (p + r) % RANKS

    def on_ring(r):
        return ring_place((ring + r) % RANKS)

    def remote(src, dst, ss, rs, pipe, rank, half):
        return pltpu.make_async_remote_copy(
            src_ref=src,
            dst_ref=dst,
            send_sem=ss,
            recv_sem=rs,
            device_id=(pipe, place(rank, half)),
            device_id_type=MESH,
        )

    def peer(src, dst, ss, rs, r):
        return remote(src, dst, ss, rs, p, next_rank(r), c)

    def plane(src, dst, ss, rs, r):
        return remote(src, dst, ss, rs, next_pipe(r), t, c)

    def sibling(src, dst, ss, rs):
        return remote(src, dst, ss, rs, p, t, 1 - c)

    def start_any(is_self, src, dst, ss, rs, pipe, rank):
        @pl.when(is_self)
        def _():
            pltpu.make_async_copy(src, dst, ss).start()

        @pl.when(jnp.logical_not(is_self))
        def _():
            remote(src, dst, ss, rs, pipe, rank, c).start()

    def sent_any(is_self, src, dst, ss, rs, pipe, rank):
        @pl.when(is_self)
        def _():
            pltpu.make_async_copy(src, dst, ss).wait()

        @pl.when(jnp.logical_not(is_self))
        def _():
            remote(src, dst, ss, rs, pipe, rank, c).wait_send()

    def got(dst, rs):
        remote(dst, dst, rs, rs, next_pipe(1), t, c).wait_recv()

    def got_any(is_self, dst, rs):
        @pl.when(jnp.logical_not(is_self))
        def _():
            got(dst, rs)

    barrier = pltpu.get_barrier_semaphore()
    for a in range(RANKS):
        for b in range(RANKS):
            if a or b:
                pl.semaphore_signal(
                    barrier,
                    inc=1,
                    device_id=(next_pipe(a), place(next_rank(b), c)),
                    device_id_type=MESH,
                )
    for b in range(RANKS):
        pl.semaphore_signal(
            barrier, inc=1, device_id=(p, place(next_rank(b), 1 - c)), device_id_type=MESH
        )
    pl.semaphore_wait(barrier, RANKS * RANKS - 1 + RANKS)

    raw = (wk, wv, wr, wfr)

    def w1(m, r):
        rank = next_rank(r)
        if m < 4:
            cols = pl.ds(pl.multiple_of(quarter * rank, quarter), quarter)
            return peer(
                raw[m].at[:, cols],
                wA.at[p, t, c, :, pl.ds(m * quarter, quarter)],
                w1_s.at[m, r - 1],
                w1_r.at[m, r - 1],
                r,
            )
        cols = pl.ds(pl.multiple_of(hidden * rank, hidden), hidden)
        return peer(wfk.at[:, cols], wK.at[p, t, c], w1_s.at[m, r - 1], w1_r.at[m, r - 1], r)

    def w1_own(m):
        if m < 4:
            return pltpu.make_async_copy(
                raw[m].at[:, my_cols], wA.at[p, t, c, :, pl.ds(m * quarter, quarter)], w1_l.at[m]
            )
        if m == 4:
            return pltpu.make_async_copy(wfk.at[:, my_hidden], wK.at[p, t, c], w1_l.at[m])
        if m == 5:
            return pltpu.make_async_copy(wo, wO.at[p, c], w1_l.at[m])
        return pltpu.make_async_copy(wfv, wV.at[p, c], w1_l.at[m])

    for m in range(4):
        for r in range(1, RANKS):
            w1(m, r).start()
    for m in range(7):
        w1_own(m).start()

    lane = lax.broadcasted_iota(jnp.int32, info.shape, 1)
    line = lax.broadcasted_iota(jnp.int32, info.shape, 0)
    marks = jnp.full(info.shape, -1, jnp.int32)
    for b in range(micro):
        at = b * (rows // micro)
        for s in range(per):
            index = b * per + s
            marks = jnp.where(jnp.logical_and(line == 0, lane == index), at, marks)
            at = at + lens[b, s]
            marks = jnp.where(line == 8 + index, at - 1, marks)
    info[...] = marks.astype(F32)

    swap_self = p == t
    swaps = [(tok, tokb), (info, infob), (cot, cotb)]
    for i, (src, dst) in enumerate(swaps):
        start_any(swap_self, src, dst, x_s.at[i], x_r.at[i], t, p)

    par[0:2, :] = gain[0]
    par[2:4, :] = bias[0]
    par[4:9, :] = mixes[0]
    par[9:10, :] = decay[...]
    par[10:11, :] = first[...]
    par[11:16, :] = jnp.zeros((5, width), F32)

    def par_copy(r):
        return plane(par, parb.at[p], par_s.at[r - 1], par_r.at[p], r)

    for r in range(1, RANKS):
        par_copy(r).start()
    parb[p] = par[...]

    carried_rows = held[:, :, 0].reshape(seqs, 5, width)
    spare = jnp.zeros((8, width), F32)
    stsrc[...] = jnp.concatenate([carried_rows[:, i] for i in range(3)] + [spare], axis=0).astype(BF)
    shsrc[...] = jnp.concatenate([carried_rows[:, 3], carried_rows[:, 4]], axis=0).astype(BF)

    def state_args(rank):
        return (
            jnp.logical_and(swap_self, rank == t),
            stsrc.at[:, pl.ds(quarter * rank, quarter)],
            stb.at[p],
            st_s.at[rank],
            st_r.at[p],
            t,
            rank,
        )

    def shift_args(rank):
        return (
            jnp.logical_and(swap_self, rank == t),
            shsrc,
            shb.at[p],
            sh_s.at[rank],
            sh_r.at[p],
            t,
            rank,
        )

    def send_carried(l):
        @pl.when(p == l)
        def _():
            for rank in range(RANKS):
                start_any(*shift_args(rank))
                start_any(*state_args(rank))

    def get_carried(l):
        from_self = jnp.logical_and(swap_self, p == l)

        @pl.when(from_self)
        def _():
            for rank in range(RANKS):

                @pl.when(rank == t)
                def _():
                    pltpu.make_async_copy(*shift_args(rank)[1:4]).wait()
                    pltpu.make_async_copy(*state_args(rank)[1:4]).wait()

        got_any(from_self, shb.at[l], sh_r.at[l])
        got_any(from_self, stb.at[l], st_r.at[l])
        got_any(p == l, parb.at[l], par_r.at[l])

    def carried_sent():
        for rank in range(RANKS):

            @pl.when(jnp.logical_not(jnp.logical_and(swap_self, rank == t)))
            def _():
                remote(*shift_args(rank)[1:], c).wait_send()
                remote(*state_args(rank)[1:], c).wait_send()

    def piece(store, at, i, way, half):
        a, small_one, k, v = store
        if i in (A0, A1):
            return a.at[at, 2 * way + i - A0, half]
        if i in (K0, K1):
            return k.at[at, 2 * way + i - K0, half]
        size = (small_one if i == OO else v).shape[2] // 2
        if i == OO:
            return small_one.at[at, half, pl.ds(way * size, size)]
        return v.at[at, half, pl.ds(way * size + (i - V0) * (size // 2), size // 2)]

    def group(store, at, i, half):
        a, small_one, k, v = store
        if i == A0:
            return a.at[at, :, half]
        if i == K0:
            return k.at[at, :, half]
        return small_one.at[at, half] if i == OO else v.at[at, half]

    def group_of(i):
        return GROUPS.index({A1: A0, V1: V0, K1: K0}.get(i, i))

    weights = (wA, wO, wK, wV)
    grads = (dA, dO, dK, dV)

    def steps_from(l, way):
        home = ring_place(l)
        return (ring - home + RANKS) % RANKS if way == 0 else (home - ring + RANKS) % RANKS

    def forth_copy(l, i, way):
        return remote(
            piece(weights, l, i, way, c),
            piece(weights, l, i, way, c),
            rw_s.at[l, i, way],
            rw_r.at[l, i, way],
            on_ring(1 if way == 0 else RANKS - 1),
            t,
            c,
        )

    def pair_copy(l, i, way):
        g = group_of(i)
        return sibling(
            piece(weights, l, i, way, c),
            piece(weights, l, i, way, c),
            w3_s.at[l, g],
            w3_r.at[l, g],
        )

    def bring(l, i, hop):
        for way in range(2):

            @pl.when(steps_from(l, way) == hop)
            def _():
                if hop:
                    forth_copy(l, i, way).wait_recv()
                if hop < RANKS - 1:
                    forth_copy(l, i, way).start()
                pair_copy(l, i, way).start()

    def due(plan, time):
        for l, i, slots in plan:
            for hop, slot in enumerate(slots):
                if slot == time:
                    yield l, i, hop

    def first_of(l, pieces):
        return min((slots[0], n, i) for n, (at, i, slots) in enumerate(FORTH) if at == l and i in pieces)[2]

    def serve_forth(time):
        for l, i, hop in due(FORTH, time):
            if hop == 0:

                @pl.when(p == l)
                def _():
                    if i == first_of(l, (A0, A1)):
                        for m in range(4):
                            w1_own(m).wait()
                            for r in range(1, RANKS):
                                w1(m, r).wait_recv()
                        for r in range(1, RANKS):
                            w1(4, r).start()
                    if i == first_of(l, (K0, K1)):
                        w1_own(4).wait()
                        for r in range(1, RANKS):
                            w1(4, r).wait_recv()
                    if i == OO:
                        w1_own(5).wait()
                    if i == first_of(l, (V0, V1)):
                        w1_own(6).wait()

            bring(l, i, hop)

    def weights_here(l, i):
        ref = group(weights, l, i, 1 - c)
        sem = w3_r.at[l, group_of(i)]
        sibling(ref, ref, sem, sem).wait_recv()

    send_carried(0)
    for time in range(-SERVICES, 0):
        serve_forth(time)

    for i in range(2):
        src, dst = swaps[i]
        sent_any(swap_self, src, dst, x_s.at[i], x_r.at[i], t, p)
        got_any(swap_self, dst, x_r.at[i])

    def ag(buf, r):
        return peer(buf.at[:, mine], buf.at[:, mine], ag_s.at[r - 1], ag_r.at[r - 1], r)

    def ag_start(buf):
        for r in range(1, RANKS):
            ag(buf, r).start()

    def ag_wait(buf):
        for r in range(1, RANKS):
            ag(buf, r).wait()

    def rs(r):
        theirs = pl.ds(pl.multiple_of(chunk * next_rank(r), chunk), chunk)
        return peer(part.at[:, theirs], rbuf.at[r - 1], rs_s.at[r - 1], rs_r.at[r - 1], r)

    def rs_start(values):
        part[...] = values.astype(BF).reshape(part.shape)
        for r in range(1, RANKS):
            rs(r).start()

    def rs_wait():
        for r in range(1, RANKS):
            rs(r).wait()
        total = part[:, mine, :].astype(F32)
        for r in range(1, RANKS):
            total = total + rbuf[r - 1].astype(F32)
        return total.reshape(micro * chunk, width)

    cur[...] = tokb[...].astype(F32).reshape(cur.shape)

    starts = infob[0:1, 0:seqs]
    ends = infob[8 : 8 + seqs, :]
    line = lax.broadcasted_iota(jnp.int32, (rows, seqs), 0).astype(F32)
    hot = (line == starts).astype(F32)
    onset = jnp.sum(hot, axis=1, keepdims=True)
    stay = 1.0 - onset
    none = jnp.zeros_like(hot)
    hots = [jnp.concatenate(pair, axis=1).astype(BF) for pair in ((hot, none), (none, hot))]
    place_in = line[:, 0:1] - jnp.max(jnp.where(starts <= line, starts, 0.0), axis=1, keepdims=True)
    lane = lax.broadcasted_iota(jnp.int32, (seqs, rows), 1).astype(F32)
    last_hot = (lane == ends).astype(F32)
    last_low = last_hot.astype(BF)
    reaches = []
    reach = 1
    while reach < longest:
        reaches.append(reach)
        reach *= 2

    def whole(ref):
        return ref[...].reshape(rows, ref.shape[-1])

    def before(n, l, which):
        return rolled(n, 1) * stay + dot(hots[which], shb[l])

    def rate(l, i):
        return parb[l, 4 + i : 5 + i, :]

    def fin_args(l):
        return (
            jnp.logical_and(l == p, swap_self),
            finb.at[l],
            finout.at[:, :, my_cols],
            fin_s.at[l],
            fin_r.at[t],
            l,
            p,
        )

    def forward(l, carry):
        def serve(k):
            if k == 0:

                @pl.when(l + 1 < layers)
                def _():
                    send_carried(l + 1)

            for at in range(layers):

                @pl.when(l == at)
                def _():
                    serve_forth(SERVICES * at + k)

        h = cur[...]
        hsave[l] = h
        get_carried(l)
        hat, _ = normed(h)
        n = hat * parb[l, 0:1, :] + parb[l, 2:3, :]
        here = nsave.at[l]
        here[:, mine, :] = n.astype(BF).reshape(micro, chunk, width)
        ag_start(here)
        serve(0)
        serve(1)
        ag_wait(here)
        n = whole(here).astype(F32)
        prev = before(n, l, 0)
        gap = n - prev
        weights_here(l, A0)
        mats = []
        for i in range(3):
            mix = (prev + gap * rate(l, i)).astype(BF)
            mats.append(
                dot(mix, wA[l, :, :, :, i * quarter : (i + 1) * quarter].reshape(width, quarter))
            )
        k, v, r = mats
        w = -jnp.exp(parb[l, 9:10, my_cols])
        u = parb[l, 10:11, my_cols]
        states = stb[l].astype(F32)
        init = [dot(hot, states[i * seqs : (i + 1) * seqs]) for i in range(3)]
        top = jnp.where(onset > 0.5, jnp.maximum(k, w + init[2]), k)
        for s in reaches:
            top = jnp.maximum(top, jnp.where(place_in >= s, rolled(top, s) + s * w, -1e30))
        top_prev = rolled(top, 1) * stay + init[2]
        al = jnp.exp(w + top_prev - top)
        be = jnp.exp(k - top)
        num = be * v + onset * al * init[0]
        den = be + onset * al * init[1]
        keep = al * stay
        for i, s in enumerate(reaches):
            num = num + keep * rolled(num, s)
            den = den + keep * rolled(den, s)
            if i + 1 < len(reaches):
                keep = keep * rolled(keep, s)
        num_prev = rolled(num, 1) * stay + init[0]
        den_prev = rolled(den, 1) * stay + init[1]
        now = u + k
        peak = jnp.maximum(top_prev, now)
        e1 = jnp.exp(top_prev - peak)
        e2 = jnp.exp(now - peak)
        inv = 1.0 / (e1 * den_prev + e2)
        e1 = e1 * inv
        e2 = e2 * inv
        y = e1 * num_prev + e2 * v
        sr = jax.nn.sigmoid(r)
        g = (sr * y).astype(BF)
        weights_here(l, OO)
        rs_start(dot(g, wO[l].reshape(quarter, width)))
        alsave[l] = al
        besave[l] = be
        for i, value in enumerate((v, y, sr, e1, e2, num_prev, den_prev)):
            smsave[l, i] = value.astype(BF)
        for i, value in enumerate((num, den, top)):
            finb[l, i] = dot(last_hot, value, HIGH)
        finb[l, 3] = dot(last_low, nsave[l, :, :, my_cols].reshape(rows, quarter))
        serve(2)
        serve(3)
        m = h + rs_wait()
        msave[l] = m
        hat, _ = normed(m)
        n2 = hat * parb[l, 1:2, :] + parb[l, 3:4, :]
        here = n2save.at[l]
        here[:, mine, :] = n2.astype(BF).reshape(micro, chunk, width)
        ag_start(here)
        serve(4)
        serve(5)
        ag_wait(here)
        n = whole(here).astype(F32)
        prev = before(n, l, 1)
        gap = n - prev
        mix = (prev + gap * rate(l, 4)).astype(BF)
        r2st[...] = (
            dot(mix, wA[l, :, :, :, 3 * quarter :].reshape(width, quarter))
            .astype(BF)
            .reshape(r2st.shape)
        )

        def a2(r):
            theirs = pl.ds(pl.multiple_of(chunk * next_rank(r), chunk), chunk)
            return peer(
                r2st.at[:, theirs], r2full.at[:, :, my_cols], a2_s.at[r - 1], a2_r.at[r - 1], r
            )

        for r in range(1, RANKS):
            a2(r).start()
        r2full[:, :, my_cols] = r2st[:, mine, :]
        mix = (prev + gap * rate(l, 3)).astype(BF)
        weights_here(l, K0)
        z = dot(mix, wK[l].reshape(width, hidden))
        act = jnp.maximum(z, 0.0)
        weights_here(l, V0)
        rs_start(dot((act * act).astype(BF), wV[l].reshape(hidden, width)))
        zsave[l] = z.astype(BF)
        finb[l, 4] = dot(last_low, n2save[l, :, :, my_cols].reshape(rows, quarter))
        start_any(*fin_args(l))
        serve(6)
        serve(7)
        for r in range(1, RANKS):
            a2(r).wait()
        kv = rs_wait()
        gate = jax.nn.sigmoid(r2full[...].astype(F32).reshape(kv.shape))
        kvsave[l] = kv
        gatesave[l] = gate
        result = (m + gate * kv).astype(BF)
        mixb[...] = result.reshape(mixb.shape)
        cur[...] = result.astype(F32)
        return carry

    lax.fori_loop(0, layers, forward, 0)

    for m in range(5):
        for r in range(1, RANKS):
            w1(m, r).wait_send()
    for l in range(layers):
        for i in PIECES:
            for way in range(2):

                @pl.when(steps_from(l, way) < RANKS - 1)
                def _():
                    forth_copy(l, i, way).wait_send()

        for i in GROUPS:
            ref = group(weights, l, i, c)
            sem = w3_s.at[l, group_of(i)]
            sibling(ref, ref, sem, sem).wait_send()

    start_any(swap_self, mixb, mixed, out_s.at[0], out_r.at[0], t, p)
    sent_any(swap_self, cot, cotb, x_s.at[2], x_r.at[2], t, p)
    got_any(swap_self, cotb, x_r.at[2])
    cur[...] = cotb[...].astype(F32).reshape(cur.shape)
    sg[...] = jnp.zeros_like(sg)

    def free(l, kind):
        for way in range(2):
            pl.semaphore_signal(
                credit.at[l, kind, way],
                inc=1,
                device_id=(on_ring(1 if way == 0 else RANKS - 1), place(t, c)),
                device_id_type=MESH,
            )
        pl.semaphore_signal(
            sib_credit.at[kind], inc=1, device_id=(p, place(t, 1 - c)), device_id_type=MESH
        )

    def add_to(into, ours, theirs):
        into[...] = (ours[...].astype(F32) + theirs[...].astype(F32)).astype(BF)

    def half_copy(l, parity, i):
        g = group_of(i)
        return sibling(
            group(grads, parity, i, 1 - c), group(weights, l, i, c), a_s.at[l, g], a_r.at[l, g]
        )

    def half_sum(l, parity, i):
        half_copy(l, parity, i).wait_recv()
        for j in PIECES:
            if GROUPS[group_of(j)] == i:
                for way in range(2):
                    ours = piece(grads, parity, j, way, c)
                    add_to(ours, ours, piece(weights, l, j, way, 1 - c))

    def back_copy(l, parity, i, way):
        return remote(
            piece(grads, parity, i, way, c),
            piece(weights, l, i, way, c),
            rd_s.at[l, i, way],
            rd_r.at[l, i, way],
            on_ring(RANKS - 1 if way == 0 else 1),
            t,
            c,
        )

    def home_args(i, way):
        ours = piece(weights, p, i, way, c)
        if i in (A0, A1):
            rank = 2 * way + i - A0
            return [
                (
                    t == rank,
                    ours.at[:, pl.ds(m * quarter, quarter)],
                    grad.at[:, my_cols],
                    r1_s.at[m, rank],
                    r1_r.at[m, t],
                    p,
                    rank,
                )
                for m, grad in enumerate((gk, gv, gr, gfr))
            ]
        rank = 2 * way + i - K0
        return [
            (t == rank, ours, gfk.at[:, my_hidden], r1_s.at[4, rank], r1_r.at[4, t], p, rank)
        ]

    def home_own(i, way):
        ours = piece(weights, p, i, way, c)
        size = ours.shape[0]
        if i == OO:
            return pltpu.make_async_copy(ours, go.at[pl.ds(way * size, size)], r1_l.at[4 + way])
        n = 2 * way + i - V0
        return pltpu.make_async_copy(ours, gfv.at[pl.ds(n * size, size)], r1_l.at[n])

    def hand_out(i):
        for way in range(2):
            if i in (V0, V1, OO):
                home_own(i, way).start()
            else:
                for args in home_args(i, way):
                    start_any(*args)

    def first_back(step, pieces, hop):
        return min(
            (slots[hop], n, i) for n, (at, i, slots) in enumerate(BACK) if at == step and i in pieces
        )[2]

    def collect(step, i, hop):
        l, parity = layers - 1 - step, step % 2
        kinds = ((V0, V1, K0, K1), (A0, A1, OO))
        for way in range(2):

            @pl.when(steps_from(l, way) == RANKS - 1 - hop)
            def _():
                for kind, pieces in enumerate(kinds):
                    if i == first_back(step, pieces, hop):
                        pl.semaphore_wait(credit.at[l, kind, way], 1)
                ours = piece(grads, parity, i, way, c)
                theirs = piece(weights, l, i, way, c)
                if hop:
                    back_copy(l, parity, i, way).wait_recv()
                    add_to(theirs if hop == RANKS - 1 else ours, ours, theirs)
                if hop < RANKS - 1:
                    back_copy(l, parity, i, way).start()

        if hop == RANKS - 1 and late(step, i):

            @pl.when(l == p)
            def _():
                hand_out(i)

    def late(step, i):
        return any(
            at == step and j == i and slots[-1] >= SERVICES * layers for at, j, slots in BACK
        )

    def serve_back(time):
        for at in range(layers):
            for i, when in ((V0, RANKS), (K0, RANKS), (A0, SERVICES), (OO, SERVICES)):
                if time == SERVICES * at + when:
                    half_sum(layers - 1 - at, at % 2, i)
        for step, i, hop in due(BACK, time):
            collect(step, i, hop)

    def all_sent(l, parity, pieces):
        for i in pieces:
            for way in range(2):

                @pl.when(steps_from(l, way) != 0)
                def _():
                    back_copy(l, parity, i, way).wait_send()

    def backward(step, carry):
        l = layers - 1 - step
        parity = step % 2

        def serve(k):
            for at in range(layers):

                @pl.when(step == at)
                def _():
                    serve_back(SERVICES * at + k)

        dout = cur[...]
        gate = gatesave[l]
        dkvall[:, mine, :] = (dout * gate).astype(BF).reshape(micro, chunk, width)
        ag_start(dkvall)
        dr2o[...] = (dout * kvsave[l] * gate * (1.0 - gate)).astype(BF).reshape(dr2o.shape)

        def a2(r):
            theirs = pl.ds(pl.multiple_of(quarter * next_rank(r), quarter), quarter)
            return peer(
                dr2o.at[:, :, theirs], dr2c.at[:, mine], a2b_s.at[r - 1], a2b_r.at[r - 1], r
            )

        for r in range(1, RANKS):
            a2(r).start()
        dr2c[:, mine, :] = dr2o[:, :, my_cols]
        n = n2save[l].reshape(rows, width).astype(F32)
        prev = before(n, l, 1)
        gap = n - prev
        act = jnp.maximum(zsave[l].astype(F32), 0.0)
        serve(0)
        serve(1)
        ag_wait(dkvall)
        for r in range(1, RANKS):
            a2(r).wait()
        dkv = whole(dkvall)
        dz = (2.0 * act * dot_nt(dkv, wV[l].reshape(hidden, width))).astype(BF)
        dr2 = whole(dr2c)
        dx = dot_nt(dz, wK[l].reshape(width, hidden))
        dxr = dot_nt(dr2, wA[l, :, :, :, 3 * quarter :].reshape(width, quarter))
        mixed_part = dx * rate(l, 3) + dxr * rate(l, 4)
        shifted = (dx + dxr - mixed_part) * stay
        rs_start(mixed_part + rolled(shifted, rows - 1))
        free(l, 0)
        sg[l, 7:8, :] = column_sum(dx * gap)
        sg[l, 8:9, :] = column_sum(dxr * gap)

        @pl.when(step > 1)
        def _():
            all_sent(l + 2, parity, (V0, V1, K0, K1))

        squared = (act * act).astype(BF)
        size = dV.shape[2] // RANKS
        for b in range(HALVES * RANKS):
            half, q = b // RANKS, b % RANKS
            dV[parity, half, q * size : (q + 1) * size, :] = dot_tn(
                squared[:, b * size : (b + 1) * size], dkv
            ).astype(BF)
        mix = (prev + gap * rate(l, 3)).astype(BF)
        for b in range(HALVES * RANKS):
            dK[parity, b // HALVES, b % HALVES] = dot_tn(
                mix[:, b * block : (b + 1) * block], dz
            ).astype(BF)
        mix_r = (prev + gap * rate(l, 4)).astype(BF)
        pl.semaphore_wait(sib_credit.at[0], 1)
        half_copy(l, parity, V0).start()
        half_copy(l, parity, K0).start()
        serve(2)
        serve(3)

        dn = rs_wait()
        hat, rstd = normed(msave[l])
        sg[l, 1:2, :] = column_sum(dn * hat)
        sg[l, 3:4, :] = column_sum(dn)
        dm = dout + norm_back(dn, parb[l, 1:2, :], hat, rstd)
        dmall[:, mine, :] = dm.astype(BF).reshape(micro, chunk, width)
        ag_start(dmall)
        n = nsave[l].reshape(rows, width).astype(F32)
        prev = before(n, l, 0)
        gap = n - prev
        al = alsave[l]
        be = besave[l]
        v, y, sr, e1, e2, num_prev, den_prev = [smsave[l, i].astype(F32) for i in range(7)]
        w = -jnp.exp(parb[l, 9:10, my_cols])
        serve(4)

        @pl.when(step > 1)
        def _():
            all_sent(l + 2, parity, (A0, A1, OO))

        for b in range(HALVES * RANKS):
            dA[parity, b // HALVES, b % HALVES, :, 3 * quarter :] = dot_tn(
                mix_r[:, b * block : (b + 1) * block], dr2
            ).astype(BF)
        serve(5)
        ag_wait(dmall)
        dmw = whole(dmall)
        dg = dot_nt(dmw, wO[l].reshape(quarter, width))
        dr = (dg * y * sr * (1.0 - sr)).astype(BF)
        dy = dg * sr
        keep = rolled(al * stay, rows - 1)
        into = dy * e1 * stay
        ga = rolled(into, rows - 1)
        gb = -rolled(into * y, rows - 1)
        for i, s in enumerate(reaches):
            ga = ga + keep * rolled(ga, rows - s)
            gb = gb + keep * rolled(gb, rows - s)
            if i + 1 < len(reaches):
                keep = keep * rolled(keep, rows - s)
        near = dy * e2
        now = near * (v - y)
        dv = (be * ga + near).astype(BF)
        dk = (be * (v * ga + gb) + now).astype(BF)
        sg[l, 9:10, my_cols] = w * column_sum(al * (ga * num_prev + gb * den_prev))
        sg[l, 10:11, my_cols] = column_sum(now)
        lefts = (dk, dv, dr)
        total = None
        mixed_part = None
        for i in range(3):
            dx = dot_nt(
                lefts[i], wA[l, :, :, :, i * quarter : (i + 1) * quarter].reshape(width, quarter)
            )
            sg[l, 4 + i : 5 + i, :] = column_sum(dx * gap)
            scaled = dx * rate(l, i)
            total = dx if total is None else total + dx
            mixed_part = scaled if mixed_part is None else mixed_part + scaled
        shifted = (total - mixed_part) * stay
        rs_start(mixed_part + rolled(shifted, rows - 1))
        free(l, 1)

        g = (sr * y).astype(BF)
        size = dO.shape[2]
        for half in range(HALVES):
            dO[parity, half] = dot_tn(g[:, half * size : (half + 1) * size], dmw).astype(BF)
        for i in range(3):
            mix = (prev + gap * rate(l, i)).astype(BF)
            for b in range(HALVES * RANKS):
                dA[parity, b // HALVES, b % HALVES, :, i * quarter : (i + 1) * quarter] = dot_tn(
                    mix[:, b * block : (b + 1) * block], lefts[i]
                ).astype(BF)
        pl.semaphore_wait(sib_credit.at[1], 1)
        half_copy(l, parity, A0).start()
        half_copy(l, parity, OO).start()
        serve(6)
        serve(7)

        dn = rs_wait()
        hat, rstd = normed(hsave[l])
        sg[l, 0:1, :] = column_sum(dn * hat)
        sg[l, 2:3, :] = column_sum(dn)
        dh = dm + norm_back(dn, parb[l, 0:1, :], hat, rstd)
        result = dh.astype(BF)
        gradb[...] = result.reshape(gradb.shape)
        cur[...] = result.astype(F32)
        for i in GROUPS:
            half_copy(l, parity, i).wait_send()
        return carry

    lax.fori_loop(0, layers, backward, 0)

    tg_args = (swap_self, gradb, tgrad, out_s.at[1], out_r.at[1], t, p)
    start_any(*tg_args)

    def sg_copy(r):
        return plane(sg.at[next_pipe(r)], sgr.at[r - 1], sg_s.at[r - 1], sg_r.at[r - 1], r)

    lanes = sg8.shape[-1]

    def sg_cols(rank, half):
        return pl.ds(pl.multiple_of(lanes * (rank * HALVES + half), lanes), lanes)

    def sg8_copy(a, b):
        rank, half = next_rank(a), (c + b) % HALVES
        n = a * HALVES + b
        return remote(
            sgt.at[:, sg_cols(rank, half)], sg8.at[n], sg8_s.at[n], sg8_r.at[n], p, rank, half
        )

    others = [(a, b) for a in range(RANKS) for b in range(HALVES) if a or b]
    for r in range(1, RANKS):
        sg_copy(r).start()
    for l in range(layers):

        @pl.when(l == p)
        def _():
            for i in PIECES:
                if not late(layers - 1 - l, i):
                    hand_out(i)

    end = SERVICES * layers
    for time in range(end, 1 + max(slots[-1] for _, _, slots in BACK)):
        serve_back(time)
        if time == end + 1:
            for r in range(1, RANKS):
                sg_copy(r).wait()
            total = sg[p]
            for r in range(1, RANKS):
                total = total + sgr[r - 1]
            sgt[...] = total
            for a, b in others:
                sg8_copy(a, b).start()
    total = sgt[:, sg_cols(t, c)]
    for a, b in others:
        sg8_copy(a, b).wait()
        total = total + sg8[a * HALVES + b]
    small[...] = total

    for l in range(layers):
        sent_any(*fin_args(l))
    for r in range(1, RANKS):
        par_copy(r).wait_send()
    carried_sent()
    sent_any(swap_self, mixb, mixed, out_s.at[0], out_r.at[0], t, p)
    got_any(swap_self, mixed, out_r.at[0])
    sent_any(*tg_args)
    got_any(swap_self, tgrad, out_r.at[1])
    for l in range(2):
        all_sent(l, (layers - 1 - l) % 2, PIECES)
    for i in PIECES:
        for way in range(2):
            if i in (V0, V1, OO):
                home_own(i, way).wait()
            else:
                for args in home_args(i, way):
                    sent_any(*args)
    for src in range(RANKS):
        cols = pl.ds(src * quarter, quarter)
        got_any(jnp.logical_and(swap_self, t == src), finout.at[:, :, cols], fin_r.at[src])
        for m, grad in enumerate((gk, gv, gr, gfr)):
            got_any(t == src, grad.at[:, cols], r1_r.at[m, src])
        got_any(t == src, gfk.at[:, pl.ds(src * hidden, hidden)], r1_r.at[4, src])


def on_device(
    outer,
    tokens,
    cotangent,
    lengths,
    carried,
    norm_gain,
    norm_bias,
    mix_rates,
    time_decay,
    time_first,
    attention_accept_proj,
    attention_lookup_proj,
    attention_content_proj,
    attention_result_proj,
    feedforward_accept_proj,
    feedforward_lookup_proj,
    feedforward_content_proj,
):
    layers = lax.axis_size("pipe")
    micro, chunk, width = tokens.shape
    row_count = chunk * RANKS
    rows = micro * row_count
    per = lengths.shape[1]
    seqs = micro * per
    weights = [
        attention_lookup_proj[0],
        attention_content_proj[0],
        attention_accept_proj[0],
        feedforward_accept_proj[0],
        attention_result_proj[0],
        feedforward_lookup_proj[0],
        feedforward_content_proj[0],
    ]
    near = [[b * outer + i for i in range(outer)] for b in range(RANKS * HALVES)]
    if outer > 1:
        weights = [
            lax.all_gather(w, "dp", axis=0, tiled=True, axis_index_groups=near) for w in weights
        ]
    block = width // (RANKS * HALVES)
    hidden = weights[5].shape[1] // RANKS
    quarter = width // RANKS
    vmem = pl.BlockSpec(memory_space=pltpu.VMEM)
    smem = pl.BlockSpec(memory_space=pltpu.SMEM)
    hbm = pl.BlockSpec(memory_space=pl.ANY)
    dma = pltpu.SemaphoreType.DMA
    regular = pltpu.SemaphoreType.REGULAR
    n_peers = RANKS - 1
    own = (micro, chunk, width)
    full = (micro, row_count, width)

    def stores(count):
        return [
            pltpu.VMEM((count, RANKS, HALVES, block, width), BF),
            pltpu.VMEM((count, HALVES, block, width), BF),
            pltpu.VMEM((count, RANKS, HALVES, block, hidden), BF),
            pltpu.VMEM((count, HALVES, hidden // HALVES, width), BF),
        ]

    outs = pl.pallas_call(
        partial(layers_kernel, outer, row_count // 2),
        out_shape=(
            jax.ShapeDtypeStruct(own, BF),
            jax.ShapeDtypeStruct(own, BF),
            jax.ShapeDtypeStruct((5, seqs, width), F32),
            jax.ShapeDtypeStruct((16, block), F32),
        )
        + tuple(jax.ShapeDtypeStruct(w.shape, BF) for w in weights),
        in_specs=[vmem] * 2 + [smem] + [vmem] * 6 + [hbm] * 7,
        out_specs=(vmem,) * 4 + (hbm,) * 7,
        scratch_shapes=stores(layers)
        + stores(2)
        + [
            pltpu.VMEM(own, BF),
            pltpu.VMEM(own, BF),
            pltpu.VMEM((16, 128), F32),
            pltpu.VMEM((16, 128), F32),
            pltpu.VMEM((32, width), BF),
            pltpu.VMEM((layers, 32, quarter), BF),
            pltpu.VMEM((16, width), BF),
            pltpu.VMEM((layers, 16, width), BF),
            pltpu.VMEM((16, width), F32),
            pltpu.VMEM((layers, 16, width), F32),
            pltpu.VMEM((layers,) + full, BF),
            pltpu.VMEM((layers,) + full, BF),
            pltpu.VMEM((layers, micro * chunk, width), F32),
            pltpu.VMEM((layers, micro * chunk, width), F32),
            pltpu.VMEM((layers, micro * chunk, width), F32),
            pltpu.VMEM((layers, micro * chunk, width), F32),
            pltpu.VMEM((layers, rows, hidden), BF),
            pltpu.VMEM((layers, rows, quarter), F32),
            pltpu.VMEM((layers, rows, quarter), F32),
            pltpu.VMEM((layers, 7, rows, quarter), BF),
            pltpu.VMEM(full, BF),
            pltpu.VMEM((n_peers,) + own, BF),
            pltpu.VMEM((micro, row_count, quarter), BF),
            pltpu.VMEM(own, BF),
            pltpu.VMEM((micro * chunk, width), F32),
            pltpu.VMEM((layers, 5, seqs, quarter), F32),
            pltpu.VMEM(own, BF),
            pltpu.VMEM(own, BF),
            pltpu.VMEM(full, BF),
            pltpu.VMEM(full, BF),
            pltpu.VMEM(own, BF),
            pltpu.VMEM((micro, row_count, quarter), BF),
            pltpu.VMEM((layers, 16, width), F32),
            pltpu.VMEM((n_peers, 16, width), F32),
            pltpu.VMEM((16, width), F32),
            pltpu.VMEM((RANKS * HALVES, 16, block), F32),
            dma((3,)),
            dma((3,)),
            dma((RANKS,)),
            dma((layers,)),
            dma((RANKS,)),
            dma((layers,)),
            dma((n_peers,)),
            dma((layers,)),
            dma((5, n_peers)),
            dma((5, n_peers)),
            dma((7,)),
            dma((layers, 7, 2)),
            dma((layers, 7, 2)),
            dma((layers, 4)),
            dma((layers, 4)),
            dma((n_peers,)),
            dma((n_peers,)),
            dma((n_peers,)),
            dma((n_peers,)),
            dma((n_peers,)),
            dma((n_peers,)),
            dma((n_peers,)),
            dma((n_peers,)),
            dma((layers,)),
            dma((RANKS,)),
            dma((2,)),
            dma((2,)),
            dma((layers, 4)),
            dma((layers, 4)),
            dma((layers, 7, 2)),
            dma((layers, 7, 2)),
            dma((5, RANKS)),
            dma((5, RANKS)),
            dma((6,)),
            dma((n_peers,)),
            dma((n_peers,)),
            dma((RANKS * HALVES,)),
            dma((RANKS * HALVES,)),
            regular((layers, 2, 2)),
            regular((2,)),
        ],
        compiler_params=pltpu.CompilerParams(
            collective_id=0, has_side_effects=True, vmem_limit_bytes=60 * 2**20
        ),
        name="layers",
    )(
        tokens,
        cotangent,
        lengths,
        carried,
        norm_gain,
        norm_bias,
        mix_rates,
        time_decay,
        time_first,
        *weights,
    )
    mixed, tgrad, fin, small, *grads = outs
    if outer > 1:
        grads = [
            lax.psum_scatter(g, "dp", scatter_dimension=0, tiled=True, axis_index_groups=near)
            for g in grads
        ]
        small = lax.psum_scatter(
            small, "dp", scatter_dimension=1, tiled=True, axis_index_groups=near
        )
    gk, gv, gr, gfr, go, gfk, gfv = [g.astype(F32)[None] for g in grads]
    small = small[None]
    return (
        mixed,
        tgrad.astype(F32),
        fin.transpose(1, 0, 2).reshape(micro, per, 1, 5, width),
        small[:, 0:2],
        small[:, 2:4],
        small[:, 4:9],
        small[:, 9],
        small[:, 10],
        gr,
        gk,
        gv,
        go,
        gfr,
        gfk,
        gfv,
    )


def solution(mesh):
    outer = mesh.shape["dp"] // (RANKS * HALVES)
    placed = (
        P("dp", "pipe", None),
        P("dp", "pipe", None),
        P("dp", None),
        P("dp", None, "pipe", None, None),
        P("pipe", None, None),
        P("pipe", None, None),
        P("pipe", None, None),
        P("pipe", None),
        P("pipe", None),
    ) + (P("pipe", "dp", None),) * 7
    return jax.shard_map(
        partial(on_device, outer),
        mesh=mesh,
        in_specs=placed,
        out_specs=(
            P("dp", "pipe", None),
            P("dp", "pipe", None),
            P("dp", None, "pipe", None, None),
            P("pipe", None, "dp"),
            P("pipe", None, "dp"),
            P("pipe", None, "dp"),
            P("pipe", "dp"),
            P("pipe", "dp"),
        )
        + (P("pipe", "dp", None),) * 7,
        check_vma=False,
    )
```

```python
from functools import partial

import jax
import jax.numpy as jnp
from jax import lax
from jax.sharding import PartitionSpec as P
from jax.experimental import pallas as pl
from jax.experimental.pallas import tpu as pltpu

EPS = 1e-05
BF = jnp.bfloat16
F32 = jnp.float32
HIGH = lax.Precision.HIGHEST
MESH = pl.DeviceIdType.MESH
RANKS = 4
HALVES = 2


def dot(a, b, precision=None):
    return jnp.dot(a, b, precision=precision, preferred_element_type=F32)


def dot_nt(a, b):
    return lax.dot_general(a, b, (((1,), (1,)), ((), ())), preferred_element_type=F32)


def dot_tn(a, b):
    return lax.dot_general(a, b, (((0,), (0,)), ((), ())), preferred_element_type=F32)


def rolled(x, shift):
    return pltpu.roll(x, shift % x.shape[0], 0)


def normed(h):
    center = h - jnp.mean(h, axis=-1, keepdims=True)
    spread = jnp.mean(center * center, axis=-1, keepdims=True)
    rstd = lax.rsqrt(spread + EPS)
    return center * rstd, rstd


def norm_back(dn, gain, hat, rstd):
    dh = dn * gain
    return rstd * (
        dh
        - jnp.mean(dh, axis=-1, keepdims=True)
        - hat * jnp.mean(dh * hat, axis=-1, keepdims=True)
    )


def column_sum(x):
    return jnp.sum(x, axis=0, keepdims=True)


def ring_place(pipe):
    return pipe + (pipe // 2) * (5 - 2 * pipe)


A0, A1, V0, V1, K0, K1, OO = range(7)
FORTH = (
    (0, A0, 0, (-8, -3, -1, 0)),
    (0, A0, 1, (-8, -3, -1, 0)),
    (0, A1, 0, (-6, -2, 0, 1)),
    (0, A1, 1, (-6, -3, 0, 1)),
    (0, V0, 0, (-6, -2, 1, 4)),
    (0, V0, 1, (-9, -6, -3, 1)),
    (0, V1, 0, (-1, 0, 2, 3)),
    (0, V1, 1, (-9, -2, 1, 3)),
    (0, K0, 0, (-5, 0, 3, 5)),
    (0, K0, 1, (-5, 0, 3, 4)),
    (0, K1, 0, (0, 1, 4, 5)),
    (0, K1, 1, (0, 1, 4, 5)),
    (0, OO, 0, (-12, -6, -3, -2)),
    (0, OO, 1, (-12, -4, -3, -2)),
    (1, A0, 0, (-10, -5, -4, 3)),
    (1, A0, 1, (-10, -2, -1, 3)),
    (1, A1, 0, (-6, -2, 2, 7)),
    (1, A1, 1, (-3, 3, 5, 8)),
    (1, V0, 0, (2, 5, 7, 13)),
    (1, V0, 1, (-4, -1, 1, 7)),
    (1, V1, 0, (-8, -5, 2, 9)),
    (1, V1, 1, (-3, 0, 6, 12)),
    (1, K0, 0, (3, 7, 9, 13)),
    (1, K0, 1, (1, 4, 9, 12)),
    (1, K1, 0, (2, 6, 8, 12)),
    (1, K1, 1, (4, 6, 7, 11)),
    (1, OO, 0, (-8, -4, -1, 6)),
    (1, OO, 1, (-9, 3, 5, 8)),
    (2, A0, 0, (-7, 2, 3, 10)),
    (2, A0, 1, (-7, 2, 5, 12)),
    (2, A1, 0, (-1, 8, 13, 16)),
    (2, A1, 1, (1, 6, 10, 15)),
    (2, V0, 0, (-8, 12, 14, 20)),
    (2, V0, 1, (14, 16, 19, 21)),
    (2, V1, 0, (-3, 6, 9, 19)),
    (2, V1, 1, (-10, 5, 7, 12)),
    (2, K0, 0, (-3, 4, 8, 14)),
    (2, K0, 1, (12, 15, 18, 21)),
    (2, K1, 0, (-1, 17, 18, 20)),
    (2, K1, 1, (9, 13, 16, 19)),
    (2, OO, 0, (-10, 3, 8, 16)),
    (2, OO, 1, (-10, 4, 9, 14)),
    (3, A0, 0, (-6, 3, 9, 20)),
    (3, A0, 1, (-6, 3, 9, 20)),
    (3, A1, 0, (12, 14, 20, 23)),
    (3, A1, 1, (10, 13, 21, 24)),
    (3, V0, 0, (9, 12, 18, 20)),
    (3, V0, 1, (-9, -2, 12, 16)),
    (3, V1, 0, (15, 19, 21, 27)),
    (3, V1, 1, (-10, -4, 7, 21)),
    (3, K0, 0, (12, 16, 18, 28)),
    (3, K0, 1, (6, 12, 19, 24)),
    (3, K1, 0, (10, 16, 23, 28)),
    (3, K1, 1, (8, 14, 17, 27)),
    (3, OO, 0, (-9, 1, 11, 16)),
    (3, OO, 1, (-9, 1, 10, 15)),
)
BACK = (
    (0, A0, 0, (8, 10, 17, 20)),
    (0, A0, 1, (8, 9, 11, 18)),
    (0, A1, 0, (10, 13, 19, 20)),
    (0, A1, 1, (12, 16, 17, 20)),
    (0, V0, 0, (4, 7, 9, 15)),
    (0, V0, 1, (6, 8, 10, 17)),
    (0, V1, 0, (9, 12, 15, 18)),
    (0, V1, 1, (4, 6, 8, 13)),
    (0, K0, 0, (7, 8, 13, 17)),
    (0, K0, 1, (5, 7, 9, 17)),
    (0, K1, 0, (5, 7, 10, 13)),
    (0, K1, 1, (10, 11, 13, 17)),
    (0, OO, 0, (8, 11, 17, 19)),
    (0, OO, 1, (8, 10, 12, 17)),
    (1, A0, 0, (17, 20, 24, 28)),
    (1, A0, 1, (21, 22, 25, 28)),
    (1, A1, 0, (18, 19, 25, 28)),
    (1, A1, 1, (16, 19, 22, 26)),
    (1, V0, 0, (12, 13, 15, 19)),
    (1, V0, 1, (13, 15, 18, 21)),
    (1, V1, 0, (14, 15, 17, 24)),
    (1, V1, 1, (13, 16, 19, 26)),
    (1, K0, 0, (13, 14, 16, 26)),
    (1, K0, 1, (17, 20, 23, 26)),
    (1, K1, 0, (15, 16, 18, 24)),
    (1, K1, 1, (12, 14, 17, 19)),
    (1, OO, 0, (21, 22, 24, 27)),
    (1, OO, 1, (16, 21, 24, 27)),
    (2, A0, 0, (38, 39, 40, 41)),
    (2, A0, 1, (26, 30, 33, 35)),
    (2, A1, 0, (25, 32, 33, 38)),
    (2, A1, 1, (27, 32, 34, 37)),
    (2, V0, 0, (20, 23, 26, 35)),
    (2, V0, 1, (21, 25, 27, 37)),
    (2, V1, 0, (20, 24, 26, 37)),
    (2, V1, 1, (35, 38, 39, 41)),
    (2, K0, 0, (34, 39, 40, 41)),
    (2, K0, 1, (20, 23, 28, 33)),
    (2, K1, 0, (22, 26, 28, 39)),
    (2, K1, 1, (25, 29, 31, 37)),
    (2, OO, 0, (31, 33, 38, 39)),
    (2, OO, 1, (32, 34, 38, 39)),
    (3, A0, 0, (38, 39, 40, 41)),
    (3, A0, 1, (34, 37, 38, 40)),
    (3, A1, 0, (32, 36, 37, 39)),
    (3, A1, 1, (34, 38, 39, 40)),
    (3, V0, 0, (32, 37, 38, 40)),
    (3, V0, 1, (33, 37, 38, 40)),
    (3, V1, 0, (29, 32, 35, 40)),
    (3, V1, 1, (34, 38, 39, 41)),
    (3, K0, 0, (32, 37, 38, 39)),
    (3, K0, 1, (29, 32, 34, 37)),
    (3, K1, 0, (28, 30, 32, 33)),
    (3, K1, 1, (28, 31, 32, 35)),
    (3, OO, 0, (36, 38, 39, 41)),
    (3, OO, 1, (34, 38, 39, 41)),
)
PIECES = range(7)
SERVICES = 8
ROWS_FROM = {(A0, 0): 0, (A1, 0): 1, (A0, 1): 3, (A1, 1): 2, (K0, 0): 0, (K1, 0): 1, (K0, 1): 3, (K1, 1): 2}
GROUPS = (A0, V0, K0, OO)


def layers_kernel(
    outer,
    longest,
    tok,
    cot,
    lens,
    held,
    gain,
    bias,
    mixes,
    decay,
    first,
    wk,
    wv,
    wr,
    wfr,
    wo,
    wfk,
    wfv,
    mixed,
    tgrad,
    finout,
    small,
    gk,
    gv,
    gr,
    gfr,
    go,
    gfk,
    gfv,
    wA,
    wO,
    wK,
    wV,
    dA,
    dO,
    dK,
    dV,
    tokb,
    cotb,
    info,
    infob,
    stsrc,
    stb,
    shsrc,
    shb,
    par,
    parb,
    nsave,
    n2save,
    hsave,
    msave,
    kvsave,
    gatesave,
    zsave,
    alsave,
    besave,
    smsave,
    part,
    rbuf,
    r2st,
    r2full,
    cur,
    finb,
    mixb,
    gradb,
    dkvall,
    dmall,
    dr2o,
    dr2c,
    mixk,
    mixr,
    squares,
    dzs,
    mixes3,
    lefts,
    gated,
    sg,
    sgr,
    sgt,
    sg8,
    x_s,
    x_r,
    st_s,
    st_r,
    sh_s,
    sh_r,
    par_s,
    par_r,
    w1_s,
    w1_r,
    w1_l,
    rw_s,
    rw_r,
    w3_s,
    w3_r,
    ag_s,
    ag_r,
    rs_s,
    rs_r,
    a2_s,
    a2_r,
    a2b_s,
    a2b_r,
    fin_s,
    fin_r,
    out_s,
    out_r,
    a_s,
    a_r,
    rd_s,
    rd_r,
    r1_s,
    r1_r,
    r1_l,
    sg_s,
    sg_r,
    sg8_s,
    sg8_r,
    credit,
    sib_credit,
):
    p = lax.axis_index("pipe")
    d = lax.axis_index("dp")
    t = d // (HALVES * outer)
    c = (d // outer) % HALVES
    o = d % outer
    ring = ring_place(p)
    micro, chunk, width = tok.shape
    layers = stb.shape[0]
    rows = micro * chunk * RANKS
    quarter = width // RANKS
    mine = pl.ds(pl.multiple_of(chunk * t, chunk), chunk)
    my_cols = pl.ds(pl.multiple_of(quarter * t, quarter), quarter)
    hidden = wfk.shape[1] // RANKS
    my_hidden = pl.ds(pl.multiple_of(hidden * t, hidden), hidden)
    block = wk.shape[0]
    seqs = held.shape[0] * held.shape[1]
    per = held.shape[1]

    def place(rank, half):
        return (rank * HALVES + half) * outer + o

    def next_rank(r):
        return (t + r) % RANKS

    def next_pipe(r):
        return (p + r) % RANKS

    def on_ring(r):
        return ring_place((ring + r) % RANKS)

    def remote(src, dst, ss, rs, pipe, rank, half):
        return pltpu.make_async_remote_copy(
            src_ref=src,
            dst_ref=dst,
            send_sem=ss,
            recv_sem=rs,
            device_id=(pipe, place(rank, half)),
            device_id_type=MESH,
        )

    def peer(src, dst, ss, rs, r):
        return remote(src, dst, ss, rs, p, next_rank(r), c)

    def plane(src, dst, ss, rs, r):
        return remote(src, dst, ss, rs, next_pipe(r), t, c)

    def sibling(src, dst, ss, rs):
        return remote(src, dst, ss, rs, p, t, 1 - c)

    def start_any(is_self, src, dst, ss, rs, pipe, rank):
        @pl.when(is_self)
        def _():
            pltpu.make_async_copy(src, dst, ss).start()

        @pl.when(jnp.logical_not(is_self))
        def _():
            remote(src, dst, ss, rs, pipe, rank, c).start()

    def sent_any(is_self, src, dst, ss, rs, pipe, rank):
        @pl.when(is_self)
        def _():
            pltpu.make_async_copy(src, dst, ss).wait()

        @pl.when(jnp.logical_not(is_self))
        def _():
            remote(src, dst, ss, rs, pipe, rank, c).wait_send()

    def got(dst, rs):
        remote(dst, dst, rs, rs, next_pipe(1), t, c).wait_recv()

    def got_any(is_self, dst, rs):
        @pl.when(jnp.logical_not(is_self))
        def _():
            got(dst, rs)

    barrier = pltpu.get_barrier_semaphore()
    for a in range(RANKS):
        for b in range(RANKS):
            if a or b:
                pl.semaphore_signal(
                    barrier,
                    inc=1,
                    device_id=(next_pipe(a), place(next_rank(b), c)),
                    device_id_type=MESH,
                )
    for b in range(RANKS):
        pl.semaphore_signal(
            barrier, inc=1, device_id=(p, place(next_rank(b), 1 - c)), device_id_type=MESH
        )
    pl.semaphore_wait(barrier, RANKS * RANKS - 1 + RANKS)

    raw = (wk, wv, wr, wfr)

    def w1(m, r):
        rank = next_rank(r)
        if m < 4:
            cols = pl.ds(pl.multiple_of(quarter * rank, quarter), quarter)
            return peer(
                raw[m].at[:, cols],
                wA.at[p, t, c, :, pl.ds(m * quarter, quarter)],
                w1_s.at[m, r - 1],
                w1_r.at[m, r - 1],
                r,
            )
        cols = pl.ds(pl.multiple_of(hidden * rank, hidden), hidden)
        return peer(wfk.at[:, cols], wK.at[p, t, c], w1_s.at[m, r - 1], w1_r.at[m, r - 1], r)

    def w1_own(m):
        if m < 4:
            return pltpu.make_async_copy(
                raw[m].at[:, my_cols], wA.at[p, t, c, :, pl.ds(m * quarter, quarter)], w1_l.at[m]
            )
        if m == 4:
            return pltpu.make_async_copy(wfk.at[:, my_hidden], wK.at[p, t, c], w1_l.at[m])
        if m == 5:
            return pltpu.make_async_copy(wo, wO.at[p, c], w1_l.at[m])
        return pltpu.make_async_copy(wfv, wV.at[p, c], w1_l.at[m])

    for m in range(7):
        w1_own(m).start()
    for group_m in ((0, 1, 2, 3), (4,)):
        for r in (1, 3, 2):
            for m in group_m:
                w1(m, r).start()

    lane = lax.broadcasted_iota(jnp.int32, info.shape, 1)
    line = lax.broadcasted_iota(jnp.int32, info.shape, 0)
    marks = jnp.full(info.shape, -1, jnp.int32)
    for b in range(micro):
        at = b * (rows // micro)
        for s in range(per):
            index = b * per + s
            marks = jnp.where(jnp.logical_and(line == 0, lane == index), at, marks)
            at = at + lens[b, s]
            marks = jnp.where(line == 8 + index, at - 1, marks)
    info[...] = marks.astype(F32)

    swap_self = p == t
    swaps = [(tok, tokb), (info, infob), (cot, cotb)]
    for i, (src, dst) in enumerate(swaps):
        start_any(swap_self, src, dst, x_s.at[i], x_r.at[i], t, p)

    par[0:2, :] = gain[0]
    par[2:4, :] = bias[0]
    par[4:9, :] = mixes[0]
    par[9:10, :] = decay[...]
    par[10:11, :] = first[...]
    par[11:16, :] = jnp.zeros((5, width), F32)

    def par_copy(r):
        return plane(par, parb.at[p], par_s.at[r - 1], par_r.at[p], r)

    for r in range(1, RANKS):
        par_copy(r).start()
    parb[p] = par[...]

    carried_rows = held[:, :, 0].reshape(seqs, 5, width)
    spare = jnp.zeros((8, width), F32)
    stsrc[...] = jnp.concatenate([carried_rows[:, i] for i in range(3)] + [spare], axis=0).astype(BF)
    shsrc[...] = jnp.concatenate([carried_rows[:, 3], carried_rows[:, 4]], axis=0).astype(BF)

    def state_args(rank):
        return (
            jnp.logical_and(swap_self, rank == t),
            stsrc.at[:, pl.ds(quarter * rank, quarter)],
            stb.at[p],
            st_s.at[rank],
            st_r.at[p],
            t,
            rank,
        )

    def shift_args(rank):
        return (
            jnp.logical_and(swap_self, rank == t),
            shsrc,
            shb.at[p],
            sh_s.at[rank],
            sh_r.at[p],
            t,
            rank,
        )

    def send_carried(l):
        @pl.when(p == l)
        def _():
            for rank in range(RANKS):
                start_any(*shift_args(rank))
                start_any(*state_args(rank))

    def get_carried(l):
        from_self = jnp.logical_and(swap_self, p == l)

        @pl.when(from_self)
        def _():
            for rank in range(RANKS):

                @pl.when(rank == t)
                def _():
                    pltpu.make_async_copy(*shift_args(rank)[1:4]).wait()
                    pltpu.make_async_copy(*state_args(rank)[1:4]).wait()

        got_any(from_self, shb.at[l], sh_r.at[l])
        got_any(from_self, stb.at[l], st_r.at[l])
        got_any(p == l, parb.at[l], par_r.at[l])

    def carried_sent():
        for rank in range(RANKS):

            @pl.when(jnp.logical_not(jnp.logical_and(swap_self, rank == t)))
            def _():
                remote(*shift_args(rank)[1:], c).wait_send()
                remote(*state_args(rank)[1:], c).wait_send()

    def piece(store, at, i, way, half):
        a, small_one, k, v = store
        if i in (A0, A1, K0, K1):
            return (a if i in (A0, A1) else k).at[at, next_rank(ROWS_FROM[i, way]), half]
        size = (small_one if i == OO else v).shape[2] // 2
        if i == OO:
            return small_one.at[at, half, pl.ds(way * size, size)]
        return v.at[at, half, pl.ds(way * size + (i - V0) * (size // 2), size // 2)]

    def group(store, at, i, half):
        a, small_one, k, v = store
        if i == A0:
            return a.at[at, :, half]
        if i == K0:
            return k.at[at, :, half]
        return small_one.at[at, half] if i == OO else v.at[at, half]

    def group_of(i):
        return GROUPS.index({A1: A0, V1: V0, K1: K0}.get(i, i))

    weights = (wA, wO, wK, wV)
    grads = (dA, dO, dK, dV)

    def steps_from(l, way):
        home = ring_place(l)
        return (ring - home + RANKS) % RANKS if way == 0 else (home - ring + RANKS) % RANKS

    def forth_copy(l, i, way):
        return remote(
            piece(weights, l, i, way, c),
            piece(weights, l, i, way, c),
            rw_s.at[l, i, way],
            rw_r.at[l, i, way],
            on_ring(1 if way == 0 else RANKS - 1),
            t,
            c,
        )

    def pair_copy(l, i, way):
        g = group_of(i)
        return sibling(
            piece(weights, l, i, way, c),
            piece(weights, l, i, way, c),
            w3_s.at[l, g],
            w3_r.at[l, g],
        )

    def bring(l, i, way, hop):
        @pl.when(steps_from(l, way) == hop)
        def _():
            if hop:
                forth_copy(l, i, way).wait_recv()
            else:
                rows_in(i, way)
            if hop < RANKS - 1:
                forth_copy(l, i, way).start()
            pair_copy(l, i, way).start()

    def rows_in(i, way):
        if i == OO:
            return None
        if i in (V0, V1):
            return None
        for m in range(4) if i in (A0, A1) else (4,):
            if ROWS_FROM[i, way]:
                w1(m, RANKS - ROWS_FROM[i, way]).wait_recv()
            else:
                w1_own(m).wait()

    def due(plan, time):
        for l, i, way, slots in plan:
            for hop, slot in enumerate(slots):
                if slot == time:
                    yield l, i, way, hop

    def serve_forth(time):
        for l, i, way, hop in due(FORTH, time):
            bring(l, i, way, hop)

    def weights_here(l, i):
        ref = group(weights, l, i, 1 - c)
        sem = w3_r.at[l, group_of(i)]
        sibling(ref, ref, sem, sem).wait_recv()

    send_carried(0)
    w1_own(5).wait()
    w1_own(6).wait()
    for time in range(min(slots[0] for _, _, _, slots in FORTH), 0):
        serve_forth(time)

    for i in range(2):
        src, dst = swaps[i]
        sent_any(swap_self, src, dst, x_s.at[i], x_r.at[i], t, p)
        got_any(swap_self, dst, x_r.at[i])

    streams = range(micro)
    span = rows // micro

    def ag(buf, r, b):
        return peer(buf.at[b, mine], buf.at[b, mine], ag_s.at[b, r - 1], ag_r.at[b, r - 1], r)

    def ag_start(buf, b):
        for r in range(1, RANKS):
            ag(buf, r, b).start()

    def ag_wait(buf, b):
        for r in range(1, RANKS):
            ag(buf, r, b).wait()

    def rs(r, b):
        theirs = pl.ds(pl.multiple_of(chunk * next_rank(r), chunk), chunk)
        return peer(
            part.at[b, theirs], rbuf.at[b, r - 1], rs_s.at[b, r - 1], rs_r.at[b, r - 1], r
        )

    def rs_start(values, b):
        part[b] = values.astype(BF)
        for r in range(1, RANKS):
            rs(r, b).start()

    def rs_wait(b):
        for r in range(1, RANKS):
            rs(r, b).wait()
        total = part[b, mine, :].astype(F32)
        for r in range(1, RANKS):
            total = total + rbuf[b, r - 1].astype(F32)
        return total

    cur[...] = tokb[...].astype(F32)

    starts = infob[0:1, 0:seqs]
    ends = infob[8 : 8 + seqs, 0:span]
    line = lax.broadcasted_iota(jnp.int32, (span, seqs), 0).astype(F32)
    lane = lax.broadcasted_iota(jnp.int32, (seqs, span), 1).astype(F32)
    none = jnp.zeros((span, seqs), F32)
    hot, onset, stay, hots, place_in, last_hot = [], [], [], [], [], []
    for b in streams:
        at = line + b * span
        hot.append((at == starts).astype(F32))
        onset.append(jnp.sum(hot[b], axis=1, keepdims=True))
        stay.append(1.0 - onset[b])
        hots.append(
            [jnp.concatenate(pair, axis=1).astype(BF) for pair in ((hot[b], none), (none, hot[b]))]
        )
        begun = jnp.max(jnp.where(starts <= at, starts, 0.0), axis=1, keepdims=True)
        place_in.append(at[:, 0:1] - begun)
        last_hot.append((lane + b * span == ends).astype(F32))
    reaches = []
    reach = 1
    while reach < longest:
        reaches.append(reach)
        reach *= 2

    def whole(ref):
        return ref[...].reshape(rows, ref.shape[-1])

    def before(n, l, which, b):
        return rolled(n, 1) * stay[b] + dot(hots[b][which], shb[l])

    def rate(l, i):
        return parb[l, 4 + i : 5 + i, :]

    def fin_args(l):
        return (
            jnp.logical_and(l == p, swap_self),
            finb.at[l],
            finout.at[:, :, my_cols],
            fin_s.at[l],
            fin_r.at[t],
            l,
            p,
        )

    def forward(l, carry):
        def serve(k):
            if k == 0:

                @pl.when(l + 1 < layers)
                def _():
                    send_carried(l + 1)

            for at in range(layers):

                @pl.when(l == at)
                def _():
                    serve_forth(SERVICES * at + k)

        get_carried(l)
        for b in streams:
            h = cur[b]
            hsave[l, b] = h
            hat, _ = normed(h)
            n = hat * parb[l, 0:1, :] + parb[l, 2:3, :]
            nsave[l, b, mine, :] = n.astype(BF)
            ag_start(nsave.at[l], b)
        serve(0)
        serve(1)
        w = -jnp.exp(parb[l, 9:10, my_cols])
        u = parb[l, 10:11, my_cols]
        states = stb[l].astype(F32)
        for b in streams:
            ag_wait(nsave.at[l], b)
            n = nsave[l, b].astype(F32)
            prev = before(n, l, 0, b)
            gap = n - prev
            if b == 0:
                weights_here(l, A0)
            mats = []
            for i in range(3):
                mix = (prev + gap * rate(l, i)).astype(BF)
                mats.append(
                    dot(
                        mix, wA[l, :, :, :, i * quarter : (i + 1) * quarter].reshape(width, quarter)
                    )
                )
            k, v, r = mats
            init = [dot(hot[b], states[i * seqs : (i + 1) * seqs]) for i in range(3)]
            top = jnp.where(onset[b] > 0.5, jnp.maximum(k, w + init[2]), k)
            for s in reaches:
                top = jnp.maximum(top, jnp.where(place_in[b] >= s, rolled(top, s) + s * w, -1e30))
            top_prev = rolled(top, 1) * stay[b] + init[2]
            al = jnp.exp(w + top_prev - top)
            be = jnp.exp(k - top)
            num = be * v + onset[b] * al * init[0]
            den = be + onset[b] * al * init[1]
            keep = al * stay[b]
            for i, s in enumerate(reaches):
                num = num + keep * rolled(num, s)
                den = den + keep * rolled(den, s)
                if i + 1 < len(reaches):
                    keep = keep * rolled(keep, s)
            num_prev = rolled(num, 1) * stay[b] + init[0]
            den_prev = rolled(den, 1) * stay[b] + init[1]
            now = u + k
            peak = jnp.maximum(top_prev, now)
            e1 = jnp.exp(top_prev - peak)
            e2 = jnp.exp(now - peak)
            inv = 1.0 / (e1 * den_prev + e2)
            e1 = e1 * inv
            e2 = e2 * inv
            y = e1 * num_prev + e2 * v
            sr = jax.nn.sigmoid(r)
            g = (sr * y).astype(BF)
            if b == 0:
                weights_here(l, OO)
            rs_start(dot(g, wO[l].reshape(quarter, width)), b)
            alsave[l, b] = al
            besave[l, b] = be
            for i, value in enumerate((v, y, sr, e1, e2, num_prev, den_prev)):
                smsave[l, i, b] = value.astype(BF)
            lasts = [dot(last_hot[b], value, HIGH) for value in (num, den, top)]
            lasts.append(dot(last_hot[b].astype(BF), nsave[l, b, :, my_cols]))
            ending = [x + y for x, y in zip(ending, lasts)] if b else lasts
            serve(2 + b)
        for b in streams:
            m = hsave[l, b] + rs_wait(b)
            msave[l, b] = m
            hat, _ = normed(m)
            n2 = hat * parb[l, 1:2, :] + parb[l, 3:4, :]
            n2save[l, b, mine, :] = n2.astype(BF)
            ag_start(n2save.at[l], b)
        serve(4)
        serve(5)

        def a2(r, b):
            theirs = pl.ds(pl.multiple_of(chunk * next_rank(r), chunk), chunk)
            return peer(
                r2st.at[b, theirs],
                r2full.at[b, :, my_cols],
                a2_s.at[b, r - 1],
                a2_r.at[b, r - 1],
                r,
            )

        for b in streams:
            ag_wait(n2save.at[l], b)
            n = n2save[l, b].astype(F32)
            prev = before(n, l, 1, b)
            gap = n - prev
            mix = (prev + gap * rate(l, 4)).astype(BF)
            r2st[b] = dot(mix, wA[l, :, :, :, 3 * quarter :].reshape(width, quarter)).astype(BF)
            for r in range(1, RANKS):
                a2(r, b).start()
            r2full[b, :, my_cols] = r2st[b, mine, :]
            mix = (prev + gap * rate(l, 3)).astype(BF)
            if b == 0:
                weights_here(l, K0)
            z = dot(mix, wK[l].reshape(width, hidden))
            act = jnp.maximum(z, 0.0)
            if b == 0:
                weights_here(l, V0)
            rs_start(dot((act * act).astype(BF), wV[l].reshape(hidden, width)), b)
            zsave[l, b] = z.astype(BF)
            value = dot(last_hot[b].astype(BF), n2save[l, b, :, my_cols])
            last_n2 = last_n2 + value if b else value
            serve(6 + b)
        for i, value in enumerate(ending + [last_n2]):
            finb[l, i] = value
        start_any(*fin_args(l))
        for b in streams:
            for r in range(1, RANKS):
                a2(r, b).wait()
            kv = rs_wait(b)
            gate = jax.nn.sigmoid(r2full[b].astype(F32))
            kvsave[l, b] = kv
            gatesave[l, b] = gate
            result = (msave[l, b] + gate * kv).astype(BF)
            mixb[b] = result
            cur[b] = result.astype(F32)
        return carry

    lax.fori_loop(0, layers, forward, 0)

    for m in range(5):
        for r in range(1, RANKS):
            w1(m, r).wait_send()
    for l in range(layers):
        for i in PIECES:
            for way in range(2):

                @pl.when(steps_from(l, way) < RANKS - 1)
                def _():
                    forth_copy(l, i, way).wait_send()

        for i in GROUPS:
            ref = group(weights, l, i, c)
            sem = w3_s.at[l, group_of(i)]
            sibling(ref, ref, sem, sem).wait_send()

    start_any(swap_self, mixb, mixed, out_s.at[0], out_r.at[0], t, p)
    sent_any(swap_self, cot, cotb, x_s.at[2], x_r.at[2], t, p)
    got_any(swap_self, cotb, x_r.at[2])
    cur[...] = cotb[...].astype(F32)
    sg[...] = jnp.zeros_like(sg)

    def free(l, kind):
        for way in range(2):
            pl.semaphore_signal(
                credit.at[l, kind, way],
                inc=1,
                device_id=(on_ring(1 if way == 0 else RANKS - 1), place(t, c)),
                device_id_type=MESH,
            )
        pl.semaphore_signal(
            sib_credit.at[kind], inc=1, device_id=(p, place(t, 1 - c)), device_id_type=MESH
        )

    def add_to(into, ours, theirs):
        def some(n, carry):
            part_rows = pl.ds(pl.multiple_of(n * 32, 32), 32)
            into[part_rows, :] = (
                ours[part_rows, :].astype(F32) + theirs[part_rows, :].astype(F32)
            ).astype(BF)
            return carry

        lax.fori_loop(0, ours.shape[0] // 32, some, 0)

    def half_copy(l, parity, i):
        g = group_of(i)
        return sibling(
            group(grads, parity, i, 1 - c), group(weights, l, i, c), a_s.at[l, g], a_r.at[l, g]
        )

    def half_sum(l, parity, i):
        half_copy(l, parity, i).wait_recv()
        for j in PIECES:
            if GROUPS[group_of(j)] == i:
                for way in range(2):
                    ours = piece(grads, parity, j, way, c)
                    add_to(ours, ours, piece(weights, l, j, way, 1 - c))

    def back_copy(l, parity, i, way):
        return remote(
            piece(grads, parity, i, way, c),
            piece(weights, l, i, way, c),
            rd_s.at[l, i, way],
            rd_r.at[l, i, way],
            on_ring(RANKS - 1 if way == 0 else 1),
            t,
            c,
        )

    def home_args(i, way):
        ours = piece(weights, p, i, way, c)
        r = ROWS_FROM[i, way]
        if i in (A0, A1):
            return [
                (ours.at[:, pl.ds(m * quarter, quarter)], grad.at[:, my_cols], m, r)
                for m, grad in enumerate((gk, gv, gr, gfr))
            ]
        return [(ours, gfk.at[:, my_hidden], 4, r)]

    def home_copy(src, dst, m, r):
        if r:
            return peer(src, dst, r1_s.at[m, r], r1_r.at[m, r], r)
        return pltpu.make_async_copy(src, dst, r1_s.at[m, 0])

    def home_own(i, way):
        ours = piece(weights, p, i, way, c)
        size = ours.shape[0]
        if i == OO:
            return pltpu.make_async_copy(ours, go.at[pl.ds(way * size, size)], r1_l.at[4 + way])
        n = 2 * way + i - V0
        return pltpu.make_async_copy(ours, gfv.at[pl.ds(n * size, size)], r1_l.at[n])

    def hand_out(i, way):
        if i in (V0, V1, OO):
            home_own(i, way).start()
        else:
            for args in home_args(i, way):
                home_copy(*args).start()

    kinds = ((V0, V1, K0, K1), (A0, A1, OO))

    def opens(step, i, way, hop):
        kind = kinds[0] if i in kinds[0] else kinds[1]
        return i == min(
            (slots[hop], n, j)
            for n, (at, j, to, slots) in enumerate(BACK)
            if at == step and to == way and j in kind
        )[2]

    def collect(step, i, way, hop):
        l, parity = layers - 1 - step, step % 2

        @pl.when(steps_from(l, way) == RANKS - 1 - hop)
        def _():
            if opens(step, i, way, hop):
                pl.semaphore_wait(credit.at[l, int(i in kinds[1]), way], 1)
            ours = piece(grads, parity, i, way, c)
            theirs = piece(weights, l, i, way, c)
            if hop:
                back_copy(l, parity, i, way).wait_recv()
                add_to(theirs if hop == RANKS - 1 else ours, ours, theirs)
            if hop < RANKS - 1:
                back_copy(l, parity, i, way).start()
            elif late(step, i, way):
                hand_out(i, way)

    def late(step, i, way):
        return any(
            (at, j, to) == (step, i, way) and slots[-1] >= SERVICES * layers
            for at, j, to, slots in BACK
        )

    def serve_back(time):
        for at in range(layers):
            for i, when in ((V0, RANKS), (K0, RANKS), (A0, SERVICES), (OO, SERVICES)):
                if time == SERVICES * at + when:
                    half_sum(layers - 1 - at, at % 2, i)
        for step, i, way, hop in due(BACK, time):
            collect(step, i, way, hop)

    def all_sent(l, parity, pieces):
        for i in pieces:
            for way in range(2):

                @pl.when(steps_from(l, way) != 0)
                def _():
                    back_copy(l, parity, i, way).wait_send()

    def each_block(left_ref, right_ref, store, count=HALVES * RANKS):
        def body(n, carry):
            cols = pl.ds(pl.multiple_of(n * block, block), block)
            left = left_ref[:, :, cols].reshape(rows, block)
            store(n, dot_tn(left, whole(right_ref)).astype(BF))
            return carry

        lax.fori_loop(0, count, body, 0, unroll=2)

    def backward(step, carry):
        l = layers - 1 - step
        parity = step % 2

        def serve(k):
            for at in range(layers):

                @pl.when(step == at)
                def _():
                    serve_back(SERVICES * at + k)

        def a2(r, b):
            theirs = pl.ds(pl.multiple_of(quarter * next_rank(r), quarter), quarter)
            return peer(
                dr2o.at[b, :, theirs], dr2c.at[b, mine], a2b_s.at[b, r - 1], a2b_r.at[b, r - 1], r
            )

        sums = {}

        def add_small(i, value):
            sums[i] = sums[i] + value if i in sums else value

        for b in streams:
            dout = cur[b]
            gate = gatesave[l, b]
            dkvall[b, mine, :] = (dout * gate).astype(BF)
            ag_start(dkvall, b)
            dr2o[b] = (dout * kvsave[l, b] * gate * (1.0 - gate)).astype(BF)
            for r in range(1, RANKS):
                a2(r, b).start()
            dr2c[b, mine, :] = dr2o[b, :, my_cols]
        serve(0)
        for b in streams:
            n = n2save[l, b].astype(F32)
            prev = before(n, l, 1, b)
            gap = n - prev
            mixk[b] = (prev + gap * rate(l, 3)).astype(BF)
            mixr[b] = (prev + gap * rate(l, 4)).astype(BF)
            act = jnp.maximum(zsave[l, b].astype(F32), 0.0)
            squares[b] = (act * act).astype(BF)
            ag_wait(dkvall, b)
            for r in range(1, RANKS):
                a2(r, b).wait()
            dz = (2.0 * act * dot_nt(dkvall[b], wV[l].reshape(hidden, width))).astype(BF)
            dzs[b] = dz
            dx = dot_nt(dz, wK[l].reshape(width, hidden))
            dxr = dot_nt(dr2c[b], wA[l, :, :, :, 3 * quarter :].reshape(width, quarter))
            mixed_part = dx * rate(l, 3) + dxr * rate(l, 4)
            shifted = (dx + dxr - mixed_part) * stay[b]
            rs_start(mixed_part + rolled(shifted, span - 1), b)
            add_small(7, column_sum(dx * gap))
            add_small(8, column_sum(dxr * gap))
            serve(1 + b)
        free(l, 0)

        @pl.when(step > 1)
        def _():
            all_sent(l + 2, parity, (V0, V1, K0, K1))

        each_block(
            squares,
            dkvall,
            lambda n, value: dV.__setitem__(
                (parity, n // RANKS, pl.ds(pl.multiple_of((n % RANKS) * block, block), block)), value
            ),
        )
        each_block(
            mixk,
            dzs,
            lambda n, value: dK.__setitem__((parity, n // HALVES, n % HALVES), value),
        )
        pl.semaphore_wait(sib_credit.at[0], 1)
        half_copy(l, parity, V0).start()
        half_copy(l, parity, K0).start()
        serve(3)
        for b in streams:
            dn = rs_wait(b)
            hat, rstd = normed(msave[l, b])
            add_small(1, column_sum(dn * hat))
            add_small(3, column_sum(dn))
            dm = cur[b] + norm_back(dn, parb[l, 1:2, :], hat, rstd)
            cur[b] = dm
            dmall[b, mine, :] = dm.astype(BF)
            ag_start(dmall, b)
        serve(4)

        @pl.when(step > 1)
        def _():
            all_sent(l + 2, parity, (A0, A1, OO))

        def to_dA(m):
            def store(n, value):
                dA[parity, n // HALVES, n % HALVES, :, m * quarter : (m + 1) * quarter] = value

            return store

        each_block(mixr, dr2c, to_dA(3))
        w = -jnp.exp(parb[l, 9:10, my_cols])
        for b in streams:
            n = nsave[l, b].astype(F32)
            prev = before(n, l, 0, b)
            gap = n - prev
            for i in range(3):
                mixes3[i, b] = (prev + gap * rate(l, i)).astype(BF)
            al = alsave[l, b]
            be = besave[l, b]
            v, y, sr, e1, e2, num_prev, den_prev = [smsave[l, i, b].astype(F32) for i in range(7)]
            gated[b] = (sr * y).astype(BF)
            ag_wait(dmall, b)
            dg = dot_nt(dmall[b], wO[l].reshape(quarter, width))
            dr = (dg * y * sr * (1.0 - sr)).astype(BF)
            dy = dg * sr
            keep = rolled(al * stay[b], span - 1)
            into = dy * e1 * stay[b]
            ga = rolled(into, span - 1)
            gb = -rolled(into * y, span - 1)
            for i, s in enumerate(reaches):
                ga = ga + keep * rolled(ga, span - s)
                gb = gb + keep * rolled(gb, span - s)
                if i + 1 < len(reaches):
                    keep = keep * rolled(keep, span - s)
            near = dy * e2
            now = near * (v - y)
            dv = (be * ga + near).astype(BF)
            dk = (be * (v * ga + gb) + now).astype(BF)
            add_small(9, w * column_sum(al * (ga * num_prev + gb * den_prev)))
            add_small(10, column_sum(now))
            total = None
            mixed_part = None
            for i, left in enumerate((dk, dv, dr)):
                lefts[i, b] = left
                dx = dot_nt(
                    left, wA[l, :, :, :, i * quarter : (i + 1) * quarter].reshape(width, quarter)
                )
                add_small(4 + i, column_sum(dx * gap))
                scaled = dx * rate(l, i)
                total = dx if total is None else total + dx
                mixed_part = scaled if mixed_part is None else mixed_part + scaled
            shifted = (total - mixed_part) * stay[b]
            rs_start(mixed_part + rolled(shifted, span - 1), b)
            serve(5 + b)
        free(l, 1)

        each_block(
            gated, dmall, lambda n, value: dO.__setitem__((parity, n), value), HALVES
        )
        for i in range(3):
            each_block(mixes3.at[i], lefts.at[i], to_dA(i))
        pl.semaphore_wait(sib_credit.at[1], 1)
        half_copy(l, parity, A0).start()
        half_copy(l, parity, OO).start()
        serve(7)
        for b in streams:
            dn = rs_wait(b)
            hat, rstd = normed(hsave[l, b])
            add_small(0, column_sum(dn * hat))
            add_small(2, column_sum(dn))
            dh = cur[b] + norm_back(dn, parb[l, 0:1, :], hat, rstd)
            result = dh.astype(BF)
            gradb[b] = result
            cur[b] = result.astype(F32)
        for i, value in sums.items():
            sg[l, i : i + 1, my_cols if i in (9, 10) else slice(None)] = value
        for i in GROUPS:
            half_copy(l, parity, i).wait_send()
        return carry

    lax.fori_loop(0, layers, backward, 0)

    tg_args = (swap_self, gradb, tgrad, out_s.at[1], out_r.at[1], t, p)
    start_any(*tg_args)

    def sg_copy(r):
        return plane(sg.at[next_pipe(r)], sgr.at[r - 1], sg_s.at[r - 1], sg_r.at[r - 1], r)

    lanes = sg8.shape[-1]

    def sg_cols(rank, half):
        return pl.ds(pl.multiple_of(lanes * (rank * HALVES + half), lanes), lanes)

    def sg8_copy(a, b):
        rank, half = next_rank(a), (c + b) % HALVES
        n = a * HALVES + b
        return remote(
            sgt.at[:, sg_cols(rank, half)], sg8.at[n], sg8_s.at[n], sg8_r.at[n], p, rank, half
        )

    others = [(a, b) for a in range(RANKS) for b in range(HALVES) if a or b]
    for r in range(1, RANKS):
        sg_copy(r).start()
    for l in range(layers):

        @pl.when(l == p)
        def _():
            for i in PIECES:
                for way in range(2):
                    if not late(layers - 1 - l, i, way):
                        hand_out(i, way)

    end = SERVICES * layers
    for time in range(end, 1 + max(slots[-1] for _, _, _, slots in BACK)):
        serve_back(time)
        if time == end + 1:
            for r in range(1, RANKS):
                sg_copy(r).wait()
            total = sg[p]
            for r in range(1, RANKS):
                total = total + sgr[r - 1]
            sgt[...] = total
            for a, b in others:
                sg8_copy(a, b).start()
    total = sgt[:, sg_cols(t, c)]
    for a, b in others:
        sg8_copy(a, b).wait()
        total = total + sg8[a * HALVES + b]
    small[...] = total

    for l in range(layers):
        sent_any(*fin_args(l))
    for r in range(1, RANKS):
        par_copy(r).wait_send()
    carried_sent()
    sent_any(swap_self, mixb, mixed, out_s.at[0], out_r.at[0], t, p)
    got_any(swap_self, mixed, out_r.at[0])
    sent_any(*tg_args)
    got_any(swap_self, tgrad, out_r.at[1])
    for l in range(2):
        all_sent(l, (layers - 1 - l) % 2, PIECES)
    for i in PIECES:
        for way in range(2):
            if i in (V0, V1, OO):
                home_own(i, way).wait()
            else:
                for args in home_args(i, way):
                    if args[-1]:
                        home_copy(*args).wait_send()
                    else:
                        home_copy(*args).wait()
    for src in range(RANKS):
        cols = pl.ds(src * quarter, quarter)
        got_any(jnp.logical_and(swap_self, t == src), finout.at[:, :, cols], fin_r.at[src])
        if src:
            for m, grad in enumerate((gk, gv, gr, gfr)):
                got(grad.at[:, cols], r1_r.at[m, src])
            got(gfk.at[:, pl.ds(src * hidden, hidden)], r1_r.at[4, src])


def on_device(
    outer,
    tokens,
    cotangent,
    lengths,
    carried,
    norm_gain,
    norm_bias,
    mix_rates,
    time_decay,
    time_first,
    attention_accept_proj,
    attention_lookup_proj,
    attention_content_proj,
    attention_result_proj,
    feedforward_accept_proj,
    feedforward_lookup_proj,
    feedforward_content_proj,
):
    layers = lax.axis_size("pipe")
    micro, chunk, width = tokens.shape
    row_count = chunk * RANKS
    rows = micro * row_count
    per = lengths.shape[1]
    seqs = micro * per
    weights = [
        attention_lookup_proj[0],
        attention_content_proj[0],
        attention_accept_proj[0],
        feedforward_accept_proj[0],
        attention_result_proj[0],
        feedforward_lookup_proj[0],
        feedforward_content_proj[0],
    ]
    near = [[b * outer + i for i in range(outer)] for b in range(RANKS * HALVES)]
    if outer > 1:
        weights = [
            lax.all_gather(w, "dp", axis=0, tiled=True, axis_index_groups=near) for w in weights
        ]
    block = width // (RANKS * HALVES)
    hidden = weights[5].shape[1] // RANKS
    quarter = width // RANKS
    vmem = pl.BlockSpec(memory_space=pltpu.VMEM)
    smem = pl.BlockSpec(memory_space=pltpu.SMEM)
    hbm = pl.BlockSpec(memory_space=pl.ANY)
    dma = pltpu.SemaphoreType.DMA
    regular = pltpu.SemaphoreType.REGULAR
    n_peers = RANKS - 1
    own = (micro, chunk, width)
    full = (micro, row_count, width)

    def stores(count):
        return [
            pltpu.VMEM((count, RANKS, HALVES, block, width), BF),
            pltpu.VMEM((count, HALVES, block, width), BF),
            pltpu.VMEM((count, RANKS, HALVES, block, hidden), BF),
            pltpu.VMEM((count, HALVES, hidden // HALVES, width), BF),
        ]

    outs = pl.pallas_call(
        partial(layers_kernel, outer, row_count // 2),
        out_shape=(
            jax.ShapeDtypeStruct(own, BF),
            jax.ShapeDtypeStruct(own, BF),
            jax.ShapeDtypeStruct((5, seqs, width), F32),
            jax.ShapeDtypeStruct((16, block), F32),
        )
        + tuple(jax.ShapeDtypeStruct(w.shape, BF) for w in weights),
        in_specs=[vmem] * 2 + [smem] + [vmem] * 6 + [hbm] * 7,
        out_specs=(vmem,) * 4 + (hbm,) * 7,
        scratch_shapes=stores(layers)
        + stores(2)
        + [
            pltpu.VMEM(own, BF),
            pltpu.VMEM(own, BF),
            pltpu.VMEM((16, 128), F32),
            pltpu.VMEM((16, 128), F32),
            pltpu.VMEM((32, width), BF),
            pltpu.VMEM((layers, 32, quarter), BF),
            pltpu.VMEM((16, width), BF),
            pltpu.VMEM((layers, 16, width), BF),
            pltpu.VMEM((16, width), F32),
            pltpu.VMEM((layers, 16, width), F32),
            pltpu.VMEM((layers,) + full, BF),
            pltpu.VMEM((layers,) + full, BF),
            pltpu.VMEM((layers,) + own, F32),
            pltpu.VMEM((layers,) + own, F32),
            pltpu.VMEM((layers,) + own, F32),
            pltpu.VMEM((layers,) + own, F32),
            pltpu.VMEM((layers, micro, row_count, hidden), BF),
            pltpu.VMEM((layers, micro, row_count, quarter), F32),
            pltpu.VMEM((layers, micro, row_count, quarter), F32),
            pltpu.VMEM((layers, 7, micro, row_count, quarter), BF),
            pltpu.VMEM(full, BF),
            pltpu.VMEM((micro, n_peers, chunk, width), BF),
            pltpu.VMEM((micro, row_count, quarter), BF),
            pltpu.VMEM(own, BF),
            pltpu.VMEM(own, F32),
            pltpu.VMEM((layers, 5, seqs, quarter), F32),
            pltpu.VMEM(own, BF),
            pltpu.VMEM(own, BF),
            pltpu.VMEM(full, BF),
            pltpu.VMEM(full, BF),
            pltpu.VMEM(own, BF),
            pltpu.VMEM((micro, row_count, quarter), BF),
            pltpu.VMEM(full, BF),
            pltpu.VMEM(full, BF),
            pltpu.VMEM((micro, row_count, hidden), BF),
            pltpu.VMEM((micro, row_count, hidden), BF),
            pltpu.VMEM((3,) + full, BF),
            pltpu.VMEM((3, micro, row_count, quarter), BF),
            pltpu.VMEM((micro, row_count, quarter), BF),
            pltpu.VMEM((layers, 16, width), F32),
            pltpu.VMEM((n_peers, 16, width), F32),
            pltpu.VMEM((16, width), F32),
            pltpu.VMEM((RANKS * HALVES, 16, block), F32),
            dma((3,)),
            dma((3,)),
            dma((RANKS,)),
            dma((layers,)),
            dma((RANKS,)),
            dma((layers,)),
            dma((n_peers,)),
            dma((layers,)),
            dma((5, n_peers)),
            dma((5, n_peers)),
            dma((7,)),
            dma((layers, 7, 2)),
            dma((layers, 7, 2)),
            dma((layers, 4)),
            dma((layers, 4)),
            dma((micro, n_peers)),
            dma((micro, n_peers)),
            dma((micro, n_peers)),
            dma((micro, n_peers)),
            dma((micro, n_peers)),
            dma((micro, n_peers)),
            dma((micro, n_peers)),
            dma((micro, n_peers)),
            dma((layers,)),
            dma((RANKS,)),
            dma((2,)),
            dma((2,)),
            dma((layers, 4)),
            dma((layers, 4)),
            dma((layers, 7, 2)),
            dma((layers, 7, 2)),
            dma((5, RANKS)),
            dma((5, RANKS)),
            dma((6,)),
            dma((n_peers,)),
            dma((n_peers,)),
            dma((RANKS * HALVES,)),
            dma((RANKS * HALVES,)),
            regular((layers, 2, 2)),
            regular((2,)),
        ],
        compiler_params=pltpu.CompilerParams(
            collective_id=0, has_side_effects=True, vmem_limit_bytes=60 * 2**20
        ),
        name="layers",
    )(
        tokens,
        cotangent,
        lengths,
        carried,
        norm_gain,
        norm_bias,
        mix_rates,
        time_decay,
        time_first,
        *weights,
    )
    mixed, tgrad, fin, small, *grads = outs
    if outer > 1:
        grads = [
            lax.psum_scatter(g, "dp", scatter_dimension=0, tiled=True, axis_index_groups=near)
            for g in grads
        ]
        small = lax.psum_scatter(
            small, "dp", scatter_dimension=1, tiled=True, axis_index_groups=near
        )
    gk, gv, gr, gfr, go, gfk, gfv = [g.astype(F32)[None] for g in grads]
    small = small[None]
    return (
        mixed,
        tgrad.astype(F32),
        fin.transpose(1, 0, 2).reshape(micro, per, 1, 5, width),
        small[:, 0:2],
        small[:, 2:4],
        small[:, 4:9],
        small[:, 9],
        small[:, 10],
        gr,
        gk,
        gv,
        go,
        gfr,
        gfk,
        gfv,
    )


def solution(mesh):
    outer = mesh.shape["dp"] // (RANKS * HALVES)
    placed = (
        P("dp", "pipe", None),
        P("dp", "pipe", None),
        P("dp", None),
        P("dp", None, "pipe", None, None),
        P("pipe", None, None),
        P("pipe", None, None),
        P("pipe", None, None),
        P("pipe", None),
        P("pipe", None),
    ) + (P("pipe", "dp", None),) * 7
    return jax.shard_map(
        partial(on_device, outer),
        mesh=mesh,
        in_specs=placed,
        out_specs=(
            P("dp", "pipe", None),
            P("dp", "pipe", None),
            P("dp", None, "pipe", None, None),
            P("pipe", None, "dp"),
            P("pipe", None, "dp"),
            P("pipe", None, "dp"),
            P("pipe", "dp"),
            P("pipe", "dp"),
        )
        + (P("pipe", "dp", None),) * 7,
        check_vma=False,
    )
```

```python
from functools import partial

import jax
import jax.numpy as jnp
from jax import lax
from jax.sharding import PartitionSpec as P
from jax.experimental import pallas as pl
from jax.experimental.pallas import tpu as pltpu

EPS = 1e-05
BF = jnp.bfloat16
F32 = jnp.float32
HIGH = lax.Precision.HIGHEST
MESH = pl.DeviceIdType.MESH
RANKS = 4
HALVES = 2


def dot(a, b, precision=None):
    return jnp.dot(a, b, precision=precision, preferred_element_type=F32)


def dot_nt(a, b):
    return lax.dot_general(a, b, (((1,), (1,)), ((), ())), preferred_element_type=F32)


def dot_tn(a, b):
    return lax.dot_general(a, b, (((0,), (0,)), ((), ())), preferred_element_type=F32)


def rolled(x, shift):
    return pltpu.roll(x, shift % x.shape[0], 0)


def normed(h):
    center = h - jnp.mean(h, axis=-1, keepdims=True)
    spread = jnp.mean(center * center, axis=-1, keepdims=True)
    rstd = lax.rsqrt(spread + EPS)
    return center * rstd, rstd


def norm_back(dn, gain, hat, rstd):
    dh = dn * gain
    return rstd * (
        dh
        - jnp.mean(dh, axis=-1, keepdims=True)
        - hat * jnp.mean(dh * hat, axis=-1, keepdims=True)
    )


def column_sum(x):
    return jnp.sum(x, axis=0, keepdims=True)


def ring_place(pipe):
    return pipe + (pipe // 2) * (5 - 2 * pipe)


A0, A1, V0, V1, K0, K1, OO = range(7)
FORTH = (
    (0, A0, 0, (-8, -3, -1, 0)),
    (0, A0, 1, (-8, -3, -1, 0)),
    (0, A1, 0, (-6, -2, 0, 1)),
    (0, A1, 1, (-6, -3, 0, 1)),
    (0, V0, 0, (-6, -2, 1, 4)),
    (0, V0, 1, (-9, -6, -3, 1)),
    (0, V1, 0, (-1, 0, 2, 3)),
    (0, V1, 1, (-9, -2, 1, 3)),
    (0, K0, 0, (-5, 0, 3, 5)),
    (0, K0, 1, (-5, 0, 3, 4)),
    (0, K1, 0, (0, 1, 4, 5)),
    (0, K1, 1, (0, 1, 4, 5)),
    (0, OO, 0, (-12, -6, -3, -2)),
    (0, OO, 1, (-12, -4, -3, -2)),
    (1, A0, 0, (-10, -5, -4, 3)),
    (1, A0, 1, (-10, -2, -1, 3)),
    (1, A1, 0, (-6, -2, 2, 7)),
    (1, A1, 1, (-3, 3, 5, 8)),
    (1, V0, 0, (2, 5, 7, 13)),
    (1, V0, 1, (-4, -1, 1, 7)),
    (1, V1, 0, (-8, -5, 2, 9)),
    (1, V1, 1, (-3, 0, 6, 12)),
    (1, K0, 0, (3, 7, 9, 13)),
    (1, K0, 1, (1, 4, 9, 12)),
    (1, K1, 0, (2, 6, 8, 12)),
    (1, K1, 1, (4, 6, 7, 11)),
    (1, OO, 0, (-8, -4, -1, 6)),
    (1, OO, 1, (-9, 3, 5, 8)),
    (2, A0, 0, (-7, 2, 3, 10)),
    (2, A0, 1, (-7, 2, 5, 12)),
    (2, A1, 0, (-1, 8, 13, 16)),
    (2, A1, 1, (1, 6, 10, 15)),
    (2, V0, 0, (-8, 12, 14, 20)),
    (2, V0, 1, (14, 16, 19, 21)),
    (2, V1, 0, (-3, 6, 9, 19)),
    (2, V1, 1, (-10, 5, 7, 12)),
    (2, K0, 0, (-3, 4, 8, 14)),
    (2, K0, 1, (12, 15, 18, 21)),
    (2, K1, 0, (-1, 17, 18, 20)),
    (2, K1, 1, (9, 13, 16, 19)),
    (2, OO, 0, (-10, 3, 8, 16)),
    (2, OO, 1, (-10, 4, 9, 14)),
    (3, A0, 0, (-6, 3, 9, 20)),
    (3, A0, 1, (-6, 3, 9, 20)),
    (3, A1, 0, (12, 14, 20, 23)),
    (3, A1, 1, (10, 13, 21, 24)),
    (3, V0, 0, (9, 12, 18, 20)),
    (3, V0, 1, (-9, -2, 12, 16)),
    (3, V1, 0, (15, 19, 21, 27)),
    (3, V1, 1, (-10, -4, 7, 21)),
    (3, K0, 0, (12, 16, 18, 28)),
    (3, K0, 1, (6, 12, 19, 24)),
    (3, K1, 0, (10, 16, 23, 28)),
    (3, K1, 1, (8, 14, 17, 27)),
    (3, OO, 0, (-9, 1, 11, 16)),
    (3, OO, 1, (-9, 1, 10, 15)),
)
BACK = (
    (0, A0, 0, (8, 10, 17, 20)),
    (0, A0, 1, (8, 9, 11, 18)),
    (0, A1, 0, (10, 13, 19, 20)),
    (0, A1, 1, (12, 16, 17, 20)),
    (0, V0, 0, (4, 7, 9, 15)),
    (0, V0, 1, (6, 8, 10, 17)),
    (0, V1, 0, (9, 12, 15, 18)),
    (0, V1, 1, (4, 6, 8, 13)),
    (0, K0, 0, (7, 8, 13, 17)),
    (0, K0, 1, (5, 7, 9, 17)),
    (0, K1, 0, (5, 7, 10, 13)),
    (0, K1, 1, (10, 11, 13, 17)),
    (0, OO, 0, (8, 11, 17, 19)),
    (0, OO, 1, (8, 10, 12, 17)),
    (1, A0, 0, (17, 20, 24, 28)),
    (1, A0, 1, (21, 22, 25, 28)),
    (1, A1, 0, (18, 19, 25, 28)),
    (1, A1, 1, (16, 19, 22, 26)),
    (1, V0, 0, (12, 13, 15, 19)),
    (1, V0, 1, (13, 15, 18, 21)),
    (1, V1, 0, (14, 15, 17, 24)),
    (1, V1, 1, (13, 16, 19, 26)),
    (1, K0, 0, (13, 14, 16, 26)),
    (1, K0, 1, (17, 20, 23, 26)),
    (1, K1, 0, (15, 16, 18, 24)),
    (1, K1, 1, (12, 14, 17, 19)),
    (1, OO, 0, (21, 22, 24, 27)),
    (1, OO, 1, (16, 21, 24, 27)),
    (2, A0, 0, (38, 39, 40, 41)),
    (2, A0, 1, (26, 30, 33, 35)),
    (2, A1, 0, (25, 32, 33, 38)),
    (2, A1, 1, (27, 32, 34, 37)),
    (2, V0, 0, (20, 23, 26, 35)),
    (2, V0, 1, (21, 25, 27, 37)),
    (2, V1, 0, (20, 24, 26, 37)),
    (2, V1, 1, (35, 38, 39, 41)),
    (2, K0, 0, (34, 39, 40, 41)),
    (2, K0, 1, (20, 23, 28, 33)),
    (2, K1, 0, (22, 26, 28, 39)),
    (2, K1, 1, (25, 29, 31, 37)),
    (2, OO, 0, (31, 33, 38, 39)),
    (2, OO, 1, (32, 34, 38, 39)),
    (3, A0, 0, (38, 39, 40, 41)),
    (3, A0, 1, (34, 37, 38, 40)),
    (3, A1, 0, (32, 36, 37, 39)),
    (3, A1, 1, (34, 38, 39, 40)),
    (3, V0, 0, (32, 37, 38, 40)),
    (3, V0, 1, (33, 37, 38, 40)),
    (3, V1, 0, (29, 32, 35, 40)),
    (3, V1, 1, (34, 38, 39, 41)),
    (3, K0, 0, (32, 37, 38, 39)),
    (3, K0, 1, (29, 32, 34, 37)),
    (3, K1, 0, (28, 30, 32, 33)),
    (3, K1, 1, (28, 31, 32, 35)),
    (3, OO, 0, (36, 38, 39, 41)),
    (3, OO, 1, (34, 38, 39, 41)),
)
PIECES = range(7)
SERVICES = 8
ROWS_FROM = {(A0, 0): 0, (A1, 0): 1, (A0, 1): 3, (A1, 1): 2, (K0, 0): 0, (K1, 0): 1, (K0, 1): 3, (K1, 1): 2}
GROUPS = (A0, V0, K0, OO)


def layers_kernel(
    outer,
    longest,
    tok,
    cot,
    lens,
    held,
    gain,
    bias,
    mixes,
    decay,
    first,
    wk,
    wv,
    wr,
    wfr,
    wo,
    wfk,
    wfv,
    mixed,
    tgrad,
    finout,
    small,
    gk,
    gv,
    gr,
    gfr,
    go,
    gfk,
    gfv,
    wA,
    wO,
    wK,
    wV,
    dA,
    dO,
    dK,
    dV,
    tokb,
    cotb,
    info,
    infob,
    stsrc,
    stb,
    shsrc,
    shb,
    par,
    parb,
    nsave,
    n2save,
    hsave,
    msave,
    kvsave,
    gatesave,
    zsave,
    alsave,
    besave,
    smsave,
    part,
    rbuf,
    r2st,
    r2full,
    cur,
    finb,
    mixb,
    gradb,
    dkvall,
    dmall,
    dr2o,
    dr2c,
    mixk,
    mixr,
    squares,
    dzs,
    mixes3,
    lefts,
    gated,
    sg,
    sgr,
    sgt,
    sg8,
    x_s,
    x_r,
    st_s,
    st_r,
    sh_s,
    sh_r,
    par_s,
    par_r,
    w1_s,
    w1_r,
    w1_l,
    rw_s,
    rw_r,
    w3_s,
    w3_r,
    ag_s,
    ag_r,
    rs_s,
    rs_r,
    a2_s,
    a2_r,
    a2b_s,
    a2b_r,
    fin_s,
    fin_r,
    out_s,
    out_r,
    a_s,
    a_r,
    rd_s,
    rd_r,
    r1_s,
    r1_r,
    r1_l,
    sg_s,
    sg_r,
    sg8_s,
    sg8_r,
    credit,
    sib_credit,
):
    p = lax.axis_index("pipe")
    d = lax.axis_index("dp")
    t = d // (HALVES * outer)
    c = (d // outer) % HALVES
    o = d % outer
    ring = ring_place(p)
    micro, chunk, width = tok.shape
    layers = stb.shape[0]
    rows = micro * chunk * RANKS
    quarter = width // RANKS
    mine = pl.ds(pl.multiple_of(chunk * t, chunk), chunk)
    my_cols = pl.ds(pl.multiple_of(quarter * t, quarter), quarter)
    hidden = wfk.shape[1] // RANKS
    my_hidden = pl.ds(pl.multiple_of(hidden * t, hidden), hidden)
    block = wk.shape[0]
    seqs = held.shape[0] * held.shape[1]
    per = held.shape[1]

    def place(rank, half):
        return (rank * HALVES + half) * outer + o

    def next_rank(r):
        return (t + r) % RANKS

    def next_pipe(r):
        return (p + r) % RANKS

    def on_ring(r):
        return ring_place((ring + r) % RANKS)

    def remote(src, dst, ss, rs, pipe, rank, half):
        return pltpu.make_async_remote_copy(
            src_ref=src,
            dst_ref=dst,
            send_sem=ss,
            recv_sem=rs,
            device_id=(pipe, place(rank, half)),
            device_id_type=MESH,
        )

    def peer(src, dst, ss, rs, r):
        return remote(src, dst, ss, rs, p, next_rank(r), c)

    def plane(src, dst, ss, rs, r):
        return remote(src, dst, ss, rs, next_pipe(r), t, c)

    def sibling(src, dst, ss, rs):
        return remote(src, dst, ss, rs, p, t, 1 - c)

    def start_any(is_self, src, dst, ss, rs, pipe, rank):
        @pl.when(is_self)
        def _():
            pltpu.make_async_copy(src, dst, ss).start()

        @pl.when(jnp.logical_not(is_self))
        def _():
            remote(src, dst, ss, rs, pipe, rank, c).start()

    def sent_any(is_self, src, dst, ss, rs, pipe, rank):
        @pl.when(is_self)
        def _():
            pltpu.make_async_copy(src, dst, ss).wait()

        @pl.when(jnp.logical_not(is_self))
        def _():
            remote(src, dst, ss, rs, pipe, rank, c).wait_send()

    def got(dst, rs):
        remote(dst, dst, rs, rs, next_pipe(1), t, c).wait_recv()

    def got_any(is_self, dst, rs):
        @pl.when(jnp.logical_not(is_self))
        def _():
            got(dst, rs)

    barrier = pltpu.get_barrier_semaphore()
    for a in range(RANKS):
        for b in range(RANKS):
            if a or b:
                pl.semaphore_signal(
                    barrier,
                    inc=1,
                    device_id=(next_pipe(a), place(next_rank(b), c)),
                    device_id_type=MESH,
                )
    for b in range(RANKS):
        pl.semaphore_signal(
            barrier, inc=1, device_id=(p, place(next_rank(b), 1 - c)), device_id_type=MESH
        )
    pl.semaphore_wait(barrier, RANKS * RANKS - 1 + RANKS)

    raw = (wk, wv, wr, wfr)

    def w1(m, r):
        rank = next_rank(r)
        if m < 4:
            cols = pl.ds(pl.multiple_of(quarter * rank, quarter), quarter)
            return peer(
                raw[m].at[:, cols],
                wA.at[p, t, c, :, pl.ds(m * quarter, quarter)],
                w1_s.at[m, r - 1],
                w1_r.at[m, r - 1],
                r,
            )
        cols = pl.ds(pl.multiple_of(hidden * rank, hidden), hidden)
        return peer(wfk.at[:, cols], wK.at[p, t, c], w1_s.at[m, r - 1], w1_r.at[m, r - 1], r)

    def w1_own(m):
        if m < 4:
            return pltpu.make_async_copy(
                raw[m].at[:, my_cols], wA.at[p, t, c, :, pl.ds(m * quarter, quarter)], w1_l.at[m]
            )
        if m == 4:
            return pltpu.make_async_copy(wfk.at[:, my_hidden], wK.at[p, t, c], w1_l.at[m])
        if m == 5:
            return pltpu.make_async_copy(wo, wO.at[p, c], w1_l.at[m])
        return pltpu.make_async_copy(wfv, wV.at[p, c], w1_l.at[m])

    for m in range(7):
        w1_own(m).start()
    for group_m in ((0, 1, 2, 3), (4,)):
        for r in (1, 3, 2):
            for m in group_m:
                w1(m, r).start()

    lane = lax.broadcasted_iota(jnp.int32, info.shape, 1)
    line = lax.broadcasted_iota(jnp.int32, info.shape, 0)
    marks = jnp.full(info.shape, -1, jnp.int32)
    for b in range(micro):
        at = b * (rows // micro)
        for s in range(per):
            index = b * per + s
            marks = jnp.where(jnp.logical_and(line == 0, lane == index), at, marks)
            at = at + lens[b, s]
            marks = jnp.where(line == 8 + index, at - 1, marks)
    info[...] = marks.astype(F32)

    swap_self = p == t
    swaps = [(tok, tokb), (info, infob), (cot, cotb)]
    for i, (src, dst) in enumerate(swaps):
        start_any(swap_self, src, dst, x_s.at[i], x_r.at[i], t, p)

    par[0:2, :] = gain[0]
    par[2:4, :] = bias[0]
    for i in range(mixes.shape[0]):
        par[4 + i : 5 + i, :] = mixes[i]
    par[9:10, :] = decay[...]
    par[10:11, :] = first[...]
    par[11:16, :] = jnp.zeros((5, width), F32)

    def par_copy(r):
        return plane(par, parb.at[p], par_s.at[r - 1], par_r.at[p], r)

    for r in range(1, RANKS):
        par_copy(r).start()
    parb[p] = par[...]

    carried_rows = [
        jnp.concatenate([held[b, s, i] for b in range(micro) for s in range(per)], axis=0)
        for i in range(5)
    ]
    spare = jnp.zeros((8, width), F32)
    stsrc[...] = jnp.concatenate(carried_rows[0:3] + [spare], axis=0).astype(BF)
    shsrc[...] = jnp.concatenate(carried_rows[3:5], axis=0).astype(BF)

    def state_args(rank):
        return (
            jnp.logical_and(swap_self, rank == t),
            stsrc.at[:, pl.ds(quarter * rank, quarter)],
            stb.at[p],
            st_s.at[rank],
            st_r.at[p],
            t,
            rank,
        )

    def shift_args(rank):
        return (
            jnp.logical_and(swap_self, rank == t),
            shsrc,
            shb.at[p],
            sh_s.at[rank],
            sh_r.at[p],
            t,
            rank,
        )

    def send_carried(l):
        @pl.when(p == l)
        def _():
            for rank in range(RANKS):
                start_any(*shift_args(rank))
                start_any(*state_args(rank))

    def get_carried(l):
        from_self = jnp.logical_and(swap_self, p == l)

        @pl.when(from_self)
        def _():
            for rank in range(RANKS):

                @pl.when(rank == t)
                def _():
                    pltpu.make_async_copy(*shift_args(rank)[1:4]).wait()
                    pltpu.make_async_copy(*state_args(rank)[1:4]).wait()

        got_any(from_self, shb.at[l], sh_r.at[l])
        got_any(from_self, stb.at[l], st_r.at[l])
        got_any(p == l, parb.at[l], par_r.at[l])

    def carried_sent():
        for rank in range(RANKS):

            @pl.when(jnp.logical_not(jnp.logical_and(swap_self, rank == t)))
            def _():
                remote(*shift_args(rank)[1:], c).wait_send()
                remote(*state_args(rank)[1:], c).wait_send()

    def piece(store, at, i, way, half):
        a, small_one, k, v = store
        if i in (A0, A1, K0, K1):
            return (a if i in (A0, A1) else k).at[at, next_rank(ROWS_FROM[i, way]), half]
        size = (small_one if i == OO else v).shape[2] // 2
        if i == OO:
            return small_one.at[at, half, pl.ds(way * size, size)]
        return v.at[at, half, pl.ds(way * size + (i - V0) * (size // 2), size // 2)]

    def group(store, at, i, half):
        a, small_one, k, v = store
        if i == A0:
            return a.at[at, :, half]
        if i == K0:
            return k.at[at, :, half]
        return small_one.at[at, half] if i == OO else v.at[at, half]

    def group_of(i):
        return GROUPS.index({A1: A0, V1: V0, K1: K0}.get(i, i))

    weights = (wA, wO, wK, wV)
    grads = (dA, dO, dK, dV)

    def steps_from(l, way):
        home = ring_place(l)
        return (ring - home + RANKS) % RANKS if way == 0 else (home - ring + RANKS) % RANKS

    def forth_copy(l, i, way):
        return remote(
            piece(weights, l, i, way, c),
            piece(weights, l, i, way, c),
            rw_s.at[l, i, way],
            rw_r.at[l, i, way],
            on_ring(1 if way == 0 else RANKS - 1),
            t,
            c,
        )

    def pair_copy(l, i, way):
        g = group_of(i)
        return sibling(
            piece(weights, l, i, way, c),
            piece(weights, l, i, way, c),
            w3_s.at[l, g],
            w3_r.at[l, g],
        )

    def bring(l, i, way, hop):
        @pl.when(steps_from(l, way) == hop)
        def _():
            if hop:
                forth_copy(l, i, way).wait_recv()
            else:
                rows_in(i, way)
            if hop < RANKS - 1:
                forth_copy(l, i, way).start()
            pair_copy(l, i, way).start()

    def rows_in(i, way):
        if i == OO:
            return None
        if i in (V0, V1):
            return None
        for m in range(4) if i in (A0, A1) else (4,):
            if ROWS_FROM[i, way]:
                w1(m, RANKS - ROWS_FROM[i, way]).wait_recv()
            else:
                w1_own(m).wait()

    def due(plan, time):
        for l, i, way, slots in plan:
            for hop, slot in enumerate(slots):
                if slot == time:
                    yield l, i, way, hop

    def serve_forth(time):
        for l, i, way, hop in due(FORTH, time):
            bring(l, i, way, hop)

    def weights_here(l, i):
        ref = group(weights, l, i, 1 - c)
        sem = w3_r.at[l, group_of(i)]
        sibling(ref, ref, sem, sem).wait_recv()

    send_carried(0)
    w1_own(5).wait()
    w1_own(6).wait()
    for time in range(min(slots[0] for _, _, _, slots in FORTH), 0):
        serve_forth(time)

    for i in range(2):
        src, dst = swaps[i]
        sent_any(swap_self, src, dst, x_s.at[i], x_r.at[i], t, p)
        got_any(swap_self, dst, x_r.at[i])

    streams = range(micro)
    span = rows // micro

    def ag(buf, r, b):
        return peer(buf.at[b, mine], buf.at[b, mine], ag_s.at[b, r - 1], ag_r.at[b, r - 1], r)

    def ag_start(buf, b):
        for r in range(1, RANKS):
            ag(buf, r, b).start()

    def ag_wait(buf, b):
        for r in range(1, RANKS):
            ag(buf, r, b).wait()

    def rs(r, b):
        theirs = pl.ds(pl.multiple_of(chunk * next_rank(r), chunk), chunk)
        return peer(
            part.at[b, theirs], rbuf.at[b, r - 1], rs_s.at[b, r - 1], rs_r.at[b, r - 1], r
        )

    def rs_start(values, b):
        part[b] = values.astype(BF)
        for r in range(1, RANKS):
            rs(r, b).start()

    def rs_wait(b):
        for r in range(1, RANKS):
            rs(r, b).wait()
        total = part[b, mine, :].astype(F32)
        for r in range(1, RANKS):
            total = total + rbuf[b, r - 1].astype(F32)
        return total

    cur[...] = tokb[...].astype(F32)

    starts = infob[0:1, 0:seqs]
    ends = infob[8 : 8 + seqs, 0:span]
    line = lax.broadcasted_iota(jnp.int32, (span, seqs), 0).astype(F32)
    lane = lax.broadcasted_iota(jnp.int32, (seqs, span), 1).astype(F32)
    none = jnp.zeros((span, seqs), F32)
    hot, onset, stay, hots, place_in, last_hot = [], [], [], [], [], []
    for b in streams:
        at = line + b * span
        hot.append((at == starts).astype(F32))
        onset.append(jnp.sum(hot[b], axis=1, keepdims=True))
        stay.append(1.0 - onset[b])
        hots.append(
            [jnp.concatenate(pair, axis=1).astype(BF) for pair in ((hot[b], none), (none, hot[b]))]
        )
        begun = jnp.max(jnp.where(starts <= at, starts, 0.0), axis=1, keepdims=True)
        place_in.append(at[:, 0:1] - begun)
        last_hot.append((lane + b * span == ends).astype(F32))
    reaches = []
    reach = 1
    while reach < longest:
        reaches.append(reach)
        reach *= 2

    def whole(ref):
        return ref[...].reshape(rows, ref.shape[-1])

    def before(n, l, which, b):
        return rolled(n, 1) * stay[b] + dot(hots[b][which], shb[l])

    def rate(l, i):
        return parb[l, 4 + i : 5 + i, :]

    def fin_args(l):
        return (
            jnp.logical_and(l == p, swap_self),
            finb.at[l],
            finout.at[:, :, my_cols],
            fin_s.at[l],
            fin_r.at[t],
            l,
            p,
        )

    def forward(l, carry):
        def serve(k):
            if k == 0:

                @pl.when(l + 1 < layers)
                def _():
                    send_carried(l + 1)

            for at in range(layers):

                @pl.when(l == at)
                def _():
                    serve_forth(SERVICES * at + k)

        get_carried(l)
        for b in streams:
            h = cur[b]
            hsave[l, b] = h
            hat, _ = normed(h)
            n = hat * parb[l, 0:1, :] + parb[l, 2:3, :]
            nsave[l, b, mine, :] = n.astype(BF)
            ag_start(nsave.at[l], b)
        serve(0)
        serve(1)
        w = -jnp.exp(parb[l, 9:10, my_cols])
        u = parb[l, 10:11, my_cols]
        states = stb[l].astype(F32)
        for b in streams:
            ag_wait(nsave.at[l], b)
            n = nsave[l, b].astype(F32)
            prev = before(n, l, 0, b)
            gap = n - prev
            if b == 0:
                weights_here(l, A0)
            mats = []
            for i in range(3):
                mix = (prev + gap * rate(l, i)).astype(BF)
                mats.append(
                    dot(
                        mix, wA[l, :, :, :, i * quarter : (i + 1) * quarter].reshape(width, quarter)
                    )
                )
            k, v, r = mats
            init = [dot(hot[b], states[i * seqs : (i + 1) * seqs]) for i in range(3)]
            top = jnp.where(onset[b] > 0.5, jnp.maximum(k, w + init[2]), k)
            for s in reaches:
                top = jnp.maximum(top, jnp.where(place_in[b] >= s, rolled(top, s) + s * w, -1e30))
            top_prev = rolled(top, 1) * stay[b] + init[2]
            al = jnp.exp(w + top_prev - top)
            be = jnp.exp(k - top)
            num = be * v + onset[b] * al * init[0]
            den = be + onset[b] * al * init[1]
            keep = al * stay[b]
            for i, s in enumerate(reaches):
                num = num + keep * rolled(num, s)
                den = den + keep * rolled(den, s)
                if i + 1 < len(reaches):
                    keep = keep * rolled(keep, s)
            num_prev = rolled(num, 1) * stay[b] + init[0]
            den_prev = rolled(den, 1) * stay[b] + init[1]
            now = u + k
            peak = jnp.maximum(top_prev, now)
            e1 = jnp.exp(top_prev - peak)
            e2 = jnp.exp(now - peak)
            inv = 1.0 / (e1 * den_prev + e2)
            e1 = e1 * inv
            e2 = e2 * inv
            y = e1 * num_prev + e2 * v
            sr = jax.nn.sigmoid(r)
            g = (sr * y).astype(BF)
            if b == 0:
                weights_here(l, OO)
            rs_start(dot(g, wO[l].reshape(quarter, width)), b)
            alsave[l, b] = al
            besave[l, b] = be
            for i, value in enumerate((v, y, sr, e1, e2, num_prev, den_prev)):
                smsave[l, i, b] = value.astype(BF)
            lasts = [dot(last_hot[b], value, HIGH) for value in (num, den, top)]
            lasts.append(dot(last_hot[b].astype(BF), nsave[l, b, :, my_cols]))
            ending = [x + y for x, y in zip(ending, lasts)] if b else lasts
            serve(2 + b)
        for b in streams:
            m = hsave[l, b] + rs_wait(b)
            msave[l, b] = m
            hat, _ = normed(m)
            n2 = hat * parb[l, 1:2, :] + parb[l, 3:4, :]
            n2save[l, b, mine, :] = n2.astype(BF)
            ag_start(n2save.at[l], b)
        serve(4)
        serve(5)

        def a2(r, b):
            theirs = pl.ds(pl.multiple_of(chunk * next_rank(r), chunk), chunk)
            return peer(
                r2st.at[b, theirs],
                r2full.at[b, :, my_cols],
                a2_s.at[b, r - 1],
                a2_r.at[b, r - 1],
                r,
            )

        for b in streams:
            ag_wait(n2save.at[l], b)
            n = n2save[l, b].astype(F32)
            prev = before(n, l, 1, b)
            gap = n - prev
            mix = (prev + gap * rate(l, 4)).astype(BF)
            r2st[b] = dot(mix, wA[l, :, :, :, 3 * quarter :].reshape(width, quarter)).astype(BF)
            for r in range(1, RANKS):
                a2(r, b).start()
            r2full[b, :, my_cols] = r2st[b, mine, :]
            mix = (prev + gap * rate(l, 3)).astype(BF)
            if b == 0:
                weights_here(l, K0)
            z = dot(mix, wK[l].reshape(width, hidden))
            act = jnp.maximum(z, 0.0)
            if b == 0:
                weights_here(l, V0)
            rs_start(dot((act * act).astype(BF), wV[l].reshape(hidden, width)), b)
            zsave[l, b] = z.astype(BF)
            value = dot(last_hot[b].astype(BF), n2save[l, b, :, my_cols])
            last_n2 = last_n2 + value if b else value
            serve(6 + b)
        for i, value in enumerate(ending + [last_n2]):
            finb[l, i] = value
        start_any(*fin_args(l))
        for b in streams:
            for r in range(1, RANKS):
                a2(r, b).wait()
            kv = rs_wait(b)
            gate = jax.nn.sigmoid(r2full[b].astype(F32))
            kvsave[l, b] = kv
            gatesave[l, b] = gate
            result = (msave[l, b] + gate * kv).astype(BF)
            mixb[b] = result
            cur[b] = result.astype(F32)
        return carry

    lax.fori_loop(0, layers, forward, 0)

    for m in range(5):
        for r in range(1, RANKS):
            w1(m, r).wait_send()
    for l in range(layers):
        for i in PIECES:
            for way in range(2):

                @pl.when(steps_from(l, way) < RANKS - 1)
                def _():
                    forth_copy(l, i, way).wait_send()

        for i in GROUPS:
            ref = group(weights, l, i, c)
            sem = w3_s.at[l, group_of(i)]
            sibling(ref, ref, sem, sem).wait_send()

    start_any(swap_self, mixb, mixed, out_s.at[0], out_r.at[0], t, p)
    sent_any(swap_self, cot, cotb, x_s.at[2], x_r.at[2], t, p)
    got_any(swap_self, cotb, x_r.at[2])
    cur[...] = cotb[...].astype(F32)
    sg[...] = jnp.zeros_like(sg)

    def free(l, kind):
        for way in range(2):
            pl.semaphore_signal(
                credit.at[l, kind, way],
                inc=1,
                device_id=(on_ring(1 if way == 0 else RANKS - 1), place(t, c)),
                device_id_type=MESH,
            )
        pl.semaphore_signal(
            sib_credit.at[kind], inc=1, device_id=(p, place(t, 1 - c)), device_id_type=MESH
        )

    def add_to(into, ours, theirs):
        def some(n, carry):
            part_rows = pl.ds(pl.multiple_of(n * 32, 32), 32)
            into[part_rows, :] = (
                ours[part_rows, :].astype(F32) + theirs[part_rows, :].astype(F32)
            ).astype(BF)
            return carry

        lax.fori_loop(0, ours.shape[0] // 32, some, 0)

    def half_copy(l, parity, i):
        g = group_of(i)
        return sibling(
            group(grads, parity, i, 1 - c), group(weights, l, i, c), a_s.at[l, g], a_r.at[l, g]
        )

    def half_sum(l, parity, i):
        half_copy(l, parity, i).wait_recv()
        for j in PIECES:
            if GROUPS[group_of(j)] == i:
                for way in range(2):
                    ours = piece(grads, parity, j, way, c)
                    add_to(ours, ours, piece(weights, l, j, way, 1 - c))

    def back_copy(l, parity, i, way):
        return remote(
            piece(grads, parity, i, way, c),
            piece(weights, l, i, way, c),
            rd_s.at[l, i, way],
            rd_r.at[l, i, way],
            on_ring(RANKS - 1 if way == 0 else 1),
            t,
            c,
        )

    def home_args(i, way):
        ours = piece(weights, p, i, way, c)
        r = ROWS_FROM[i, way]
        if i in (A0, A1):
            return [
                (ours.at[:, pl.ds(m * quarter, quarter)], grad.at[:, my_cols], m, r)
                for m, grad in enumerate((gk, gv, gr, gfr))
            ]
        return [(ours, gfk.at[:, my_hidden], 4, r)]

    def home_copy(src, dst, m, r):
        if r:
            return peer(src, dst, r1_s.at[m, r], r1_r.at[m, r], r)
        return pltpu.make_async_copy(src, dst, r1_s.at[m, 0])

    def home_own(i, way):
        ours = piece(weights, p, i, way, c)
        size = ours.shape[0]
        if i == OO:
            return pltpu.make_async_copy(ours, go.at[pl.ds(way * size, size)], r1_l.at[4 + way])
        n = 2 * way + i - V0
        return pltpu.make_async_copy(ours, gfv.at[pl.ds(n * size, size)], r1_l.at[n])

    def hand_out(i, way):
        if i in (V0, V1, OO):
            home_own(i, way).start()
        else:
            for args in home_args(i, way):
                home_copy(*args).start()

    kinds = ((V0, V1, K0, K1), (A0, A1, OO))

    def opens(step, i, way, hop):
        kind = kinds[0] if i in kinds[0] else kinds[1]
        return i == min(
            (slots[hop], n, j)
            for n, (at, j, to, slots) in enumerate(BACK)
            if at == step and to == way and j in kind
        )[2]

    def collect(step, i, way, hop):
        l, parity = layers - 1 - step, step % 2

        @pl.when(steps_from(l, way) == RANKS - 1 - hop)
        def _():
            if opens(step, i, way, hop):
                pl.semaphore_wait(credit.at[l, int(i in kinds[1]), way], 1)
            ours = piece(grads, parity, i, way, c)
            theirs = piece(weights, l, i, way, c)
            if hop:
                back_copy(l, parity, i, way).wait_recv()
                add_to(theirs if hop == RANKS - 1 else ours, ours, theirs)
            if hop < RANKS - 1:
                back_copy(l, parity, i, way).start()
            elif late(step, i, way):
                hand_out(i, way)

    def late(step, i, way):
        return any(
            (at, j, to) == (step, i, way) and slots[-1] >= SERVICES * layers
            for at, j, to, slots in BACK
        )

    def serve_back(time):
        for at in range(layers):
            for i, when in ((V0, RANKS), (K0, RANKS), (A0, SERVICES), (OO, SERVICES)):
                if time == SERVICES * at + when:
                    half_sum(layers - 1 - at, at % 2, i)
        for step, i, way, hop in due(BACK, time):
            collect(step, i, way, hop)

    def all_sent(l, parity, pieces):
        for i in pieces:
            for way in range(2):

                @pl.when(steps_from(l, way) != 0)
                def _():
                    back_copy(l, parity, i, way).wait_send()

    def each_block(left_ref, right_ref, store, count=HALVES * RANKS):
        def body(n, carry):
            cols = pl.ds(pl.multiple_of(n * block, block), block)
            left = left_ref[:, :, cols].reshape(rows, block)
            store(n, dot_tn(left, whole(right_ref)).astype(BF))
            return carry

        lax.fori_loop(0, count, body, 0, unroll=2)

    def backward(step, carry):
        l = layers - 1 - step
        parity = step % 2

        def serve(k):
            for at in range(layers):

                @pl.when(step == at)
                def _():
                    serve_back(SERVICES * at + k)

        def a2(r, b):
            theirs = pl.ds(pl.multiple_of(quarter * next_rank(r), quarter), quarter)
            return peer(
                dr2o.at[b, :, theirs], dr2c.at[b, mine], a2b_s.at[b, r - 1], a2b_r.at[b, r - 1], r
            )

        sums = {}

        def add_small(i, value):
            sums[i] = sums[i] + value if i in sums else value

        for b in streams:
            dout = cur[b]
            gate = gatesave[l, b]
            dkvall[b, mine, :] = (dout * gate).astype(BF)
            ag_start(dkvall, b)
            dr2o[b] = (dout * kvsave[l, b] * gate * (1.0 - gate)).astype(BF)
            for r in range(1, RANKS):
                a2(r, b).start()
            dr2c[b, mine, :] = dr2o[b, :, my_cols]
        serve(0)
        for b in streams:
            n = n2save[l, b].astype(F32)
            prev = before(n, l, 1, b)
            gap = n - prev
            mixk[b] = (prev + gap * rate(l, 3)).astype(BF)
            mixr[b] = (prev + gap * rate(l, 4)).astype(BF)
            act = jnp.maximum(zsave[l, b].astype(F32), 0.0)
            squares[b] = (act * act).astype(BF)
            ag_wait(dkvall, b)
            for r in range(1, RANKS):
                a2(r, b).wait()
            dz = (2.0 * act * dot_nt(dkvall[b], wV[l].reshape(hidden, width))).astype(BF)
            dzs[b] = dz
            dx = dot_nt(dz, wK[l].reshape(width, hidden))
            dxr = dot_nt(dr2c[b], wA[l, :, :, :, 3 * quarter :].reshape(width, quarter))
            mixed_part = dx * rate(l, 3) + dxr * rate(l, 4)
            shifted = (dx + dxr - mixed_part) * stay[b]
            rs_start(mixed_part + rolled(shifted, span - 1), b)
            add_small(7, column_sum(dx * gap))
            add_small(8, column_sum(dxr * gap))
            serve(1 + b)
        free(l, 0)

        @pl.when(step > 1)
        def _():
            all_sent(l + 2, parity, (V0, V1, K0, K1))

        each_block(
            squares,
            dkvall,
            lambda n, value: dV.__setitem__(
                (parity, n // RANKS, pl.ds(pl.multiple_of((n % RANKS) * block, block), block)), value
            ),
        )
        each_block(
            mixk,
            dzs,
            lambda n, value: dK.__setitem__((parity, n // HALVES, n % HALVES), value),
        )
        pl.semaphore_wait(sib_credit.at[0], 1)
        half_copy(l, parity, V0).start()
        half_copy(l, parity, K0).start()
        serve(3)
        for b in streams:
            dn = rs_wait(b)
            hat, rstd = normed(msave[l, b])
            add_small(1, column_sum(dn * hat))
            add_small(3, column_sum(dn))
            dm = cur[b] + norm_back(dn, parb[l, 1:2, :], hat, rstd)
            cur[b] = dm
            dmall[b, mine, :] = dm.astype(BF)
            ag_start(dmall, b)
        serve(4)

        @pl.when(step > 1)
        def _():
            all_sent(l + 2, parity, (A0, A1, OO))

        def to_dA(m):
            def store(n, value):
                dA[parity, n // HALVES, n % HALVES, :, m * quarter : (m + 1) * quarter] = value

            return store

        each_block(mixr, dr2c, to_dA(3))
        w = -jnp.exp(parb[l, 9:10, my_cols])
        for b in streams:
            n = nsave[l, b].astype(F32)
            prev = before(n, l, 0, b)
            gap = n - prev
            for i in range(3):
                mixes3[i, b] = (prev + gap * rate(l, i)).astype(BF)
            al = alsave[l, b]
            be = besave[l, b]
            v, y, sr, e1, e2, num_prev, den_prev = [smsave[l, i, b].astype(F32) for i in range(7)]
            gated[b] = (sr * y).astype(BF)
            ag_wait(dmall, b)
            dg = dot_nt(dmall[b], wO[l].reshape(quarter, width))
            dr = (dg * y * sr * (1.0 - sr)).astype(BF)
            dy = dg * sr
            keep = rolled(al * stay[b], span - 1)
            into = dy * e1 * stay[b]
            ga = rolled(into, span - 1)
            gb = -rolled(into * y, span - 1)
            for i, s in enumerate(reaches):
                ga = ga + keep * rolled(ga, span - s)
                gb = gb + keep * rolled(gb, span - s)
                if i + 1 < len(reaches):
                    keep = keep * rolled(keep, span - s)
            near = dy * e2
            now = near * (v - y)
            dv = (be * ga + near).astype(BF)
            dk = (be * (v * ga + gb) + now).astype(BF)
            add_small(9, w * column_sum(al * (ga * num_prev + gb * den_prev)))
            add_small(10, column_sum(now))
            total = None
            mixed_part = None
            for i, left in enumerate((dk, dv, dr)):
                lefts[i, b] = left
                dx = dot_nt(
                    left, wA[l, :, :, :, i * quarter : (i + 1) * quarter].reshape(width, quarter)
                )
                add_small(4 + i, column_sum(dx * gap))
                scaled = dx * rate(l, i)
                total = dx if total is None else total + dx
                mixed_part = scaled if mixed_part is None else mixed_part + scaled
            shifted = (total - mixed_part) * stay[b]
            rs_start(mixed_part + rolled(shifted, span - 1), b)
            serve(5 + b)
        free(l, 1)

        each_block(
            gated, dmall, lambda n, value: dO.__setitem__((parity, n), value), HALVES
        )
        for i in range(3):
            each_block(mixes3.at[i], lefts.at[i], to_dA(i))
        pl.semaphore_wait(sib_credit.at[1], 1)
        half_copy(l, parity, A0).start()
        half_copy(l, parity, OO).start()
        serve(7)
        for b in streams:
            dn = rs_wait(b)
            hat, rstd = normed(hsave[l, b])
            add_small(0, column_sum(dn * hat))
            add_small(2, column_sum(dn))
            dh = cur[b] + norm_back(dn, parb[l, 0:1, :], hat, rstd)
            result = dh.astype(BF)
            gradb[b] = result
            cur[b] = result.astype(F32)
        for i, value in sums.items():
            sg[l, i : i + 1, my_cols if i in (9, 10) else slice(None)] = value
        for i in GROUPS:
            half_copy(l, parity, i).wait_send()
        return carry

    lax.fori_loop(0, layers, backward, 0)

    tg_args = (swap_self, gradb, tgrad, out_s.at[1], out_r.at[1], t, p)
    start_any(*tg_args)

    def sg_copy(r):
        return plane(sg.at[next_pipe(r)], sgr.at[r - 1], sg_s.at[r - 1], sg_r.at[r - 1], r)

    lanes = sg8.shape[-1]

    def sg_cols(rank, half):
        return pl.ds(pl.multiple_of(lanes * (rank * HALVES + half), lanes), lanes)

    def sg8_copy(a, b):
        rank, half = next_rank(a), (c + b) % HALVES
        n = a * HALVES + b
        return remote(
            sgt.at[:, sg_cols(rank, half)], sg8.at[n], sg8_s.at[n], sg8_r.at[n], p, rank, half
        )

    others = [(a, b) for a in range(RANKS) for b in range(HALVES) if a or b]
    for r in range(1, RANKS):
        sg_copy(r).start()
    for l in range(layers):

        @pl.when(l == p)
        def _():
            for i in PIECES:
                for way in range(2):
                    if not late(layers - 1 - l, i, way):
                        hand_out(i, way)

    end = SERVICES * layers
    for time in range(end, 1 + max(slots[-1] for _, _, _, slots in BACK)):
        serve_back(time)
        if time == end + 1:
            for r in range(1, RANKS):
                sg_copy(r).wait()
            total = sg[p]
            for r in range(1, RANKS):
                total = total + sgr[r - 1]
            sgt[...] = total
            for a, b in others:
                sg8_copy(a, b).start()
    total = sgt[:, sg_cols(t, c)]
    for a, b in others:
        sg8_copy(a, b).wait()
        total = total + sg8[a * HALVES + b]
    small[...] = total

    for l in range(layers):
        sent_any(*fin_args(l))
    for r in range(1, RANKS):
        par_copy(r).wait_send()
    carried_sent()
    sent_any(swap_self, mixb, mixed, out_s.at[0], out_r.at[0], t, p)
    got_any(swap_self, mixed, out_r.at[0])
    sent_any(*tg_args)
    got_any(swap_self, tgrad, out_r.at[1])
    for l in range(2):
        all_sent(l, (layers - 1 - l) % 2, PIECES)
    for i in PIECES:
        for way in range(2):
            if i in (V0, V1, OO):
                home_own(i, way).wait()
            else:
                for args in home_args(i, way):
                    if args[-1]:
                        home_copy(*args).wait_send()
                    else:
                        home_copy(*args).wait()
    for src in range(RANKS):
        cols = pl.ds(src * quarter, quarter)
        got_any(jnp.logical_and(swap_self, t == src), finout.at[:, :, cols], fin_r.at[src])
        if src:
            for m, grad in enumerate((gk, gv, gr, gfr)):
                got(grad.at[:, cols], r1_r.at[m, src])
            got(gfk.at[:, pl.ds(src * hidden, hidden)], r1_r.at[4, src])


def on_device(
    outer,
    tokens,
    cotangent,
    lengths,
    carried,
    norm_gain,
    norm_bias,
    mix_rates,
    time_decay,
    time_first,
    attention_accept_proj,
    attention_lookup_proj,
    attention_content_proj,
    attention_result_proj,
    feedforward_accept_proj,
    feedforward_lookup_proj,
    feedforward_content_proj,
):
    layers = lax.axis_size("pipe")
    micro, chunk, width = tokens.shape
    row_count = chunk * RANKS
    rows = micro * row_count
    per = lengths.shape[1]
    seqs = micro * per
    weights = [
        attention_lookup_proj[0],
        attention_content_proj[0],
        attention_accept_proj[0],
        feedforward_accept_proj[0],
        attention_result_proj[0],
        feedforward_lookup_proj[0],
        feedforward_content_proj[0],
    ]
    near = [[b * outer + i for i in range(outer)] for b in range(RANKS * HALVES)]
    if outer > 1:
        weights = [
            lax.all_gather(w, "dp", axis=0, tiled=True, axis_index_groups=near) for w in weights
        ]
    block = width // (RANKS * HALVES)
    hidden = weights[5].shape[1] // RANKS
    quarter = width // RANKS
    vmem = pl.BlockSpec(memory_space=pltpu.VMEM)
    smem = pl.BlockSpec(memory_space=pltpu.SMEM)
    hbm = pl.BlockSpec(memory_space=pl.ANY)
    dma = pltpu.SemaphoreType.DMA
    regular = pltpu.SemaphoreType.REGULAR
    n_peers = RANKS - 1
    own = (micro, chunk, width)
    full = (micro, row_count, width)

    def stores(count):
        return [
            pltpu.VMEM((count, RANKS, HALVES, block, width), BF),
            pltpu.VMEM((count, HALVES, block, width), BF),
            pltpu.VMEM((count, RANKS, HALVES, block, hidden), BF),
            pltpu.VMEM((count, HALVES, hidden // HALVES, width), BF),
        ]

    outs = pl.pallas_call(
        partial(layers_kernel, outer, row_count // 2),
        out_shape=(
            jax.ShapeDtypeStruct(own, BF),
            jax.ShapeDtypeStruct(own, BF),
            jax.ShapeDtypeStruct((5, seqs, width), F32),
            jax.ShapeDtypeStruct((16, block), F32),
        )
        + tuple(jax.ShapeDtypeStruct(w.shape, BF) for w in weights),
        in_specs=[vmem] * 2 + [smem] + [vmem] * 6 + [hbm] * 7,
        out_specs=(vmem,) * 4 + (hbm,) * 7,
        scratch_shapes=stores(layers)
        + stores(2)
        + [
            pltpu.VMEM(own, BF),
            pltpu.VMEM(own, BF),
            pltpu.VMEM((16, 128), F32),
            pltpu.VMEM((16, 128), F32),
            pltpu.VMEM((32, width), BF),
            pltpu.VMEM((layers, 32, quarter), BF),
            pltpu.VMEM((16, width), BF),
            pltpu.VMEM((layers, 16, width), BF),
            pltpu.VMEM((16, width), F32),
            pltpu.VMEM((layers, 16, width), F32),
            pltpu.VMEM((layers,) + full, BF),
            pltpu.VMEM((layers,) + full, BF),
            pltpu.VMEM((layers,) + own, F32),
            pltpu.VMEM((layers,) + own, F32),
            pltpu.VMEM((layers,) + own, F32),
            pltpu.VMEM((layers,) + own, F32),
            pltpu.VMEM((layers, micro, row_count, hidden), BF),
            pltpu.VMEM((layers, micro, row_count, quarter), F32),
            pltpu.VMEM((layers, micro, row_count, quarter), F32),
            pltpu.VMEM((layers, 7, micro, row_count, quarter), BF),
            pltpu.VMEM(full, BF),
            pltpu.VMEM((micro, n_peers, chunk, width), BF),
            pltpu.VMEM((micro, row_count, quarter), BF),
            pltpu.VMEM(own, BF),
            pltpu.VMEM(own, F32),
            pltpu.VMEM((layers, 5, seqs, quarter), F32),
            pltpu.VMEM(own, BF),
            pltpu.VMEM(own, BF),
            pltpu.VMEM(full, BF),
            pltpu.VMEM(full, BF),
            pltpu.VMEM(own, BF),
            pltpu.VMEM((micro, row_count, quarter), BF),
            pltpu.VMEM(full, BF),
            pltpu.VMEM(full, BF),
            pltpu.VMEM((micro, row_count, hidden), BF),
            pltpu.VMEM((micro, row_count, hidden), BF),
            pltpu.VMEM((3,) + full, BF),
            pltpu.VMEM((3, micro, row_count, quarter), BF),
            pltpu.VMEM((micro, row_count, quarter), BF),
            pltpu.VMEM((layers, 16, width), F32),
            pltpu.VMEM((n_peers, 16, width), F32),
            pltpu.VMEM((16, width), F32),
            pltpu.VMEM((RANKS * HALVES, 16, block), F32),
            dma((3,)),
            dma((3,)),
            dma((RANKS,)),
            dma((layers,)),
            dma((RANKS,)),
            dma((layers,)),
            dma((n_peers,)),
            dma((layers,)),
            dma((5, n_peers)),
            dma((5, n_peers)),
            dma((7,)),
            dma((layers, 7, 2)),
            dma((layers, 7, 2)),
            dma((layers, 4)),
            dma((layers, 4)),
            dma((micro, n_peers)),
            dma((micro, n_peers)),
            dma((micro, n_peers)),
            dma((micro, n_peers)),
            dma((micro, n_peers)),
            dma((micro, n_peers)),
            dma((micro, n_peers)),
            dma((micro, n_peers)),
            dma((layers,)),
            dma((RANKS,)),
            dma((2,)),
            dma((2,)),
            dma((layers, 4)),
            dma((layers, 4)),
            dma((layers, 7, 2)),
            dma((layers, 7, 2)),
            dma((5, RANKS)),
            dma((5, RANKS)),
            dma((6,)),
            dma((n_peers,)),
            dma((n_peers,)),
            dma((RANKS * HALVES,)),
            dma((RANKS * HALVES,)),
            regular((layers, 2, 2)),
            regular((2,)),
        ],
        compiler_params=pltpu.CompilerParams(
            collective_id=0, has_side_effects=True, vmem_limit_bytes=60 * 2**20
        ),
        name="layers",
    )(
        tokens,
        cotangent,
        lengths,
        carried.transpose(0, 1, 3, 2, 4),
        norm_gain,
        norm_bias,
        mix_rates.transpose(1, 0, 2),
        time_decay,
        time_first,
        *weights,
    )
    mixed, tgrad, fin, small, *grads = outs
    if outer > 1:
        grads = [
            lax.psum_scatter(g, "dp", scatter_dimension=0, tiled=True, axis_index_groups=near)
            for g in grads
        ]
        small = lax.psum_scatter(
            small, "dp", scatter_dimension=1, tiled=True, axis_index_groups=near
        )
    gk, gv, gr, gfr, go, gfk, gfv = [g.astype(F32)[None] for g in grads]
    small = small[None]
    return (
        mixed,
        tgrad.astype(F32),
        fin.transpose(1, 0, 2).reshape(micro, per, 1, 5, width),
        small[:, 0:2],
        small[:, 2:4],
        small[:, 4:9],
        small[:, 9],
        small[:, 10],
        gr,
        gk,
        gv,
        go,
        gfr,
        gfk,
        gfv,
    )


def solution(mesh):
    outer = mesh.shape["dp"] // (RANKS * HALVES)
    placed = (
        P("dp", "pipe", None),
        P("dp", "pipe", None),
        P("dp", None),
        P("dp", None, "pipe", None, None),
        P("pipe", None, None),
        P("pipe", None, None),
        P("pipe", None, None),
        P("pipe", None),
        P("pipe", None),
    ) + (P("pipe", "dp", None),) * 7
    return jax.shard_map(
        partial(on_device, outer),
        mesh=mesh,
        in_specs=placed,
        out_specs=(
            P("dp", "pipe", None),
            P("dp", "pipe", None),
            P("dp", None, "pipe", None, None),
            P("pipe", None, "dp"),
            P("pipe", None, "dp"),
            P("pipe", None, "dp"),
            P("pipe", "dp"),
            P("pipe", "dp"),
        )
        + (P("pipe", "dp", None),) * 7,
        check_vma=False,
    )
```

```python
from functools import partial

import jax
import jax.numpy as jnp
from jax import lax
from jax.sharding import PartitionSpec as P
from jax.experimental import pallas as pl
from jax.experimental.pallas import tpu as pltpu

EPS = 1e-05
BF = jnp.bfloat16
F32 = jnp.float32
HIGH = lax.Precision.HIGHEST
MESH = pl.DeviceIdType.MESH
RANKS = 4
HALVES = 2


def dot(a, b, precision=None):
    return jnp.dot(a, b, precision=precision, preferred_element_type=F32)


def dot_nt(a, b):
    return lax.dot_general(a, b, (((1,), (1,)), ((), ())), preferred_element_type=F32)


def dot_tn(a, b):
    return lax.dot_general(a, b, (((0,), (0,)), ((), ())), preferred_element_type=F32)


def rolled(x, shift):
    return pltpu.roll(x, shift % x.shape[0], 0)


def normed(h):
    center = h - jnp.mean(h, axis=-1, keepdims=True)
    spread = jnp.mean(center * center, axis=-1, keepdims=True)
    rstd = lax.rsqrt(spread + EPS)
    return center * rstd, rstd


def norm_back(dn, gain, hat, rstd):
    dh = dn * gain
    return rstd * (
        dh
        - jnp.mean(dh, axis=-1, keepdims=True)
        - hat * jnp.mean(dh * hat, axis=-1, keepdims=True)
    )


def column_sum(x):
    return jnp.sum(x, axis=0, keepdims=True)


def ring_place(pipe):
    return pipe + (pipe // 2) * (5 - 2 * pipe)


A0, A1, V0, V1, K0, K1, OO = range(7)
FORTH = (
    (0, A0, 0, (-8, -3, -1, 0)),
    (0, A0, 1, (-8, -3, -1, 0)),
    (0, A1, 0, (-6, -2, 0, 1)),
    (0, A1, 1, (-6, -3, 0, 1)),
    (0, V0, 0, (-6, -2, 1, 4)),
    (0, V0, 1, (-9, -6, -3, 1)),
    (0, V1, 0, (-1, 0, 2, 3)),
    (0, V1, 1, (-9, -2, 1, 3)),
    (0, K0, 0, (-5, 0, 3, 5)),
    (0, K0, 1, (-5, 0, 3, 4)),
    (0, K1, 0, (0, 1, 4, 5)),
    (0, K1, 1, (0, 1, 4, 5)),
    (0, OO, 0, (-12, -6, -3, -2)),
    (0, OO, 1, (-12, -4, -3, -2)),
    (1, A0, 0, (-10, -5, -4, 3)),
    (1, A0, 1, (-10, -2, -1, 3)),
    (1, A1, 0, (-6, -2, 2, 7)),
    (1, A1, 1, (-3, 3, 5, 8)),
    (1, V0, 0, (2, 5, 7, 13)),
    (1, V0, 1, (-4, -1, 1, 7)),
    (1, V1, 0, (-8, -5, 2, 9)),
    (1, V1, 1, (-3, 0, 6, 12)),
    (1, K0, 0, (3, 7, 9, 13)),
    (1, K0, 1, (1, 4, 9, 12)),
    (1, K1, 0, (2, 6, 8, 12)),
    (1, K1, 1, (4, 6, 7, 11)),
    (1, OO, 0, (-8, -4, -1, 6)),
    (1, OO, 1, (-9, 3, 5, 8)),
    (2, A0, 0, (-7, 2, 3, 10)),
    (2, A0, 1, (-7, 2, 5, 12)),
    (2, A1, 0, (-1, 8, 13, 16)),
    (2, A1, 1, (1, 6, 10, 15)),
    (2, V0, 0, (-8, 12, 14, 20)),
    (2, V0, 1, (14, 16, 19, 21)),
    (2, V1, 0, (-3, 6, 9, 19)),
    (2, V1, 1, (-10, 5, 7, 12)),
    (2, K0, 0, (-3, 4, 8, 14)),
    (2, K0, 1, (12, 15, 18, 21)),
    (2, K1, 0, (-1, 17, 18, 20)),
    (2, K1, 1, (9, 13, 16, 19)),
    (2, OO, 0, (-10, 3, 8, 16)),
    (2, OO, 1, (-10, 4, 9, 14)),
    (3, A0, 0, (-6, 3, 9, 20)),
    (3, A0, 1, (-6, 3, 9, 20)),
    (3, A1, 0, (12, 14, 20, 23)),
    (3, A1, 1, (10, 13, 21, 24)),
    (3, V0, 0, (9, 12, 18, 20)),
    (3, V0, 1, (-9, -2, 12, 16)),
    (3, V1, 0, (15, 19, 21, 27)),
    (3, V1, 1, (-10, -4, 7, 21)),
    (3, K0, 0, (12, 16, 18, 28)),
    (3, K0, 1, (6, 12, 19, 24)),
    (3, K1, 0, (10, 16, 23, 28)),
    (3, K1, 1, (8, 14, 17, 27)),
    (3, OO, 0, (-9, 1, 11, 16)),
    (3, OO, 1, (-9, 1, 10, 15)),
)
BACK = (
    (0, A0, 0, (8, 10, 17, 20)),
    (0, A0, 1, (8, 9, 11, 18)),
    (0, A1, 0, (10, 13, 19, 20)),
    (0, A1, 1, (12, 16, 17, 20)),
    (0, V0, 0, (4, 7, 9, 15)),
    (0, V0, 1, (6, 8, 10, 17)),
    (0, V1, 0, (9, 12, 15, 18)),
    (0, V1, 1, (4, 6, 8, 13)),
    (0, K0, 0, (7, 8, 13, 17)),
    (0, K0, 1, (5, 7, 9, 17)),
    (0, K1, 0, (5, 7, 10, 13)),
    (0, K1, 1, (10, 11, 13, 17)),
    (0, OO, 0, (8, 11, 17, 19)),
    (0, OO, 1, (8, 10, 12, 17)),
    (1, A0, 0, (17, 20, 24, 28)),
    (1, A0, 1, (21, 22, 25, 28)),
    (1, A1, 0, (18, 19, 25, 28)),
    (1, A1, 1, (16, 19, 22, 26)),
    (1, V0, 0, (12, 13, 15, 19)),
    (1, V0, 1, (13, 15, 18, 21)),
    (1, V1, 0, (14, 15, 17, 24)),
    (1, V1, 1, (13, 16, 19, 26)),
    (1, K0, 0, (13, 14, 16, 26)),
    (1, K0, 1, (17, 20, 23, 26)),
    (1, K1, 0, (15, 16, 18, 24)),
    (1, K1, 1, (12, 14, 17, 19)),
    (1, OO, 0, (21, 22, 24, 27)),
    (1, OO, 1, (16, 21, 24, 27)),
    (2, A0, 0, (38, 39, 40, 41)),
    (2, A0, 1, (26, 30, 33, 35)),
    (2, A1, 0, (25, 32, 33, 38)),
    (2, A1, 1, (27, 32, 34, 37)),
    (2, V0, 0, (20, 23, 26, 35)),
    (2, V0, 1, (21, 25, 27, 37)),
    (2, V1, 0, (20, 24, 26, 37)),
    (2, V1, 1, (35, 38, 39, 41)),
    (2, K0, 0, (34, 39, 40, 41)),
    (2, K0, 1, (20, 23, 28, 33)),
    (2, K1, 0, (22, 26, 28, 39)),
    (2, K1, 1, (25, 29, 31, 37)),
    (2, OO, 0, (31, 33, 38, 39)),
    (2, OO, 1, (32, 34, 38, 39)),
    (3, A0, 0, (38, 39, 40, 41)),
    (3, A0, 1, (34, 37, 38, 40)),
    (3, A1, 0, (32, 36, 37, 39)),
    (3, A1, 1, (34, 38, 39, 40)),
    (3, V0, 0, (32, 37, 38, 40)),
    (3, V0, 1, (33, 37, 38, 40)),
    (3, V1, 0, (29, 32, 35, 40)),
    (3, V1, 1, (34, 38, 39, 41)),
    (3, K0, 0, (32, 37, 38, 39)),
    (3, K0, 1, (29, 32, 34, 37)),
    (3, K1, 0, (28, 30, 32, 33)),
    (3, K1, 1, (28, 31, 32, 35)),
    (3, OO, 0, (36, 38, 39, 41)),
    (3, OO, 1, (34, 38, 39, 41)),
)
PIECES = range(7)
SERVICES = 8
ROWS_FROM = {(A0, 0): 0, (A1, 0): 1, (A0, 1): 3, (A1, 1): 2, (K0, 0): 0, (K1, 0): 1, (K0, 1): 3, (K1, 1): 2}
GROUPS = (A0, V0, K0, OO)


def layers_kernel(
    outer,
    longest,
    tok,
    cot,
    lens,
    held,
    gain,
    bias,
    mixes,
    decay,
    first,
    wk,
    wv,
    wr,
    wfr,
    wo,
    wfk,
    wfv,
    mixed,
    tgrad,
    finout,
    small,
    gk,
    gv,
    gr,
    gfr,
    go,
    gfk,
    gfv,
    wA,
    wO,
    wK,
    wV,
    dA,
    dO,
    dK,
    dV,
    tokb,
    cotb,
    info,
    infob,
    stsrc,
    stb,
    shsrc,
    shb,
    par,
    parb,
    nsave,
    n2save,
    hsave,
    msave,
    kvsave,
    gatesave,
    zsave,
    alsave,
    besave,
    smsave,
    part,
    rbuf,
    r2st,
    r2full,
    cur,
    finb,
    mixb,
    gradb,
    dkvall,
    dmall,
    dr2o,
    dr2c,
    mixk,
    mixr,
    squares,
    dzs,
    mixes3,
    lefts,
    gated,
    sg,
    sgr,
    sgt,
    sg8,
    x_s,
    x_r,
    st_s,
    st_r,
    sh_s,
    sh_r,
    par_s,
    par_r,
    w1_s,
    w1_r,
    w1_l,
    rw_s,
    rw_r,
    w3_s,
    w3_r,
    ag_s,
    ag_r,
    rs_s,
    rs_r,
    a2_s,
    a2_r,
    a2b_s,
    a2b_r,
    fin_s,
    fin_r,
    out_s,
    out_r,
    a_s,
    a_r,
    rd_s,
    rd_r,
    r1_s,
    r1_r,
    r1_l,
    sg_s,
    sg_r,
    sg8_s,
    sg8_r,
    credit,
    sib_credit,
):
    p = lax.axis_index("pipe")
    d = lax.axis_index("dp")
    t = d // (HALVES * outer)
    c = (d // outer) % HALVES
    o = d % outer
    ring = ring_place(p)
    micro, chunk, width = tok.shape
    layers = stb.shape[0]
    rows = micro * chunk * RANKS
    quarter = width // RANKS
    mine = pl.ds(pl.multiple_of(chunk * t, chunk), chunk)
    my_cols = pl.ds(pl.multiple_of(quarter * t, quarter), quarter)
    hidden = wfk.shape[1] // RANKS
    my_hidden = pl.ds(pl.multiple_of(hidden * t, hidden), hidden)
    block = wk.shape[0]
    seqs = held.shape[0] * held.shape[1]
    per = held.shape[1]

    def place(rank, half):
        return (rank * HALVES + half) * outer + o

    def next_rank(r):
        return (t + r) % RANKS

    def next_pipe(r):
        return (p + r) % RANKS

    def on_ring(r):
        return ring_place((ring + r) % RANKS)

    def remote(src, dst, ss, rs, pipe, rank, half):
        return pltpu.make_async_remote_copy(
            src_ref=src,
            dst_ref=dst,
            send_sem=ss,
            recv_sem=rs,
            device_id=(pipe, place(rank, half)),
            device_id_type=MESH,
        )

    def peer(src, dst, ss, rs, r):
        return remote(src, dst, ss, rs, p, next_rank(r), c)

    def plane(src, dst, ss, rs, r):
        return remote(src, dst, ss, rs, next_pipe(r), t, c)

    def sibling(src, dst, ss, rs):
        return remote(src, dst, ss, rs, p, t, 1 - c)

    def start_any(is_self, src, dst, ss, rs, pipe, rank):
        @pl.when(is_self)
        def _():
            pltpu.make_async_copy(src, dst, ss).start()

        @pl.when(jnp.logical_not(is_self))
        def _():
            remote(src, dst, ss, rs, pipe, rank, c).start()

    def sent_any(is_self, src, dst, ss, rs, pipe, rank):
        @pl.when(is_self)
        def _():
            pltpu.make_async_copy(src, dst, ss).wait()

        @pl.when(jnp.logical_not(is_self))
        def _():
            remote(src, dst, ss, rs, pipe, rank, c).wait_send()

    def got(dst, rs):
        remote(dst, dst, rs, rs, next_pipe(1), t, c).wait_recv()

    def got_any(is_self, dst, rs):
        @pl.when(jnp.logical_not(is_self))
        def _():
            got(dst, rs)

    barrier = pltpu.get_barrier_semaphore()
    for a in range(RANKS):
        for b in range(RANKS):
            if a or b:
                pl.semaphore_signal(
                    barrier,
                    inc=1,
                    device_id=(next_pipe(a), place(next_rank(b), c)),
                    device_id_type=MESH,
                )
    for b in range(RANKS):
        pl.semaphore_signal(
            barrier, inc=1, device_id=(p, place(next_rank(b), 1 - c)), device_id_type=MESH
        )
    pl.semaphore_wait(barrier, RANKS * RANKS - 1 + RANKS)

    raw = (wk, wv, wr, wfr)

    def w1(m, r):
        rank = next_rank(r)
        if m < 4:
            cols = pl.ds(pl.multiple_of(quarter * rank, quarter), quarter)
            return peer(
                raw[m].at[:, cols],
                wA.at[p, t, c, :, pl.ds(m * quarter, quarter)],
                w1_s.at[m, r - 1],
                w1_r.at[m, r - 1],
                r,
            )
        cols = pl.ds(pl.multiple_of(hidden * rank, hidden), hidden)
        return peer(wfk.at[:, cols], wK.at[p, t, c], w1_s.at[m, r - 1], w1_r.at[m, r - 1], r)

    def w1_own(m):
        if m < 4:
            return pltpu.make_async_copy(
                raw[m].at[:, my_cols], wA.at[p, t, c, :, pl.ds(m * quarter, quarter)], w1_l.at[m]
            )
        if m == 4:
            return pltpu.make_async_copy(wfk.at[:, my_hidden], wK.at[p, t, c], w1_l.at[m])
        if m == 5:
            return pltpu.make_async_copy(wo, wO.at[p, c], w1_l.at[m])
        return pltpu.make_async_copy(wfv, wV.at[p, c], w1_l.at[m])

    for m in range(7):
        w1_own(m).start()
    for group_m in ((0, 1, 2, 3), (4,)):
        for r in (1, 3, 2):
            for m in group_m:
                w1(m, r).start()

    lane = lax.broadcasted_iota(jnp.int32, info.shape, 1)
    line = lax.broadcasted_iota(jnp.int32, info.shape, 0)
    marks = jnp.full(info.shape, -1, jnp.int32)
    for b in range(micro):
        at = b * (rows // micro)
        for s in range(per):
            index = b * per + s
            marks = jnp.where(jnp.logical_and(line == 0, lane == index), at, marks)
            at = at + lens[b, s]
            marks = jnp.where(line == 8 + index, at - 1, marks)
    info[...] = marks.astype(F32)

    swap_self = p == t
    swaps = [(tok, tokb), (info, infob), (cot, cotb)]
    for i, (src, dst) in enumerate(swaps):
        start_any(swap_self, src, dst, x_s.at[i], x_r.at[i], t, p)

    par[0:2, :] = gain[0]
    par[2:4, :] = bias[0]
    for i in range(mixes.shape[0]):
        par[4 + i : 5 + i, :] = mixes[i]
    par[9:10, :] = decay[...]
    par[10:11, :] = first[...]
    par[11:16, :] = jnp.zeros((5, width), F32)

    def par_copy(r):
        return plane(par, parb.at[p], par_s.at[r - 1], par_r.at[p], r)

    for r in range(1, RANKS):
        par_copy(r).start()
    parb[p] = par[...]

    carried_rows = [
        jnp.concatenate([held[b, s, i] for b in range(micro) for s in range(per)], axis=0)
        for i in range(5)
    ]
    spare = jnp.zeros((8, width), F32)
    stsrc[...] = jnp.concatenate(carried_rows[0:3] + [spare], axis=0).astype(BF)
    shsrc[...] = jnp.concatenate(carried_rows[3:5], axis=0).astype(BF)

    def state_args(rank):
        return (
            jnp.logical_and(swap_self, rank == t),
            stsrc.at[:, pl.ds(quarter * rank, quarter)],
            stb.at[p],
            st_s.at[rank],
            st_r.at[p],
            t,
            rank,
        )

    def shift_args(rank):
        return (
            jnp.logical_and(swap_self, rank == t),
            shsrc,
            shb.at[p],
            sh_s.at[rank],
            sh_r.at[p],
            t,
            rank,
        )

    def send_carried(l):
        @pl.when(p == l)
        def _():
            for rank in range(RANKS):
                start_any(*shift_args(rank))
                start_any(*state_args(rank))

    def get_carried(l):
        from_self = jnp.logical_and(swap_self, p == l)

        @pl.when(from_self)
        def _():
            for rank in range(RANKS):

                @pl.when(rank == t)
                def _():
                    pltpu.make_async_copy(*shift_args(rank)[1:4]).wait()
                    pltpu.make_async_copy(*state_args(rank)[1:4]).wait()

        got_any(from_self, shb.at[l], sh_r.at[l])
        got_any(from_self, stb.at[l], st_r.at[l])
        got_any(p == l, parb.at[l], par_r.at[l])

    def carried_sent():
        for rank in range(RANKS):

            @pl.when(jnp.logical_not(jnp.logical_and(swap_self, rank == t)))
            def _():
                remote(*shift_args(rank)[1:], c).wait_send()
                remote(*state_args(rank)[1:], c).wait_send()

    def piece(store, at, i, way, half):
        a, small_one, k, v = store
        if i in (A0, A1, K0, K1):
            return (a if i in (A0, A1) else k).at[at, next_rank(ROWS_FROM[i, way]), half]
        size = (small_one if i == OO else v).shape[2] // 2
        if i == OO:
            return small_one.at[at, half, pl.ds(way * size, size)]
        return v.at[at, half, pl.ds(way * size + (i - V0) * (size // 2), size // 2)]

    def group(store, at, i, half):
        a, small_one, k, v = store
        if i == A0:
            return a.at[at, :, half]
        if i == K0:
            return k.at[at, :, half]
        return small_one.at[at, half] if i == OO else v.at[at, half]

    def group_of(i):
        return GROUPS.index({A1: A0, V1: V0, K1: K0}.get(i, i))

    weights = (wA, wO, wK, wV)
    grads = (dA, dO, dK, dV)

    def steps_from(l, way):
        home = ring_place(l)
        return (ring - home + RANKS) % RANKS if way == 0 else (home - ring + RANKS) % RANKS

    def forth_copy(l, i, way):
        return remote(
            piece(weights, l, i, way, c),
            piece(weights, l, i, way, c),
            rw_s.at[l, i, way],
            rw_r.at[l, i, way],
            on_ring(1 if way == 0 else RANKS - 1),
            t,
            c,
        )

    def pair_copy(l, i, way):
        g = group_of(i)
        return sibling(
            piece(weights, l, i, way, c),
            piece(weights, l, i, way, c),
            w3_s.at[l, g],
            w3_r.at[l, g],
        )

    def bring(l, i, way, hop):
        @pl.when(steps_from(l, way) == hop)
        def _():
            if hop:
                forth_copy(l, i, way).wait_recv()
            else:
                rows_in(i, way)
            if hop < RANKS - 1:
                forth_copy(l, i, way).start()
            pair_copy(l, i, way).start()

    def rows_in(i, way):
        if i == OO:
            return None
        if i in (V0, V1):
            return None
        for m in range(4) if i in (A0, A1) else (4,):
            if ROWS_FROM[i, way]:
                w1(m, RANKS - ROWS_FROM[i, way]).wait_recv()
            else:
                w1_own(m).wait()

    def due(plan, time):
        for l, i, way, slots in plan:
            for hop, slot in enumerate(slots):
                if slot == time:
                    yield l, i, way, hop

    def serve_forth(time):
        for l, i, way, hop in due(FORTH, time):
            bring(l, i, way, hop)

    def weights_here(l, i):
        ref = group(weights, l, i, 1 - c)
        sem = w3_r.at[l, group_of(i)]
        sibling(ref, ref, sem, sem).wait_recv()

    send_carried(0)
    w1_own(5).wait()
    w1_own(6).wait()
    for time in range(min(slots[0] for _, _, _, slots in FORTH), 0):
        serve_forth(time)

    for i in range(2):
        src, dst = swaps[i]
        sent_any(swap_self, src, dst, x_s.at[i], x_r.at[i], t, p)
        got_any(swap_self, dst, x_r.at[i])

    streams = range(micro)
    span = rows // micro

    def ag(buf, r, b):
        return peer(buf.at[b, mine], buf.at[b, mine], ag_s.at[b, r - 1], ag_r.at[b, r - 1], r)

    def ag_start(buf, b):
        for r in range(1, RANKS):
            ag(buf, r, b).start()

    def ag_wait(buf, b):
        for r in range(1, RANKS):
            ag(buf, r, b).wait()

    def rs(r, b):
        theirs = pl.ds(pl.multiple_of(chunk * next_rank(r), chunk), chunk)
        return peer(
            part.at[b, theirs], rbuf.at[b, r - 1], rs_s.at[b, r - 1], rs_r.at[b, r - 1], r
        )

    def rs_start(values, b):
        part[b] = values.astype(BF)
        for r in range(1, RANKS):
            rs(r, b).start()

    def rs_wait(b):
        for r in range(1, RANKS):
            rs(r, b).wait()
        total = part[b, mine, :].astype(F32)
        for r in range(1, RANKS):
            total = total + rbuf[b, r - 1].astype(F32)
        return total

    cur[...] = tokb[...].astype(F32)

    starts = infob[0:1, 0:seqs]
    ends = infob[8 : 8 + seqs, 0:span]
    line = lax.broadcasted_iota(jnp.int32, (span, seqs), 0).astype(F32)
    lane = lax.broadcasted_iota(jnp.int32, (seqs, span), 1).astype(F32)
    none = jnp.zeros((span, seqs), F32)
    hot, onset, stay, hots, place_in, last_hot = [], [], [], [], [], []
    for b in streams:
        at = line + b * span
        hot.append((at == starts).astype(F32))
        onset.append(jnp.sum(hot[b], axis=1, keepdims=True))
        stay.append(1.0 - onset[b])
        hots.append(
            [jnp.concatenate(pair, axis=1).astype(BF) for pair in ((hot[b], none), (none, hot[b]))]
        )
        begun = jnp.max(jnp.where(starts <= at, starts, 0.0), axis=1, keepdims=True)
        place_in.append(at[:, 0:1] - begun)
        last_hot.append((lane + b * span == ends).astype(F32))
    reaches = []
    reach = 1
    while reach < longest:
        reaches.append(reach)
        reach *= 2

    def whole(ref):
        return ref[...].reshape(rows, ref.shape[-1])

    def before(n, l, which, b):
        return rolled(n, 1) * stay[b] + dot(hots[b][which], shb[l])

    def rate(l, i):
        return parb[l, 4 + i : 5 + i, :]

    def fin_args(l):
        return (
            jnp.logical_and(l == p, swap_self),
            finb.at[l],
            finout.at[:, :, my_cols],
            fin_s.at[l],
            fin_r.at[t],
            l,
            p,
        )

    def forward(l, carry):
        def serve(k):
            if k == 0:

                @pl.when(l + 1 < layers)
                def _():
                    send_carried(l + 1)

            for at in range(layers):

                @pl.when(l == at)
                def _():
                    serve_forth(SERVICES * at + k)

        get_carried(l)
        for b in streams:
            h = cur[b]
            hsave[l, b] = h
            hat, _ = normed(h)
            n = hat * parb[l, 0:1, :] + parb[l, 2:3, :]
            nsave[l, b, mine, :] = n.astype(BF)
            ag_start(nsave.at[l], b)
        serve(0)
        serve(1)
        w = -jnp.exp(parb[l, 9:10, my_cols])
        u = parb[l, 10:11, my_cols]
        states = stb[l].astype(F32)
        for b in streams:
            ag_wait(nsave.at[l], b)
            n = nsave[l, b].astype(F32)
            prev = before(n, l, 0, b)
            gap = n - prev
            if b == 0:
                weights_here(l, A0)
            mats = []
            for i in range(3):
                mix = (prev + gap * rate(l, i)).astype(BF)
                mats.append(
                    dot(
                        mix, wA[l, :, :, :, i * quarter : (i + 1) * quarter].reshape(width, quarter)
                    )
                )
            k, v, r = mats
            init = [dot(hot[b], states[i * seqs : (i + 1) * seqs]) for i in range(3)]
            top = jnp.where(onset[b] > 0.5, jnp.maximum(k, w + init[2]), k)
            for s in reaches:
                top = jnp.maximum(top, jnp.where(place_in[b] >= s, rolled(top, s) + s * w, -1e30))
            top_prev = rolled(top, 1) * stay[b] + init[2]
            al = jnp.exp(w + top_prev - top)
            be = jnp.exp(k - top)
            num = be * v + onset[b] * al * init[0]
            den = be + onset[b] * al * init[1]
            keep = al * stay[b]
            for i, s in enumerate(reaches):
                num = num + keep * rolled(num, s)
                den = den + keep * rolled(den, s)
                if i + 1 < len(reaches):
                    keep = keep * rolled(keep, s)
            num_prev = rolled(num, 1) * stay[b] + init[0]
            den_prev = rolled(den, 1) * stay[b] + init[1]
            now = u + k
            peak = jnp.maximum(top_prev, now)
            e1 = jnp.exp(top_prev - peak)
            e2 = jnp.exp(now - peak)
            inv = 1.0 / (e1 * den_prev + e2)
            e1 = e1 * inv
            e2 = e2 * inv
            y = e1 * num_prev + e2 * v
            sr = jax.nn.sigmoid(r)
            g = (sr * y).astype(BF)
            if b == 0:
                weights_here(l, OO)
            rs_start(dot(g, wO[l].reshape(quarter, width)), b)
            alsave[l, b] = al
            besave[l, b] = be
            for i, value in enumerate((v, y, sr, e1, e2, num_prev, den_prev)):
                smsave[l, i, b] = value.astype(BF)
            lasts = [dot(last_hot[b], value, HIGH) for value in (num, den, top)]
            lasts.append(dot(last_hot[b].astype(BF), nsave[l, b, :, my_cols]))
            ending = [x + y for x, y in zip(ending, lasts)] if b else lasts
            serve(2 + b)
        for b in streams:
            m = hsave[l, b] + rs_wait(b)
            msave[l, b] = m
            hat, _ = normed(m)
            n2 = hat * parb[l, 1:2, :] + parb[l, 3:4, :]
            n2save[l, b, mine, :] = n2.astype(BF)
            ag_start(n2save.at[l], b)
        serve(4)
        serve(5)

        def a2(r, b):
            theirs = pl.ds(pl.multiple_of(chunk * next_rank(r), chunk), chunk)
            return peer(
                r2st.at[b, theirs],
                r2full.at[b, :, my_cols],
                a2_s.at[b, r - 1],
                a2_r.at[b, r - 1],
                r,
            )

        for b in streams:
            ag_wait(n2save.at[l], b)
            n = n2save[l, b].astype(F32)
            prev = before(n, l, 1, b)
            gap = n - prev
            mix = (prev + gap * rate(l, 4)).astype(BF)
            r2st[b] = dot(mix, wA[l, :, :, :, 3 * quarter :].reshape(width, quarter)).astype(BF)
            for r in range(1, RANKS):
                a2(r, b).start()
            r2full[b, :, my_cols] = r2st[b, mine, :]
            mix = (prev + gap * rate(l, 3)).astype(BF)
            if b == 0:
                weights_here(l, K0)
            z = dot(mix, wK[l].reshape(width, hidden))
            act = jnp.maximum(z, 0.0)
            if b == 0:
                weights_here(l, V0)
            rs_start(dot((act * act).astype(BF), wV[l].reshape(hidden, width)), b)
            zsave[l, b] = z.astype(BF)
            value = dot(last_hot[b].astype(BF), n2save[l, b, :, my_cols])
            last_n2 = last_n2 + value if b else value
            serve(6 + b)
        for i, value in enumerate(ending + [last_n2]):
            finb[l, i] = value
        start_any(*fin_args(l))
        for b in streams:
            for r in range(1, RANKS):
                a2(r, b).wait()
            kv = rs_wait(b)
            gate = jax.nn.sigmoid(r2full[b].astype(F32))
            kvsave[l, b] = kv
            gatesave[l, b] = gate
            result = (msave[l, b] + gate * kv).astype(BF)
            mixb[b] = result
            cur[b] = result.astype(F32)
        return carry

    lax.fori_loop(0, layers, forward, 0)

    for m in range(5):
        for r in range(1, RANKS):
            w1(m, r).wait_send()
    for l in range(layers):
        for i in PIECES:
            for way in range(2):

                @pl.when(steps_from(l, way) < RANKS - 1)
                def _():
                    forth_copy(l, i, way).wait_send()

        for i in GROUPS:
            ref = group(weights, l, i, c)
            sem = w3_s.at[l, group_of(i)]
            sibling(ref, ref, sem, sem).wait_send()

    start_any(swap_self, mixb, mixed, out_s.at[0], out_r.at[0], t, p)
    sent_any(swap_self, cot, cotb, x_s.at[2], x_r.at[2], t, p)
    got_any(swap_self, cotb, x_r.at[2])
    cur[...] = cotb[...].astype(F32)
    sg[...] = jnp.zeros_like(sg)

    def free(l, kind):
        for way in range(2):
            pl.semaphore_signal(
                credit.at[l, kind, way],
                inc=1,
                device_id=(on_ring(1 if way == 0 else RANKS - 1), place(t, c)),
                device_id_type=MESH,
            )
        pl.semaphore_signal(
            sib_credit.at[kind], inc=1, device_id=(p, place(t, 1 - c)), device_id_type=MESH
        )

    def add_to(into, ours, theirs):
        def some(n, carry):
            part_rows = pl.ds(pl.multiple_of(n * 64, 64), 64)
            into[part_rows, :] = (
                ours[part_rows, :].astype(F32) + theirs[part_rows, :].astype(F32)
            ).astype(BF)
            return carry

        lax.fori_loop(0, ours.shape[0] // 64, some, 0)

    def half_copy(l, parity, i):
        g = group_of(i)
        return sibling(
            group(grads, parity, i, 1 - c), group(weights, l, i, c), a_s.at[l, g], a_r.at[l, g]
        )

    def half_sum(l, parity, i):
        half_copy(l, parity, i).wait_recv()
        for j in PIECES:
            if GROUPS[group_of(j)] == i:
                for way in range(2):
                    ours = piece(grads, parity, j, way, c)
                    add_to(ours, ours, piece(weights, l, j, way, 1 - c))

    def back_copy(l, parity, i, way):
        return remote(
            piece(grads, parity, i, way, c),
            piece(weights, l, i, way, c),
            rd_s.at[l, i, way],
            rd_r.at[l, i, way],
            on_ring(RANKS - 1 if way == 0 else 1),
            t,
            c,
        )

    def home_args(i, way):
        ours = piece(weights, p, i, way, c)
        r = ROWS_FROM[i, way]
        if i in (A0, A1):
            return [
                (ours.at[:, pl.ds(m * quarter, quarter)], grad.at[:, my_cols], m, r)
                for m, grad in enumerate((gk, gv, gr, gfr))
            ]
        return [(ours, gfk.at[:, my_hidden], 4, r)]

    def home_copy(src, dst, m, r):
        if r:
            return peer(src, dst, r1_s.at[m, r], r1_r.at[m, r], r)
        return pltpu.make_async_copy(src, dst, r1_s.at[m, 0])

    def home_own(i, way):
        ours = piece(weights, p, i, way, c)
        size = ours.shape[0]
        if i == OO:
            return pltpu.make_async_copy(ours, go.at[pl.ds(way * size, size)], r1_l.at[4 + way])
        n = 2 * way + i - V0
        return pltpu.make_async_copy(ours, gfv.at[pl.ds(n * size, size)], r1_l.at[n])

    def hand_out(i, way):
        if i in (V0, V1, OO):
            home_own(i, way).start()
        else:
            for args in home_args(i, way):
                home_copy(*args).start()

    kinds = ((V0, V1, K0, K1), (A0, A1, OO))

    def opens(step, i, way, hop):
        kind = kinds[0] if i in kinds[0] else kinds[1]
        return i == min(
            (slots[hop], n, j)
            for n, (at, j, to, slots) in enumerate(BACK)
            if at == step and to == way and j in kind
        )[2]

    def collect(step, i, way, hop):
        l, parity = layers - 1 - step, step % 2

        @pl.when(steps_from(l, way) == RANKS - 1 - hop)
        def _():
            if opens(step, i, way, hop):
                pl.semaphore_wait(credit.at[l, int(i in kinds[1]), way], 1)
            ours = piece(grads, parity, i, way, c)
            theirs = piece(weights, l, i, way, c)
            if hop:
                back_copy(l, parity, i, way).wait_recv()
                add_to(theirs if hop == RANKS - 1 else ours, ours, theirs)
            if hop < RANKS - 1:
                back_copy(l, parity, i, way).start()
            elif late(step, i, way):
                hand_out(i, way)

    def late(step, i, way):
        return any(
            (at, j, to) == (step, i, way) and slots[-1] >= SERVICES * layers
            for at, j, to, slots in BACK
        )

    def serve_back(time):
        for at in range(layers):
            for i, when in ((V0, RANKS), (K0, RANKS), (A0, SERVICES), (OO, SERVICES)):
                if time == SERVICES * at + when:
                    half_sum(layers - 1 - at, at % 2, i)
        for step, i, way, hop in due(BACK, time):
            collect(step, i, way, hop)

    def all_sent(l, parity, pieces):
        for i in pieces:
            for way in range(2):

                @pl.when(steps_from(l, way) != 0)
                def _():
                    back_copy(l, parity, i, way).wait_send()

    def each_block(left_ref, right_ref, store, count=HALVES * RANKS):
        def body(n, carry):
            cols = pl.ds(pl.multiple_of(n * block, block), block)
            left = left_ref[:, :, cols].reshape(rows, block)
            store(n, dot_tn(left, whole(right_ref)).astype(BF))
            return carry

        lax.fori_loop(0, count, body, 0, unroll=min(count, 4))

    def backward(step, carry):
        l = layers - 1 - step
        parity = step % 2

        def serve(k):
            for at in range(layers):

                @pl.when(step == at)
                def _():
                    serve_back(SERVICES * at + k)

        def a2(r, b):
            theirs = pl.ds(pl.multiple_of(quarter * next_rank(r), quarter), quarter)
            return peer(
                dr2o.at[b, :, theirs], dr2c.at[b, mine], a2b_s.at[b, r - 1], a2b_r.at[b, r - 1], r
            )

        sums = {}

        def add_small(i, value):
            sums[i] = sums[i] + value if i in sums else value

        for b in streams:
            dout = cur[b]
            gate = gatesave[l, b]
            dkvall[b, mine, :] = (dout * gate).astype(BF)
            ag_start(dkvall, b)
            dr2o[b] = (dout * kvsave[l, b] * gate * (1.0 - gate)).astype(BF)
            for r in range(1, RANKS):
                a2(r, b).start()
            dr2c[b, mine, :] = dr2o[b, :, my_cols]
        serve(0)
        for b in streams:
            n = n2save[l, b].astype(F32)
            prev = before(n, l, 1, b)
            gap = n - prev
            mixk[b] = (prev + gap * rate(l, 3)).astype(BF)
            mixr[b] = (prev + gap * rate(l, 4)).astype(BF)
            act = jnp.maximum(zsave[l, b].astype(F32), 0.0)
            squares[b] = (act * act).astype(BF)
            ag_wait(dkvall, b)
            for r in range(1, RANKS):
                a2(r, b).wait()
            dz = (2.0 * act * dot_nt(dkvall[b], wV[l].reshape(hidden, width))).astype(BF)
            dzs[b] = dz
            dx = dot_nt(dz, wK[l].reshape(width, hidden))
            dxr = dot_nt(dr2c[b], wA[l, :, :, :, 3 * quarter :].reshape(width, quarter))
            mixed_part = dx * rate(l, 3) + dxr * rate(l, 4)
            shifted = (dx + dxr - mixed_part) * stay[b]
            rs_start(mixed_part + rolled(shifted, span - 1), b)
            add_small(7, column_sum(dx * gap))
            add_small(8, column_sum(dxr * gap))
            serve(1 + b)
        free(l, 0)

        @pl.when(step > 1)
        def _():
            all_sent(l + 2, parity, (V0, V1, K0, K1))

        each_block(
            squares,
            dkvall,
            lambda n, value: dV.__setitem__(
                (parity, n // RANKS, pl.ds(pl.multiple_of((n % RANKS) * block, block), block)), value
            ),
        )
        each_block(
            mixk,
            dzs,
            lambda n, value: dK.__setitem__((parity, n // HALVES, n % HALVES), value),
        )
        pl.semaphore_wait(sib_credit.at[0], 1)
        half_copy(l, parity, V0).start()
        half_copy(l, parity, K0).start()
        serve(3)
        for b in streams:
            dn = rs_wait(b)
            hat, rstd = normed(msave[l, b])
            add_small(1, column_sum(dn * hat))
            add_small(3, column_sum(dn))
            dm = cur[b] + norm_back(dn, parb[l, 1:2, :], hat, rstd)
            cur[b] = dm
            dmall[b, mine, :] = dm.astype(BF)
            ag_start(dmall, b)
        serve(4)

        @pl.when(step > 1)
        def _():
            all_sent(l + 2, parity, (A0, A1, OO))

        def to_dA(m):
            def store(n, value):
                dA[parity, n // HALVES, n % HALVES, :, m * quarter : (m + 1) * quarter] = value

            return store

        each_block(mixr, dr2c, to_dA(3))
        w = -jnp.exp(parb[l, 9:10, my_cols])
        for b in streams:
            n = nsave[l, b].astype(F32)
            prev = before(n, l, 0, b)
            gap = n - prev
            for i in range(3):
                mixes3[i, b] = (prev + gap * rate(l, i)).astype(BF)
            al = alsave[l, b]
            be = besave[l, b]
            v, y, sr, e1, e2, num_prev, den_prev = [smsave[l, i, b].astype(F32) for i in range(7)]
            gated[b] = (sr * y).astype(BF)
            ag_wait(dmall, b)
            dg = dot_nt(dmall[b], wO[l].reshape(quarter, width))
            dr = (dg * y * sr * (1.0 - sr)).astype(BF)
            dy = dg * sr
            keep = rolled(al * stay[b], span - 1)
            into = dy * e1 * stay[b]
            ga = rolled(into, span - 1)
            gb = -rolled(into * y, span - 1)
            for i, s in enumerate(reaches):
                ga = ga + keep * rolled(ga, span - s)
                gb = gb + keep * rolled(gb, span - s)
                if i + 1 < len(reaches):
                    keep = keep * rolled(keep, span - s)
            near = dy * e2
            now = near * (v - y)
            dv = (be * ga + near).astype(BF)
            dk = (be * (v * ga + gb) + now).astype(BF)
            add_small(9, w * column_sum(al * (ga * num_prev + gb * den_prev)))
            add_small(10, column_sum(now))
            total = None
            mixed_part = None
            for i, left in enumerate((dk, dv, dr)):
                lefts[i, b] = left
                dx = dot_nt(
                    left, wA[l, :, :, :, i * quarter : (i + 1) * quarter].reshape(width, quarter)
                )
                add_small(4 + i, column_sum(dx * gap))
                scaled = dx * rate(l, i)
                total = dx if total is None else total + dx
                mixed_part = scaled if mixed_part is None else mixed_part + scaled
            shifted = (total - mixed_part) * stay[b]
            rs_start(mixed_part + rolled(shifted, span - 1), b)
            serve(5 + b)
        free(l, 1)

        each_block(
            gated, dmall, lambda n, value: dO.__setitem__((parity, n), value), HALVES
        )
        for i in range(3):
            each_block(mixes3.at[i], lefts.at[i], to_dA(i))
        pl.semaphore_wait(sib_credit.at[1], 1)
        half_copy(l, parity, A0).start()
        half_copy(l, parity, OO).start()
        serve(7)
        for b in streams:
            dn = rs_wait(b)
            hat, rstd = normed(hsave[l, b])
            add_small(0, column_sum(dn * hat))
            add_small(2, column_sum(dn))
            dh = cur[b] + norm_back(dn, parb[l, 0:1, :], hat, rstd)
            result = dh.astype(BF)
            gradb[b] = result
            cur[b] = result.astype(F32)
        for i, value in sums.items():
            sg[l, i : i + 1, my_cols if i in (9, 10) else slice(None)] = value
        for i in GROUPS:
            half_copy(l, parity, i).wait_send()
        return carry

    lax.fori_loop(0, layers, backward, 0)

    tg_args = (swap_self, gradb, tgrad, out_s.at[1], out_r.at[1], t, p)
    start_any(*tg_args)

    def sg_copy(r):
        return plane(sg.at[next_pipe(r)], sgr.at[r - 1], sg_s.at[r - 1], sg_r.at[r - 1], r)

    lanes = sg8.shape[-1]

    def sg_cols(rank, half):
        return pl.ds(pl.multiple_of(lanes * (rank * HALVES + half), lanes), lanes)

    def sg8_copy(a, b):
        rank, half = next_rank(a), (c + b) % HALVES
        n = a * HALVES + b
        return remote(
            sgt.at[:, sg_cols(rank, half)], sg8.at[n], sg8_s.at[n], sg8_r.at[n], p, rank, half
        )

    others = [(a, b) for a in range(RANKS) for b in range(HALVES) if a or b]
    for r in range(1, RANKS):
        sg_copy(r).start()
    for l in range(layers):

        @pl.when(l == p)
        def _():
            for i in PIECES:
                for way in range(2):
                    if not late(layers - 1 - l, i, way):
                        hand_out(i, way)

    end = SERVICES * layers
    for time in range(end, 1 + max(slots[-1] for _, _, _, slots in BACK)):
        serve_back(time)
        if time == end + 1:
            for r in range(1, RANKS):
                sg_copy(r).wait()
            total = sg[p]
            for r in range(1, RANKS):
                total = total + sgr[r - 1]
            sgt[...] = total
            for a, b in others:
                sg8_copy(a, b).start()
    total = sgt[:, sg_cols(t, c)]
    for a, b in others:
        sg8_copy(a, b).wait()
        total = total + sg8[a * HALVES + b]
    small[...] = total

    for l in range(layers):
        sent_any(*fin_args(l))
    for r in range(1, RANKS):
        par_copy(r).wait_send()
    carried_sent()
    sent_any(swap_self, mixb, mixed, out_s.at[0], out_r.at[0], t, p)
    got_any(swap_self, mixed, out_r.at[0])
    sent_any(*tg_args)
    got_any(swap_self, tgrad, out_r.at[1])
    for l in range(2):
        all_sent(l, (layers - 1 - l) % 2, PIECES)
    for i in PIECES:
        for way in range(2):
            if i in (V0, V1, OO):
                home_own(i, way).wait()
            else:
                for args in home_args(i, way):
                    if args[-1]:
                        home_copy(*args).wait_send()
                    else:
                        home_copy(*args).wait()
    for src in range(RANKS):
        cols = pl.ds(src * quarter, quarter)
        got_any(jnp.logical_and(swap_self, t == src), finout.at[:, :, cols], fin_r.at[src])
        if src:
            for m, grad in enumerate((gk, gv, gr, gfr)):
                got(grad.at[:, cols], r1_r.at[m, src])
            got(gfk.at[:, pl.ds(src * hidden, hidden)], r1_r.at[4, src])


def on_device(
    outer,
    tokens,
    cotangent,
    lengths,
    carried,
    norm_gain,
    norm_bias,
    mix_rates,
    time_decay,
    time_first,
    attention_accept_proj,
    attention_lookup_proj,
    attention_content_proj,
    attention_result_proj,
    feedforward_accept_proj,
    feedforward_lookup_proj,
    feedforward_content_proj,
):
    layers = lax.axis_size("pipe")
    micro, chunk, width = tokens.shape
    row_count = chunk * RANKS
    rows = micro * row_count
    per = lengths.shape[1]
    seqs = micro * per
    weights = [
        attention_lookup_proj[0],
        attention_content_proj[0],
        attention_accept_proj[0],
        feedforward_accept_proj[0],
        attention_result_proj[0],
        feedforward_lookup_proj[0],
        feedforward_content_proj[0],
    ]
    near = [[b * outer + i for i in range(outer)] for b in range(RANKS * HALVES)]
    if outer > 1:
        weights = [
            lax.all_gather(w, "dp", axis=0, tiled=True, axis_index_groups=near) for w in weights
        ]
    block = width // (RANKS * HALVES)
    hidden = weights[5].shape[1] // RANKS
    quarter = width // RANKS
    vmem = pl.BlockSpec(memory_space=pltpu.VMEM)
    smem = pl.BlockSpec(memory_space=pltpu.SMEM)
    hbm = pl.BlockSpec(memory_space=pl.ANY)
    dma = pltpu.SemaphoreType.DMA
    regular = pltpu.SemaphoreType.REGULAR
    n_peers = RANKS - 1
    own = (micro, chunk, width)
    full = (micro, row_count, width)

    def stores(count):
        return [
            pltpu.VMEM((count, RANKS, HALVES, block, width), BF),
            pltpu.VMEM((count, HALVES, block, width), BF),
            pltpu.VMEM((count, RANKS, HALVES, block, hidden), BF),
            pltpu.VMEM((count, HALVES, hidden // HALVES, width), BF),
        ]

    outs = pl.pallas_call(
        partial(layers_kernel, outer, row_count // 2),
        out_shape=(
            jax.ShapeDtypeStruct(own, BF),
            jax.ShapeDtypeStruct(own, BF),
            jax.ShapeDtypeStruct((5, seqs, width), F32),
            jax.ShapeDtypeStruct((16, block), F32),
        )
        + tuple(jax.ShapeDtypeStruct(w.shape, BF) for w in weights),
        in_specs=[vmem] * 2 + [smem] + [vmem] * 6 + [hbm] * 7,
        out_specs=(vmem,) * 4 + (hbm,) * 7,
        scratch_shapes=stores(layers)
        + stores(2)
        + [
            pltpu.VMEM(own, BF),
            pltpu.VMEM(own, BF),
            pltpu.VMEM((16, 128), F32),
            pltpu.VMEM((16, 128), F32),
            pltpu.VMEM((32, width), BF),
            pltpu.VMEM((layers, 32, quarter), BF),
            pltpu.VMEM((16, width), BF),
            pltpu.VMEM((layers, 16, width), BF),
            pltpu.VMEM((16, width), F32),
            pltpu.VMEM((layers, 16, width), F32),
            pltpu.VMEM((layers,) + full, BF),
            pltpu.VMEM((layers,) + full, BF),
            pltpu.VMEM((layers,) + own, F32),
            pltpu.VMEM((layers,) + own, F32),
            pltpu.VMEM((layers,) + own, F32),
            pltpu.VMEM((layers,) + own, F32),
            pltpu.VMEM((layers, micro, row_count, hidden), BF),
            pltpu.VMEM((layers, micro, row_count, quarter), F32),
            pltpu.VMEM((layers, micro, row_count, quarter), F32),
            pltpu.VMEM((layers, 7, micro, row_count, quarter), BF),
            pltpu.VMEM(full, BF),
            pltpu.VMEM((micro, n_peers, chunk, width), BF),
            pltpu.VMEM((micro, row_count, quarter), BF),
            pltpu.VMEM(own, BF),
            pltpu.VMEM(own, F32),
            pltpu.VMEM((layers, 5, seqs, quarter), F32),
            pltpu.VMEM(own, BF),
            pltpu.VMEM(own, BF),
            pltpu.VMEM(full, BF),
            pltpu.VMEM(full, BF),
            pltpu.VMEM(own, BF),
            pltpu.VMEM((micro, row_count, quarter), BF),
            pltpu.VMEM(full, BF),
            pltpu.VMEM(full, BF),
            pltpu.VMEM((micro, row_count, hidden), BF),
            pltpu.VMEM((micro, row_count, hidden), BF),
            pltpu.VMEM((3,) + full, BF),
            pltpu.VMEM((3, micro, row_count, quarter), BF),
            pltpu.VMEM((micro, row_count, quarter), BF),
            pltpu.VMEM((layers, 16, width), F32),
            pltpu.VMEM((n_peers, 16, width), F32),
            pltpu.VMEM((16, width), F32),
            pltpu.VMEM((RANKS * HALVES, 16, block), F32),
            dma((3,)),
            dma((3,)),
            dma((RANKS,)),
            dma((layers,)),
            dma((RANKS,)),
            dma((layers,)),
            dma((n_peers,)),
            dma((layers,)),
            dma((5, n_peers)),
            dma((5, n_peers)),
            dma((7,)),
            dma((layers, 7, 2)),
            dma((layers, 7, 2)),
            dma((layers, 4)),
            dma((layers, 4)),
            dma((micro, n_peers)),
            dma((micro, n_peers)),
            dma((micro, n_peers)),
            dma((micro, n_peers)),
            dma((micro, n_peers)),
            dma((micro, n_peers)),
            dma((micro, n_peers)),
            dma((micro, n_peers)),
            dma((layers,)),
            dma((RANKS,)),
            dma((2,)),
            dma((2,)),
            dma((layers, 4)),
            dma((layers, 4)),
            dma((layers, 7, 2)),
            dma((layers, 7, 2)),
            dma((5, RANKS)),
            dma((5, RANKS)),
            dma((6,)),
            dma((n_peers,)),
            dma((n_peers,)),
            dma((RANKS * HALVES,)),
            dma((RANKS * HALVES,)),
            regular((layers, 2, 2)),
            regular((2,)),
        ],
        compiler_params=pltpu.CompilerParams(
            collective_id=0, has_side_effects=True, vmem_limit_bytes=60 * 2**20
        ),
        name="layers",
    )(
        tokens,
        cotangent,
        lengths,
        carried.transpose(0, 1, 3, 2, 4),
        norm_gain,
        norm_bias,
        mix_rates.transpose(1, 0, 2),
        time_decay,
        time_first,
        *weights,
    )
    mixed, tgrad, fin, small, *grads = outs
    if outer > 1:
        grads = [
            lax.psum_scatter(g, "dp", scatter_dimension=0, tiled=True, axis_index_groups=near)
            for g in grads
        ]
        small = lax.psum_scatter(
            small, "dp", scatter_dimension=1, tiled=True, axis_index_groups=near
        )
    gk, gv, gr, gfr, go, gfk, gfv = [g.astype(F32)[None] for g in grads]
    small = small[None]
    return (
        mixed,
        tgrad.astype(F32),
        fin.transpose(1, 0, 2).reshape(micro, per, 1, 5, width),
        small[:, 0:2],
        small[:, 2:4],
        small[:, 4:9],
        small[:, 9],
        small[:, 10],
        gr,
        gk,
        gv,
        go,
        gfr,
        gfk,
        gfv,
    )


def solution(mesh):
    outer = mesh.shape["dp"] // (RANKS * HALVES)
    placed = (
        P("dp", "pipe", None),
        P("dp", "pipe", None),
        P("dp", None),
        P("dp", None, "pipe", None, None),
        P("pipe", None, None),
        P("pipe", None, None),
        P("pipe", None, None),
        P("pipe", None),
        P("pipe", None),
    ) + (P("pipe", "dp", None),) * 7
    return jax.shard_map(
        partial(on_device, outer),
        mesh=mesh,
        in_specs=placed,
        out_specs=(
            P("dp", "pipe", None),
            P("dp", "pipe", None),
            P("dp", None, "pipe", None, None),
            P("pipe", None, "dp"),
            P("pipe", None, "dp"),
            P("pipe", None, "dp"),
            P("pipe", "dp"),
            P("pipe", "dp"),
        )
        + (P("pipe", "dp", None),) * 7,
        check_vma=False,
    )
```
